128 devices in a mesh: band: 32 (over x, y_hi, z), clip: 4 (over y_lo, core).
Axes of the slice: x: 4, y: 4 (y_hi: 2, y_lo: 2; y = y_hi * 2 + y_lo), z: 4, core: 2. Of those that a mesh axis runs over, the one named last changes fastest.
Arguments:
- latent: bfloat16 [16, 64, 512, 128], P('clip', 'band'), parts along dimension 0, may hold values from -6 to 6
- dec_kernel: bfloat16 [3, 3, 3, 128, 128], replicated, may hold values from -0.109375 to 0.109375
- rgb_kernel: bfloat16 [3, 3, 3, 128, 3], replicated, may hold values from -0.4375 to 0.4375
- target: bfloat16 [16, 64, 512, 3], P('clip', 'band'), parts along dimension 0, may hold values from -8 to 8
- vgg_first: bfloat16 [3, 3, 3, 64], replicated, may hold values from -1.25 to 1.25
- vgg_second: bfloat16 [3, 3, 64, 128], replicated, may hold values from -0.25 to 0.25
- critic_kernel: bfloat16 [3, 3, 3, 3, 64], replicated, may hold values from -0.625 to 0.625
- critic_head: float32 [64], replicated, may hold values from -2 to 2
Outputs:
- grad_latent: float32 [16, 64, 512, 128], P('clip', 'band'), parts along dimension 0
- grad_dec: float32 [12, 3, 3, 128, 128], P('clip'), parts along dimension 0
- grad_rgb: float32 [12, 3, 3, 128, 3], P('clip'), parts along dimension 0
The draws below stay inside these ranges and needn't reach their ends.
There are 4 independent parts, one for each index of `clip`. The reference program is written for one: setup_inputs(seed, part) draws one part's arguments, and reference() takes and returns one part's arrays. A program takes and returns all parts, laid end to end along the dimension named above; an argument that names none is the same for every part. Nothing has to cross between parts.
All inputs are finite; a program needn't handle non-finite values.
Results may differ from the reference program's by a relative error of at most 0.025.
Values may be sent and summed in bfloat16 or wider, within the bound.
No kernel may reach another device: no remote copies, remote signals or barrier semaphores. Data moves between devices by JAX's collectives and lax.ppermute only.
A program may use at most 128 MiB of HBM per device.

```python
import jax
import jax.numpy as jnp
from jax import lax

FRAMES = 4
CHANNELS = 128
VGG_ONE = 64
VGG_TWO = 128
CRITIC = 64
COLS = 512
ROWS = 64


def shard_levels(own_key, extent, split, low, largest):
    factor_of = 1.0
    for position, blocks in split:
        steps = jax.random.uniform(jax.random.fold_in(jax.random.fold_in(own_key, 6), position), (blocks,), jnp.float32, low / len(split), largest / len(split))
        factor_of = factor_of * jnp.repeat(jnp.exp(steps), extent[position] // blocks).reshape((-1,) + (1,) * (len(extent) - 1 - position))
    return factor_of


def gaussian(stream_key, shape, scale, limit, cuts=(), held_as=jnp.bfloat16):
    drawn = scale * jax.random.normal(stream_key, shape, jnp.float32)
    if cuts:
        drawn = drawn * shard_levels(stream_key, shape, cuts, -0.22, 0.18)
    return jnp.clip(drawn, -limit, limit).astype(held_as)


def setup_inputs(seed: int = 0, part: int = 0) -> dict:
    splits = jax.random.split(jax.random.key(seed), 9)
    part_keys = jax.random.split(jax.random.fold_in(splits[8], part), 9)
    latent = gaussian(part_keys[0], (FRAMES, ROWS, COLS, CHANNELS), 1.0, 6.0, ((1, 32),))
    dec_kernel = gaussian(splits[1], (3, 3, 3, CHANNELS, CHANNELS), (27 * CHANNELS) ** -0.5, 0.109375)
    rgb_kernel = gaussian(splits[2], (3, 3, 3, CHANNELS, 3), (27 * CHANNELS // 16) ** -0.5, 0.4375)
    target = gaussian(part_keys[3], (FRAMES, ROWS, COLS, 3), 1.5, 8.0, ((1, 32),))
    vgg_first = gaussian(splits[4], (3, 3, 3, VGG_ONE), 27 ** -0.5, 1.25)
    vgg_second = gaussian(splits[5], (3, 3, VGG_ONE, VGG_TWO), (9 * VGG_ONE) ** -0.5, 0.25)
    critic_kernel = gaussian(splits[6], (3, 3, 3, 3, CRITIC), 81 ** -0.5, 0.625)
    critic_head = gaussian(splits[7], (CRITIC,), (CRITIC // 8) ** -0.5, 2.0, (), jnp.float32)
    return dict(latent=latent, dec_kernel=dec_kernel, rgb_kernel=rgb_kernel, target=target, vgg_first=vgg_first, vgg_second=vgg_second, critic_kernel=critic_kernel, critic_head=critic_head)


HIGH = lax.Precision.HIGHEST
DEC_SPEC = ('NDHWC', 'DHWIO', 'NDHWC')
IMG_SPEC = ('NHWC', 'HWIO', 'NHWC')

def conv_same(field, kernel, spec):
    spatial = kernel.ndim - 2
    return lax.conv_general_dilated(field.astype(jnp.float32), kernel.astype(jnp.float32), (1,) * spatial, 'SAME', dimension_numbers=spec, precision=HIGH)

def flipped(kernel):
    spatial = kernel.ndim - 2
    turned = jnp.flip(kernel, axis=tuple(range(spatial)))
    return jnp.swapaxes(turned, -1, -2)

def conv_three(field, kernel):
    return conv_same(field[None], kernel, DEC_SPEC)[0]

def conv_two(field, kernel):
    return conv_same(field, kernel, IMG_SPEC)

def silu_slope(value):
    gate_value = jax.nn.sigmoid(value)
    return gate_value * (1.0 + value * (1.0 - gate_value))

def kernel_grad(source, grad_out):
    frames_n, rows_n, cols_n = (grad_out.shape[0], grad_out.shape[1], grad_out.shape[2])
    padded = jnp.pad(source.astype(jnp.float32), ((1, 1), (1, 1), (1, 1), (0, 0)))
    grad_f = grad_out.astype(jnp.float32)
    blocks = []
    for first in range(3):
        for second in range(3):
            for third in range(3):
                window = padded[first:first + frames_n, second:second + rows_n, third:third + cols_n]
                blocks.append(jnp.einsum('fhwi,fhwo->io', window, grad_f, precision=HIGH))
    total = jnp.stack(blocks).reshape((3, 3, 3) + blocks[0].shape)
    return total * float(frames_n * rows_n * cols_n) ** (-0.5)

def reference(latent, dec_kernel, rgb_kernel, target, vgg_first, vgg_second, critic_kernel, critic_head):
    frames_n = latent.shape[0]
    pre_one = conv_three(latent, dec_kernel)
    act_one = jax.nn.silu(pre_one).astype(jnp.bfloat16)
    frames = conv_three(act_one, rgb_kernel).astype(jnp.bfloat16)
    pair = jnp.concatenate([frames, target], axis=0)
    pre_vone = conv_two(pair, vgg_first)
    feat_one = jax.nn.silu(pre_vone).astype(jnp.bfloat16)
    pre_vtwo = conv_two(feat_one, vgg_second)
    feat_two = jax.nn.silu(pre_vtwo)
    gap = feat_two[:frames_n] - feat_two[frames_n:]
    grad_two = (0.25 * gap * silu_slope(pre_vtwo[:frames_n])).astype(jnp.bfloat16)
    back_one = conv_two(grad_two, flipped(vgg_second))
    grad_one = (back_one * silu_slope(pre_vone[:frames_n])).astype(jnp.bfloat16)
    vgg_back = conv_two(grad_one, flipped(vgg_first))
    crit_pre = conv_three(frames, critic_kernel)
    logits = jnp.dot(jax.nn.silu(crit_pre), critic_head, precision=HIGH)
    slope = -jax.nn.sigmoid(-logits)
    grad_crit = (slope[..., None] * critic_head * silu_slope(crit_pre)).astype(jnp.bfloat16)
    crit_back = conv_three(grad_crit, flipped(critic_kernel))
    grad_frames = (vgg_back + crit_back).astype(jnp.bfloat16)
    grad_act = conv_three(grad_frames, flipped(rgb_kernel))
    grad_pre = (grad_act * silu_slope(pre_one)).astype(jnp.bfloat16)
    grad_latent = conv_three(grad_pre, flipped(dec_kernel))
    grad_dec = kernel_grad(latent, grad_pre)
    grad_rgb = kernel_grad(act_one, grad_frames)
    return (grad_latent, grad_dec, grad_rgb)
```

```python
import jax
import jax.numpy as jnp
from jax import lax
from jax.experimental import pallas as pl
from jax.experimental.pallas import tpu as pltpu
from jax.sharding import PartitionSpec as P

F32 = jnp.float32
BF16 = jnp.bfloat16
HALO = 4


def sigmoid(value):
    return 0.5 * jnp.tanh(0.5 * value) + 0.5


def slope_of(value, gate):
    return gate * (1.0 + value * (1.0 - gate))


def dot(left, right, contract=((1,), (0,))):
    return lax.dot_general(left, right, (contract, ((), ())), preferred_element_type=F32)


def call(kernel, outs, *args, scratch=(), macs=0):
    moved = sum(a.size * a.dtype.itemsize for a in args)
    moved += sum(o.size * o.dtype.itemsize for o in outs)
    return pl.pallas_call(
        kernel,
        out_shape=outs,
        in_specs=[pl.BlockSpec(memory_space=pltpu.VMEM)] * len(args),
        out_specs=[pl.BlockSpec(memory_space=pltpu.VMEM)] * len(outs),
        scratch_shapes=list(scratch),
        compiler_params=pltpu.CompilerParams(vmem_limit_bytes=48 * 1024 * 1024),
        cost_estimate=pl.CostEstimate(flops=2 * macs, bytes_accessed=moved, transcendentals=0),
    )(*args)


def shape(dims, dtype):
    return jax.ShapeDtypeStruct(dims, dtype)


def before(value):
    row = lax.broadcasted_iota(jnp.int32, value.shape, 0)
    return jnp.where(row >= 1, pltpu.roll(value, 1, 0), 0.0)


def after(value):
    size = value.shape[0]
    row = lax.broadcasted_iota(jnp.int32, value.shape, 0)
    return jnp.where(row < size - 1, pltpu.roll(value, size - 1, 0), 0.0)


def weights_kernel(dec, rgb, own, edge, own_t, edge_t, colour, scr):
    edge[...] = jnp.zeros_like(edge)
    edge_t[...] = jnp.zeros_like(edge_t)
    for a in range(3):
        for e in range(3):
            tap = [dec[(a * 3 + b) * 3 + e] for b in range(3)]
            for j in range(2):
                for r in range(2):
                    one, two = (a * 256 + j * 128, e * 256 + r * 128)
                    own[one : one + 128, two : two + 128] = tap[j - r + 1]
                    one, two = (e * 256 + j * 128, a * 256 + r * 128)
                    own_t[one : one + 128, two : two + 128] = tap[j - r + 1]
                one, two = (a * 256 + j * 128, e * 256 + j * 128)
                edge[one : one + 128, two : two + 128] = tap[2 * j]
                edge_t[two : two + 128, one : one + 128] = tap[2 - 2 * j]
    scr[...] = jnp.zeros_like(scr)
    for f in range(4):
        for r in range(2):
            lanes = slice((f * 2 + r) * 128, (f * 2 + r + 1) * 128)
            for a in range(3):
                to = f - a + 1
                if not 0 <= to < 4:
                    continue
                for e in range(3):
                    at = e * 128 + to * 12 + r * 3
                    scr[at : at + 9, lanes] = rgb[a * 3 + e]
    colour[...] = scr[...].astype(BF16)


def frames_of(f, step):
    return [(a, f + step * (a - 1)) for a in range(3) if 0 <= f + step * (a - 1) < 4]


def conv_rows(first, second, kernel, f):
    taps = frames_of(f, 1)
    left = jnp.concatenate([half[g] for _, g in taps for half in (first, second)], axis=1)
    wide = dot(left, kernel[taps[0][0] * 256 : (taps[-1][0] + 1) * 256, :])
    return before(wide[:, :256]) + wide[:, 256:512] + after(wide[:, 512:])


def conv_rows_t(first, second, kernel, f):
    taps = frames_of(f, -1)
    left = jnp.concatenate([half[g] for _, g in taps for half in (first, second)], axis=1)
    lanes = slice(taps[0][0] * 256, (taps[-1][0] + 1) * 256)
    wide = dot(left, kernel[:, lanes], ((1,), (1,)))
    return after(wide[:, :256]) + wide[:, 256:512] + before(wide[:, 512:])


def dec_own_kernel(zero, one, kernel, out):
    for f in range(4):
        out[f] = conv_rows(zero, one, kernel, f)


def dec_edge_kernel(above, below, kernel, own, colour, target, act, slope, parts, t_scr, p_scr):
    cols = act.shape[0]
    for f in range(4):
        pre = own[f] + conv_rows(above, below, kernel, f)
        gate = sigmoid(pre)
        act[:, f * 256 : (f + 1) * 256] = (pre * gate).astype(BF16)
        slope[f] = slope_of(pre, gate)
    wide = dot(act[...], colour[...], ((1,), (1,)))
    part = before(wide[:, :128]) + wide[:, 128:256] + after(wide[:, 256:])
    t_scr[...] = jnp.zeros_like(t_scr)
    t_scr[48:72, :] = target[...].astype(F32)
    p_scr[0:8, :] = jnp.zeros((8, 128), F32)
    p_scr[cols : cols + 8, :] = jnp.zeros((8, 128), F32)
    p_scr[HALO : HALO + cols, :] = part + t_scr[...].T
    blocks, width, _ = parts.shape
    for d in range(blocks):
        start = d * (width - 2 * HALO)
        parts[d] = p_scr[start : start + width, :]


def branch_kernel(parts, mask_ref, w1, w2, w2_t, w1_t, head, out, tap_scr, e_scr, im_scr, acc, g_scr):
    blocks, wide, _ = parts.shape
    lanes = blocks * wide
    lane = lax.broadcasted_iota(jnp.int32, (1, lanes), 1)
    mask = mask_ref[0:1, :]
    lo, hi = (lane >= wide, lane < lanes - wide)

    def down(value):
        return jnp.where(lo, pltpu.roll(value, wide, 1), 0.0)

    def up(value):
        return jnp.where(hi, pltpu.roll(value, lanes - wide, 1), 0.0)

    def left(value):
        return pltpu.roll(value, 1, 1)

    def right(value):
        return pltpu.roll(value, lanes - 1, 1)

    def rounded(value):
        return value.astype(BF16).astype(F32)

    turned = parts[...].reshape(lanes, 128).T
    g_scr[...] = turned
    e_scr[...] = jnp.zeros_like(e_scr)
    tap_scr[0:64, :] = jnp.zeros((64, lanes), BF16)
    tap_scr[320:384, :] = jnp.zeros((64, lanes), BF16)

    def place(at, even, odd):
        for k, value in enumerate((even, odd)):
            e_scr[k, 0:3, :] = left(value)
            e_scr[k, 3:6, :] = value
            e_scr[k, 6:9, :] = right(value)
        even, odd = (e_scr[0], e_scr[1])
        tap_scr[at : at + 16, :] = down(odd).astype(BF16)
        tap_scr[at + 16 : at + 32, :] = even.astype(BF16)
        tap_scr[at + 32 : at + 48, :] = odd.astype(BF16)
        tap_scr[at + 48 : at + 64, :] = up(even).astype(BF16)

    for f in range(4):
        at = f * 12
        even = g_scr[at + 3 : at + 6, :] + down(g_scr[at + 9 : at + 12, :])
        odd = g_scr[at + 6 : at + 9, :] + up(g_scr[at : at + 3, :])
        place(64 + f * 64, rounded(even * mask), rounded(odd * mask))
        at = 48 + f * 6
        place(384 + f * 64, g_scr[at : at + 3, :] * mask, g_scr[at + 3 : at + 6, :] * mask)
    acc[...] = jnp.zeros_like(acc)

    def second(feat):
        for e, moved in enumerate((left(feat), feat, right(feat))):
            at = e * 256
            im_scr[at : at + 64, :] = down(moved[64:]).astype(BF16)
            im_scr[at + 64 : at + 192, :] = moved.astype(BF16)
            im_scr[at + 192 : at + 256, :] = up(moved[:64]).astype(BF16)
        return dot(w2[...], im_scr[...])

    def one_frame(f, carry):
        at = pl.multiple_of(f * 64, 64)
        pre = dot(w1[0:128, 64:128], tap_scr[pl.ds(at + 384, 64), :])
        pre_two = second(rounded(pre * sigmoid(pre) * mask))
        wanted = pre_two * sigmoid(pre_two)
        both = dot(w1[...], tap_scr[pl.ds(at, 192), :])
        pre_vone, crit = (both[:128], both[128:])
        gate = sigmoid(pre_vone)
        slope_one = slope_of(pre_vone, gate) * mask
        pre_two = second(rounded(pre_vone * gate * mask))
        gate = sigmoid(pre_two)
        gap = pre_two * gate - wanted
        grad_two = (0.25 * gap * slope_of(pre_two, gate) * mask).astype(BF16)
        spread = dot(w2_t[...], grad_two)
        rows = []
        for rr in range(4):
            at_r = rr * 64
            rows.append(
                right(spread[at_r : at_r + 64])
                + spread[256 + at_r : 320 + at_r]
                + left(spread[512 + at_r : 576 + at_r])
            )
        back = jnp.concatenate([rows[1] + down(rows[3]), rows[2] + up(rows[0])], axis=0)
        grad_one = (back * slope_one).astype(BF16)
        gate = sigmoid(crit)
        scored = crit * gate * head[...]
        slope_c = slope_of(crit, gate) * head[...] * mask
        grads = []
        for r in range(2):
            logits = jnp.sum(scored[r * 64 : (r + 1) * 64], axis=0, keepdims=True)
            grads.append(-sigmoid(-logits) * slope_c[r * 64 : (r + 1) * 64])
        grad_crit = jnp.concatenate(grads, axis=0).astype(BF16)
        spread = dot(w1_t[...], jnp.concatenate([grad_one, grad_crit], axis=0))
        for a in range(3):
            acc[f + a] += spread[a * 64 : (a + 1) * 64]
        return carry

    lax.fori_loop(0, 4, one_frame, 0)
    g_scr[...] = jnp.zeros_like(g_scr)
    for f in range(4):
        field = acc[f + 1]
        e_scr[0] = field[16:32] + down(field[48:64])
        e_scr[1] = field[32:48] + up(field[0:16])
        even, odd = [
            rounded(right(e_scr[k, 0:3, :]) + e_scr[k, 3:6, :] + left(e_scr[k, 6:9, :]))
            for k in range(2)
        ]
        at = f * 12
        for k, value in enumerate((down(odd), even, odd, up(even))):
            g_scr[at + 3 * k : at + 3 * k + 3, :] = pltpu.roll(value, lanes - HALO, 1)
    back = g_scr[...].T.reshape(blocks, wide, 128)
    out[...] = back[:, : wide - 2 * HALO].astype(BF16)


def pre_kernel(grad_in, colour, slope, act, zero, one, moved, rgb_out, gram):
    cols = act.shape[0]
    grad = grad_in[...].reshape(cols, 128).astype(F32)
    taps = jnp.concatenate([after(grad), grad, before(grad)], axis=1).astype(BF16)
    grad_act = dot(taps, colour[...])
    lane = lax.broadcasted_iota(jnp.int32, (1, cols), 1)
    for f in range(4):
        pre = (grad_act[:, f * 256 : (f + 1) * 256] * slope[f]).astype(BF16)
        zero[f] = pre[:, :128]
        one[f] = pre[:, 128:]
        turned = pre.astype(F32).T
        later = jnp.where(lane < cols - 1, pltpu.roll(turned, cols - 1, 1), 0.0)
        sooner = jnp.where(lane >= 1, pltpu.roll(turned, 1, 1), 0.0)
        for e, value in enumerate((later, turned, sooner)):
            moved[e * 256 : (e + 1) * 256, f * cols : (f + 1) * cols] = value.astype(BF16)
    gram[...] = dot(taps.astype(F32).T.astype(BF16), act[...])
    for a in range(3):
        for e in range(3):
            total = jnp.zeros((9, 128), F32)
            for f in range(4):
                to = f - a + 1
                if not 0 <= to < 4:
                    continue
                for r in range(2):
                    at = e * 128 + to * 12 + r * 3
                    total += gram[at : at + 9, (f * 2 + r) * 128 : (f * 2 + r + 1) * 128]
            for b in range(3):
                at = ((a * 3 + b) * 3 + e) * 3
                rgb_out[at : at + 3, :] = total[(2 - b) * 3 : (2 - b) * 3 + 3]


def dec_grad_kernel(moved, zero, one, above, below, rgb_grad, out, field):
    cols = zero.shape[1]
    for f in range(4):
        for k, part in enumerate((above, zero, one, below)):
            field[f * cols : (f + 1) * cols, k * 128 : (k + 1) * 128] = part[f]
    for a in range(3):
        lo, hi = (max(0, 1 - a), min(4, 5 - a))
        first, last = (lo * cols, hi * cols)
        skip = (a - 1) * cols
        for e in range(3):
            gram = dot(
                moved[e * 256 : (e + 1) * 256, first:last],
                field[first + skip : last + skip, :],
            )
            for b in range(3):
                total = gram[:128, b * 128 : b * 128 + 128] + gram[128:, b * 128 + 128 : b * 128 + 256]
                at = ((a * 3 + b) * 3 + e) * 128
                out[at : at + 128, :] = total.T.astype(BF16)
    out[27 * 128 :, :] = rgb_grad[...].astype(BF16)


def lat_own_kernel(zero, one, kernel, out):
    for f in range(4):
        wide = conv_rows_t(zero, one, kernel, f)
        out[f, 0] = wide[:, :128]
        out[f, 1] = wide[:, 128:]


def lat_edge_kernel(above, below, kernel, own, out):
    for f in range(4):
        wide = conv_rows_t(above, below, kernel, f)
        out[f, 0] = own[f, 0] + wide[:, :128]
        out[f, 1] = own[f, 1] + wide[:, 128:]


def branch_weights(vgg_first, vgg_second, critic):
    def paired(taps):
        none = jnp.zeros_like(taps[..., :1, :, :])
        return jnp.stack(
            [jnp.concatenate([taps, none], -3), jnp.concatenate([none, taps], -3)], axis=-4
        )

    def nine(taps):
        flat = taps.reshape(taps.shape[:-3] + (9, taps.shape[-1]))
        edges = [(0, 0)] * (flat.ndim - 2) + [(0, 7), (0, 0)]
        return jnp.pad(flat, edges)

    first = paired(nine(vgg_first))
    none = jnp.zeros_like(first)
    first = jnp.stack([none, first, none])
    crit = paired(nine(critic))
    w1_t = jnp.stack([first, crit])
    w1_t = w1_t.transpose(1, 3, 4, 0, 2, 5).reshape(192, 256)
    w2_t = paired(vgg_second.transpose(1, 0, 2, 3))
    w2_t = w2_t.transpose(0, 2, 3, 1, 4).reshape(768, 256)
    return (w1_t.T, w2_t.T, w2_t, w1_t)


def per_device(
    latent, dec_kernel, rgb_kernel, target, vgg_first, vgg_second, critic_kernel, critic_head
):
    size = lax.axis_size("band")
    me = lax.axis_index("band")
    cols = latent.shape[2]
    width = cols // size
    wide = width + 2 * HALO
    up = [(i, i + 1) for i in range(size - 1)]
    down = [(i + 1, i) for i in range(size - 1)]

    def neighbours(zero, one):
        return (lax.ppermute(one, "band", up), lax.ppermute(zero, "band", down))

    zero, one = (latent[:, 0], latent[:, 1])
    above, below = neighbours(zero, one)
    rgb = rgb_kernel.transpose(0, 2, 1, 4, 3)[:, :, ::-1].reshape(9, 9, 128).astype(F32)
    square = shape((768, 768), BF16)
    own_w, edge_w, own_wt, edge_wt, colour = call(
        weights_kernel,
        [square, square, square, square, shape((384, 1024), BF16)],
        dec_kernel.reshape(27, 128, 128),
        rgb,
        scratch=[pltpu.VMEM((384, 1024), F32)],
    )
    w1, w2, w2_t, w1_t = branch_weights(vgg_first, vgg_second, critic_kernel)
    head = jnp.concatenate([critic_head, critic_head]).reshape(128, 1)
    place = jnp.arange(size * wide) % wide + me * width - HALO
    mask = jnp.where((place >= 0) & (place < cols), 1.0, 0.0).astype(F32)
    mask = jnp.broadcast_to(mask, (8, size * wide))

    big = 4 * cols * 768 * 640
    (pre_own,) = call(dec_own_kernel, [shape((4, cols, 256), F32)], zero, one, own_w, macs=big)
    act, slope, parts = call(
        dec_edge_kernel,
        [
            shape((cols, 1024), BF16),
            shape((4, cols, 256), F32),
            shape((size, wide, 128), F32),
        ],
        above,
        below,
        edge_w,
        pre_own,
        colour,
        target.transpose(0, 1, 3, 2).reshape(24, cols),
        scratch=[pltpu.VMEM((128, cols), F32), pltpu.VMEM((cols + 8, 128), F32)],
        macs=big,
    )
    parts = lax.all_to_all(parts, "band", 0, 0)
    lanes = size * wide
    (grad_frames,) = call(
        branch_kernel,
        [shape((size, width, 128), BF16)],
        parts,
        mask,
        w1,
        w2,
        w2_t,
        w1_t,
        head,
        scratch=[
            pltpu.VMEM((640, lanes), BF16),
            pltpu.VMEM((2, 16, lanes), F32),
            pltpu.VMEM((768, lanes), BF16),
            pltpu.VMEM((6, 64, lanes), F32),
            pltpu.VMEM((128, lanes), F32),
        ],
        macs=4 * 768 * 768 * 700,
    )
    grad_frames = lax.all_to_all(grad_frames, "band", 0, 0)
    half = shape((4, cols, 128), BF16)
    grad_zero, grad_one, moved, rgb_grad = call(
        pre_kernel,
        [half, half, shape((768, 4 * cols), BF16), shape((128, 128), F32)],
        grad_frames,
        colour,
        slope,
        act,
        scratch=[pltpu.VMEM((384, 1024), F32)],
        macs=2 * cols * 384 * 1024,
    )
    grad_above, grad_below = neighbours(grad_zero, grad_one)
    (local,) = call(
        dec_grad_kernel,
        [shape((28 * 128, 128), BF16)],
        moved,
        zero,
        one,
        above,
        below,
        rgb_grad,
        scratch=[pltpu.VMEM((4 * cols, 512), BF16)],
        macs=2 * big,
    )
    (lat_own,) = call(
        lat_own_kernel, [shape((4, 2, cols, 128), F32)], grad_zero, grad_one, own_wt, macs=big
    )
    (grad_latent,) = call(
        lat_edge_kernel,
        [shape((4, 2, cols, 128), F32)],
        grad_above,
        grad_below,
        edge_wt,
        lat_own,
        macs=big,
    )
    pieces = lax.all_to_all(local.reshape(size, -1, 128), "band", 0, 0)
    mine = jnp.sum(pieces.astype(F32), axis=0).astype(BF16)
    whole = lax.all_to_all(jnp.broadcast_to(mine, (size,) + mine.shape), "band", 0, 0)
    whole = whole.reshape(28 * 128, 128)
    pixels = 4 * latent.shape[1] * size * cols
    factor = float(pixels) ** (-0.5)
    grad_dec = whole[: 27 * 128].astype(F32).reshape(3, 3, 3, 128, 128) * factor
    grad_rgb = whole[27 * 128 : 27 * 128 + 81].astype(F32).reshape(3, 3, 3, 3, 128) * factor
    return (grad_latent, grad_dec, grad_rgb.transpose(0, 1, 2, 4, 3))


def solution(mesh):
    placed = (
        P("clip", "band", None, None),
        P(),
        P(),
        P("clip", "band", None, None),
        P(),
        P(),
        P(),
        P(),
    )
    return jax.shard_map(
        per_device,
        mesh=mesh,
        in_specs=placed,
        out_specs=(
            P("clip", "band", None, None),
            P("clip", None, None, None, None),
            P("clip", None, None, None, None),
        ),
        check_vma=False,
    )
```

```python
import jax
import jax.numpy as jnp
from jax import lax
from jax.experimental import pallas as pl
from jax.experimental.pallas import tpu as pltpu
from jax.sharding import PartitionSpec as P

F32 = jnp.float32
BF16 = jnp.bfloat16
HBM = pltpu.HBM
EDGE_MIB = 56
PREPARE_MIB = 56
HALO = 4


def sigmoid(value):
    return 0.5 * jnp.tanh(0.5 * value) + 0.5


def slope_of(value, gate):
    return gate * (1.0 + value * (1.0 - gate))


def dot(left, right, contract=((1,), (0,))):
    return lax.dot_general(left, right, (contract, ((), ())), preferred_element_type=F32)


def call(kernel, outs, *args, scratch=(), macs=0, limit=60):
    args = [a if isinstance(a, tuple) else (a, pltpu.VMEM) for a in args]
    outs = [o if isinstance(o, tuple) else (o, pltpu.VMEM) for o in outs]
    moved = sum(a.size * a.dtype.itemsize for a, _ in args + outs)
    return pl.pallas_call(
        kernel,
        out_shape=[o for o, _ in outs],
        in_specs=[pl.BlockSpec(memory_space=m) for _, m in args],
        out_specs=[pl.BlockSpec(memory_space=m) for _, m in outs],
        scratch_shapes=list(scratch),
        compiler_params=pltpu.CompilerParams(vmem_limit_bytes=limit * 1024 * 1024),
        cost_estimate=pl.CostEstimate(flops=2 * macs, bytes_accessed=moved, transcendentals=0),
    )(*[a for a, _ in args])


def start(source, target, sem):
    copy = pltpu.make_async_copy(source, target, sem)
    copy.start()
    return copy


def shape(dims, dtype):
    return jax.ShapeDtypeStruct(dims, dtype)


def before(value):
    row = lax.broadcasted_iota(jnp.int32, value.shape, 0)
    return jnp.where(row >= 1, pltpu.roll(value, 1, 0), 0.0)


def after(value):
    size = value.shape[0]
    row = lax.broadcasted_iota(jnp.int32, value.shape, 0)
    return jnp.where(row < size - 1, pltpu.roll(value, size - 1, 0), 0.0)


def colour_rows(rgb, scr, rows):
    scr[...] = jnp.zeros_like(scr)
    for f in range(4):
        for k, j in enumerate(rows):
            lanes = slice((f * 2 + k) * 128, (f * 2 + k + 1) * 128)
            for a in range(3):
                to = f - a + 1
                if not 0 <= to < 4:
                    continue
                for e in range(3):
                    at = e * 128 + to * 24 + (j + 1) * 3
                    scr[at : at + 9, lanes] = rgb[a * 3 + e]


def frames_of(f, step):
    return [(a, f + step * (a - 1)) for a in range(3) if 0 <= f + step * (a - 1) < 4]


def wide_taps(field, taps, cols):
    return jnp.concatenate([field[g * cols : (g + 1) * cols, :] for _, g in taps], axis=1)


def conv_rows(field, kernel, f, cols):
    taps = frames_of(f, 1)
    kernel = kernel[taps[0][0] * 256 : (taps[-1][0] + 1) * 256, :]
    wide = dot(wide_taps(field, taps, cols), kernel)
    return before(wide[:, :256]) + wide[:, 256:512] + after(wide[:, 512:])


def conv_rows_t(field, kernel, f, cols):
    taps = frames_of(f, -1)
    lanes = slice(taps[0][0] * 256, (taps[-1][0] + 1) * 256)
    wide = dot(wide_taps(field, taps, cols), kernel[:, lanes], ((1,), (1,)))
    return after(wide[:, :256]) + wide[:, 256:512] + before(wide[:, 512:])


def blocks_of(dec, edge, place):
    for a in range(3):
        for e in range(3):
            tap = [dec[(a * 3 + b) * 3 + e] for b in range(3)]
            for j in range(2):
                if edge:
                    place(a * 256 + j * 128, e * 256 + j * 128, tap, 2 * j)
                else:
                    for r in range(2):
                        place(a * 256 + j * 128, e * 256 + r * 128, tap, j - r + 1)


def prepare_kernel(latent, dec, rgb, edge, pre, colour, own, field, scr):
    cols = latent.shape[2]

    def put_own(one, two, tap, b):
        own[one : one + 128, two : two + 128] = tap[b]

    def put_edge(one, two, tap, b):
        edge[one : one + 128, two : two + 128] = tap[b]

    edge[...] = jnp.zeros_like(edge)
    blocks_of(dec, False, put_own)
    blocks_of(dec, True, put_edge)
    for f in range(4):
        for r in range(2):
            field[f * cols : (f + 1) * cols, r * 128 : (r + 1) * 128] = latent[f, r]
    for f in range(4):
        pre[f] = conv_rows(field, own, f, cols)
    colour_rows(rgb, scr, (0, 1))
    colour[...] = scr[...].astype(BF16)


def edge_kernel(
    odd_ref, first, second, kernel, own, colour, target,
    act, send_first, send_second, field, parts_out,
    act_s, slope_s, field_s, t_scr, p_scr, parts, sems,
):
    odd = odd_ref[0]
    cols = first.shape[1]
    t_scr[...] = jnp.zeros_like(t_scr)
    for f in range(4):
        t_scr[f * 24 + 18 : f * 24 + 24, :] = target[f * 6 : f * 6 + 6, :].astype(F32)
    p_scr[0:8, :] = jnp.zeros((8, 128), F32)
    p_scr[cols : cols + 8, :] = jnp.zeros((8, 128), F32)
    for f in range(4):
        rows = slice(f * cols, (f + 1) * cols)
        field_s[rows, :128] = jnp.where(odd == 1, first[f], second[f])
        field_s[rows, 128:] = jnp.where(odd == 1, second[f], first[f])
    copies = [
        start(field_s.at[pl.ds(f * cols, cols)], field.at[f], sems.at[f]) for f in range(4)
    ]
    for f in range(4):
        pre = own[f] + conv_rows(field_s, kernel, f, cols)
        gate = sigmoid(pre)
        act_s[:, f * 256 : (f + 1) * 256] = (pre * gate).astype(BF16)
        slope = slope_of(pre, gate).astype(BF16)
        slope_s[0, f] = slope[:, :128]
        slope_s[1, f] = slope[:, 128:]
    copies.append(start(slope_s.at[1 - odd], send_first, sems.at[4]))
    copies.append(start(slope_s.at[odd], send_second, sems.at[5]))
    copies.append(start(act_s, act, sems.at[6]))
    wide = dot(act_s[...], colour[...], ((1,), (1,)))
    part = before(wide[:, :128]) + wide[:, 128:256] + after(wide[:, 256:])
    p_scr[HALO : HALO + cols, :] = part + t_scr[...].T
    blocks, width, _ = parts.shape
    for d in range(blocks):
        at = d * (width - 2 * HALO)
        parts[d] = p_scr[at : at + width, :]
    copies.append(start(parts, parts_out, sems.at[7]))
    for copy in copies:
        copy.wait()


def branch_scratch(bands, wide):
    return [
        pltpu.VMEM((bands * wide, 128), F32),
        pltpu.VMEM((wide + 1, 8, 128), F32),
        pltpu.VMEM((768, 256), BF16),
        pltpu.VMEM((144, 256), BF16),
        pltpu.VMEM((256, 144), BF16),
        pltpu.VMEM((48, 768), BF16),
        pltpu.VMEM((256, 768), BF16),
        pltpu.VMEM((256, 768), BF16),
        pltpu.VMEM((wide, 24, 128), F32),
        pltpu.VMEM((wide, 16, 128), F32),
        pltpu.VMEM((4, wide + 2, 16, 128), BF16),
        pltpu.VMEM((2, wide, 256, 128), BF16),
        pltpu.VMEM((wide, 128, 128), F32),
        pltpu.VMEM((wide, 256, 128), BF16),
        pltpu.VMEM((wide, 256, 128), BF16),
        pltpu.VMEM((bands * (wide - 2 * HALO), 128), F32),
        pltpu.SemaphoreType.DMA((4,)),
    ]


def branch_kernel(
    parts_in, consts_in, w2_in, w1_in,
    out,
    parts, consts, w2_t, w1_t, w1, w1_z, w2, w2_b,
    rows, taps, colours, feats, slopes, grads_two, grads, turned, sems,
):
    copies = [
        start(source, target, sems.at[k])
        for k, (source, target) in enumerate(
            [(parts_in, parts), (consts_in, consts), (w2_in, w2_t), (w1_in, w1_t)]
        )
    ]
    wide = rows.shape[0]
    bands = parts.shape[0] // wide
    own = wide - 2 * HALO
    lane = lax.broadcasted_iota(jnp.int32, (1, 128), 1)
    frame, band = (lane // bands, lane % bands)

    def rolled(value, by):
        by = by % 128
        return value if by == 0 else pltpu.roll(value, by, value.ndim - 1)

    def down(value):
        return jnp.where(band >= 1, rolled(value, 1), 0.0)

    def up(value):
        return jnp.where(band < bands - 1, rolled(value, -1), 0.0)

    def earlier(value):
        return jnp.where(frame >= 1, rolled(value, bands), 0.0)

    def later(value):
        return jnp.where(frame < 3, rolled(value, -bands), 0.0)

    def rounded(value):
        return value.astype(BF16).astype(F32)

    def tile(value, n):
        return value[:, n * 128 : (n + 1) * 128]

    def stacked(get, first, step):
        return jnp.concatenate(
            [
                jnp.concatenate([get(first + n + step * (e - 1)) for e in range(3)], axis=0)
                for n in range(4)
            ],
            axis=1,
        )

    def masks(first):
        return jnp.concatenate([consts[first + n][0:1] for n in range(4)], axis=1)

    taps[...] = jnp.zeros_like(taps)
    colours[...] = jnp.zeros_like(colours)
    grads_two[1] = jnp.zeros((256, 128), BF16)
    grads_two[wide - 2] = jnp.zeros((256, 128), BF16)
    for copy in copies:
        copy.wait()
    w1[...] = w1_t[...].astype(F32).T.astype(BF16)
    w2[...] = w2_t[...].astype(F32).T.astype(BF16)
    for e in range(3):
        w2_b[:, e * 256 : (e + 1) * 256] = w2_t[e * 256 : (e + 1) * 256, :]
        for a in range(3):
            at = (a * 3 + e) * 16
            w1_z[a * 16 : (a + 1) * 16, e * 256 : (e + 1) * 256] = w1_t[at : at + 16, :]
    head = consts[wide].T[:, 0:1]

    for k in range(wide // 4):
        block = jnp.concatenate(
            [parts[pl.ds(4 * k + m, bands, stride=wide), :] for m in range(4)], axis=0
        ).T
        for m in range(4):
            value = jnp.zeros((24, 128), F32)
            for f in range(4):
                piece = rolled(block[f * 24 : (f + 1) * 24], (f - m) * bands)
                value = jnp.where(frame == f, piece, value)
            rows[4 * k + m] = value

    mask = consts[0:wide, 0:1, :]

    def place(even, odd):
        taps[:, 0:3, :] = down(odd)
        taps[:, 3:6, :] = even
        taps[:, 6:9, :] = odd
        taps[:, 9:12, :] = up(even)
        return taps[...]

    colours[0, 1 : wide + 1] = place(rows[:, 18:21, :] * mask, rows[:, 21:24, :] * mask).astype(BF16)
    even = rounded((rows[:, 6:9, :] + down(rows[:, 12:15, :])) * mask)
    odd = rounded((rows[:, 9:12, :] + up(rows[:, 3:6, :])) * mask)
    field = place(even, odd)
    for a, value in enumerate((earlier(field), field, later(field))):
        colours[1 + a, 1 : wide + 1] = value.astype(BF16)

    def keep_feats(kind, first, feat):
        for n in range(4):
            value = tile(feat, n)
            feats[kind, first + n, 0:64] = down(value[64:]).astype(BF16)
            feats[kind, first + n, 64:192] = value.astype(BF16)
            feats[kind, first + n, 192:256] = up(value[:64]).astype(BF16)

    def first_layer(t, carry):
        c = t * 4
        mask = masks(c)
        pre = dot(w1[0:128, 48:96], stacked(lambda at: colours[0, at], c + 1, 1))
        keep_feats(0, c, rounded(pre * sigmoid(pre) * mask))
        field = [stacked(lambda at: colours[1 + a, at], c + 1, 1) for a in range(3)]
        both = dot(w1[...], jnp.concatenate(field, axis=0))
        pre, crit = (both[:128], both[128:])
        gate = sigmoid(pre)
        keep_feats(1, c, rounded(pre * gate * mask))
        slope = slope_of(pre, gate) * mask
        gate = sigmoid(crit)
        scored = crit * gate * head
        slope_c = slope_of(crit, gate) * head * mask
        logits = [jnp.sum(scored[r * 64 : r * 64 + 64], axis=0, keepdims=True) for r in range(2)]
        grad = [-sigmoid(-logits[r]) * slope_c[r * 64 : r * 64 + 64] for r in range(2)]
        grad = jnp.concatenate(grad, axis=0).astype(BF16)
        for n in range(4):
            slopes[c + n] = tile(slope, n)
            grads[c + n, 128:256] = tile(grad, n)
        return carry

    lax.fori_loop(0, wide // 4, first_layer, 0, unroll=True)

    def second_layer(t, carry):
        c = t * 4 + 2
        pre = dot(w2[...], stacked(lambda at: feats[0, at], c, 1))
        wanted = pre * sigmoid(pre)
        pre = dot(w2[...], stacked(lambda at: feats[1, at], c, 1))
        gate = sigmoid(pre)
        gap = pre * gate - wanted
        grad = (0.25 * gap * slope_of(pre, gate) * masks(c)).astype(BF16)
        for n in range(4):
            grads_two[c + n] = tile(grad, n)
        return carry

    lax.fori_loop(0, (wide - 4) // 4, second_layer, 0, unroll=True)

    def second_back(t, carry):
        c = t * 4 + 2
        spread = dot(w2_b[...], stacked(lambda at: grads_two[at], c, -1))
        for n in range(4):
            value = tile(spread, n)
            even = value[64:128] + down(value[192:256])
            odd = value[128:192] + up(value[0:64])
            grad = jnp.concatenate([even, odd], axis=0) * slopes[c + n]
            grads[c + n, 0:128] = grad.astype(BF16)
        return carry

    lax.fori_loop(0, (wide - 4) // 4, second_back, 0, unroll=True)

    def first_back(t, carry):
        c = t * 4 + HALO
        spread = dot(w1_z[...], stacked(lambda at: grads[at], c, -1))
        for n in range(4):
            value = tile(spread, n)
            taps[c + n] = later(value[0:16]) + value[16:32] + earlier(value[32:48])
        return carry

    lax.fori_loop(0, own // 4, first_back, 0, unroll=True)
    mid = slice(HALO, HALO + own)
    even = rounded(taps[mid, 3:6, :] + down(taps[mid, 9:12, :]))
    odd = rounded(taps[mid, 6:9, :] + up(taps[mid, 0:3, :]))
    for k, value in enumerate((down(even), down(odd), even, odd, up(even), up(odd))):
        rows[mid, 3 * k : 3 * k + 3, :] = value
    for k in range(own // 4):
        block = []
        for f in range(4):
            value = jnp.zeros((24, 128), F32)
            for m in range(4):
                piece = rolled(rows[HALO + 4 * k + m], (m - f) * bands)
                value = jnp.where(frame == m, piece, value)
            block.append(value)
        block = jnp.concatenate(block + [jnp.zeros((32, 128), F32)], axis=0).T
        for m in range(4):
            turned[pl.ds(4 * k + m, bands, stride=own), :] = block[m * bands : (m + 1) * bands]
    out[...] = turned[...].astype(BF16)


def taps_of(grad_in, cols):
    grad = grad_in[...].reshape(cols, 128).astype(F32)
    return jnp.concatenate([after(grad), grad, before(grad)], axis=1)


def dec_grad_kernel(
    odd_ref, grad_in, colour_in, first_in, second_in, act_in, latent, edge_in,
    local_out, grad_pre,
    local, colour, slope, act, field, pre_s, moved, gram, sems,
):
    cols = act.shape[0]
    odd = odd_ref[0]
    moves = [
        (colour_in, colour),
        (first_in, slope.at[1 - odd]),
        (second_in, slope.at[odd]),
        (act_in, act),
        (latent.at[:, 0], field.at[:, :, pl.ds(0, 128)]),
        (latent.at[:, 1], field.at[:, :, pl.ds(128, 128)]),
        (edge_in, field.at[:, :, pl.ds(256, 256)]),
    ]
    copies = [start(source, target, sems.at[k]) for k, (source, target) in enumerate(moves)]
    taps = taps_of(grad_in, cols)
    for copy in copies[:3]:
        copy.wait()
    grad_act = dot(taps.astype(BF16), colour[...])
    lane = lax.broadcasted_iota(jnp.int32, (1, cols), 1)
    for f in range(4):
        wide = grad_act[:, f * 256 : (f + 1) * 256]
        zero = (wide[:, :128] * slope[0, f].astype(F32)).astype(BF16)
        one = (wide[:, 128:] * slope[1, f].astype(F32)).astype(BF16)
        pre_s[f * cols : (f + 1) * cols, :128] = zero
        pre_s[f * cols : (f + 1) * cols, 128:] = one
        turned = jnp.concatenate([zero.astype(F32).T, one.astype(F32).T], axis=0)
        later = jnp.where(lane < cols - 1, pltpu.roll(turned, cols - 1, 1), 0.0)
        sooner = jnp.where(lane >= 1, pltpu.roll(turned, 1, 1), 0.0)
        for e, value in enumerate((later, turned, sooner)):
            moved[e * 256 : (e + 1) * 256, f * cols : (f + 1) * cols] = value.astype(BF16)
    outs = [start(pre_s, grad_pre, sems.at[7])]
    copies[3].wait()
    gram[...] = dot(taps.T.astype(BF16), act[...])
    rows = []
    for a in range(3):
        sums = []
        for e in range(3):
            total = jnp.zeros((9, 128), F32)
            for f in range(4):
                to = f - a + 1
                if not 0 <= to < 4:
                    continue
                for r in range(2):
                    at = e * 128 + to * 24 + (r + 1) * 3
                    total += gram[at : at + 9, (f * 2 + r) * 128 : (f * 2 + r + 1) * 128]
            sums.append(total)
        for b in range(3):
            for e in range(3):
                rows.append(sums[e][(2 - b) * 3 : (2 - b) * 3 + 3])
    gram[0:128, 0:128] = jnp.zeros((128, 128), F32)
    for k, value in enumerate(rows):
        gram[k * 3 : k * 3 + 3, 0:128] = value
    local[27 * 128 :, :] = gram[0:128, 0:128].astype(BF16)
    for copy in copies[4:]:
        copy.wait()
    rows_of = (2, 0, 1, 3)
    for a in range(3):
        lo, hi = (max(0, 1 - a), min(4, 5 - a))
        first, last = (lo * cols, hi * cols)
        source = field[lo + a - 1 : hi + a - 1].reshape((hi - lo) * cols, 512)
        for e in range(3):
            wide = dot(moved[e * 256 : (e + 1) * 256, first:last], source)
            for b in range(3):
                one, two = (rows_of[b] * 128, rows_of[b + 1] * 128)
                total = wide[:128, one : one + 128] + wide[128:, two : two + 128]
                at = ((a * 3 + b) * 3 + e) * 128
                local[at : at + 128, :] = total.T.astype(BF16)
        part = pl.ds(a * 9 * 128, 9 * 128 if a < 2 else 10 * 128)
        outs.append(start(local.at[part], local_out.at[part], sems.at[8 + a]))
    for copy in outs:
        copy.wait()


def latent_kernel(
    odd_ref, grad_in, dec, rgb, first, second, pre,
    out,
    own_t, edge_t, colour, edge_s, scr,
):
    cols = first.shape[1]
    odd = odd_ref[0]
    colour_rows(rgb, scr, (-1, 2))
    colour[...] = scr[...].astype(BF16)

    def put_own(one, two, tap, b):
        at, to = (two // 256 * 256 + one % 256, one // 256 * 256 + two % 256)
        own_t[at : at + 128, to : to + 128] = tap[b]

    def put_edge(one, two, tap, b):
        edge_t[two : two + 128, one : one + 128] = tap[2 - b]

    edge_t[...] = jnp.zeros_like(edge_t)
    blocks_of(dec, False, put_own)
    blocks_of(dec, True, put_edge)
    grad_act = dot(taps_of(grad_in, cols).astype(BF16), colour[...])
    for f in range(4):
        slopes = (
            jnp.where(odd == 1, first[f], second[f]),
            jnp.where(odd == 1, second[f], first[f]),
        )
        for k in range(2):
            at = (f * 2 + k) * 128
            value = grad_act[:, at : at + 128] * slopes[k].astype(F32)
            edge_s[f * cols : (f + 1) * cols, k * 128 : (k + 1) * 128] = value.astype(BF16)
    for f in range(4):
        wide = conv_rows_t(pre, own_t, f, cols) + conv_rows_t(edge_s, edge_t, f, cols)
        out[f, 0] = wide[:, :128]
        out[f, 1] = wide[:, 128:]


def branch_weights(vgg_first, vgg_second, critic):
    def paired(taps):
        none = jnp.zeros_like(taps[..., :1, :, :])
        return jnp.stack(
            [jnp.concatenate([taps, none], -3), jnp.concatenate([none, taps], -3)], axis=-4
        )

    first = paired(vgg_first.reshape(3, 9, 64)).reshape(1, 2, 4, 3, 3, 64)
    crit = paired(critic.reshape(3, 3, 9, 64)).reshape(3, 2, 4, 3, 3, 64)
    both = jnp.stack([jnp.pad(first, ((1, 1),) + ((0, 0),) * 5), crit])
    w1_t = both.transpose(1, 4, 3, 5, 0, 2, 6).reshape(9, 12, 256)
    w1_t = jnp.pad(w1_t, ((0, 0), (0, 4), (0, 0))).reshape(144, 256)
    w2_t = paired(vgg_second.transpose(1, 0, 2, 3))
    w2_t = w2_t.transpose(0, 2, 3, 1, 4).reshape(768, 256)
    return (w2_t, w1_t)


def per_device(
    latent, dec_kernel, rgb_kernel, target, vgg_first, vgg_second, critic_kernel, critic_head
):
    size = lax.axis_size("band")
    me = lax.axis_index("band")
    cols = latent.shape[2]
    width = cols // size
    wide = width + 2 * HALO
    pairs = [[(i, i + 1), (i + 1, i)] for i in range(size - 1)]
    first_pairs, second_pairs = (sum(pairs[0::2], []), sum(pairs[1::2], []))
    odd = me % 2
    odd_ref = (jnp.reshape(odd, (1,)).astype(jnp.int32), pltpu.SMEM)

    def row(index):
        return lax.dynamic_index_in_dim(latent, index, 1, keepdims=False)

    first = lax.ppermute(row(1 - odd), "band", first_pairs)
    second = lax.ppermute(row(odd), "band", second_pairs)
    rgb = rgb_kernel.transpose(0, 2, 1, 4, 3)[:, :, ::-1].reshape(9, 9, 128).astype(F32)
    big = 4 * cols * 768 * 640
    square = shape((768, 768), BF16)
    toeplitz = shape((384, 1024), BF16)
    half = shape((4, cols, 128), BF16)
    field = shape((4 * cols, 256), BF16)
    dma = pltpu.SemaphoreType.DMA
    dec = dec_kernel.reshape(27, 128, 128)
    edge_w, pre_own, colour = call(
        prepare_kernel,
        [square, shape((4, cols, 256), F32), toeplitz],
        latent,
        dec,
        rgb,
        scratch=[
            pltpu.VMEM((768, 768), BF16),
            pltpu.VMEM((4 * cols, 256), BF16),
            pltpu.VMEM((384, 1024), F32),
        ],
        macs=big,
        limit=PREPARE_MIB,
    )
    w2_t, w1_t = branch_weights(vgg_first, vgg_second, critic_kernel)
    place = jnp.arange(wide) + me * width - HALO
    mask = jnp.where((place >= 0) & (place < cols), 1.0, 0.0).astype(F32)
    consts = jnp.concatenate(
        [jnp.broadcast_to(mask[:, None], (wide, 128)), jnp.tile(critic_head, 2)[None]]
    )
    consts = jnp.broadcast_to(consts[:, None], (wide + 1, 8, 128))
    act, send_first, send_second, field_edge, parts = call(
        edge_kernel,
        [
            (shape((cols, 1024), BF16), HBM),
            (half, HBM),
            (half, HBM),
            (shape((4, cols, 256), BF16), HBM),
            (shape((size, wide, 128), F32), HBM),
        ],
        odd_ref,
        first,
        second,
        edge_w,
        pre_own,
        colour,
        target.transpose(0, 1, 3, 2).reshape(24, cols),
        scratch=[
            pltpu.VMEM((cols, 1024), BF16),
            pltpu.VMEM((2, 4, cols, 128), BF16),
            pltpu.VMEM((4 * cols, 256), BF16),
            pltpu.VMEM((128, cols), F32),
            pltpu.VMEM((cols + 8, 128), F32),
            pltpu.VMEM((size, wide, 128), F32),
            dma((8,)),
        ],
        macs=big,
        limit=EDGE_MIB,
    )
    parts = lax.all_to_all(parts, "band", 0, 0)
    parts, sent = lax.optimization_barrier((parts, send_first))
    first = lax.ppermute(sent, "band", first_pairs)
    (grad_frames,) = call(
        branch_kernel,
        [shape((size * width, 128), BF16)],
        (parts.reshape(size * wide, 128), HBM),
        (consts, HBM),
        (w2_t, HBM),
        (w1_t, HBM),
        scratch=branch_scratch(size, wide),
        macs=4 * 768 * 768 * 700,
    )
    grad_frames, first, sent = lax.optimization_barrier((grad_frames, first, send_second))
    second = lax.ppermute(sent, "band", second_pairs)
    grad_frames = lax.all_to_all(grad_frames.reshape(size, width, 128), "band", 0, 0)
    local, grad_pre = call(
        dec_grad_kernel,
        [(shape((28 * 128, 128), BF16), HBM), (field, HBM)],
        odd_ref,
        grad_frames,
        (colour, HBM),
        (send_first, HBM),
        (send_second, HBM),
        (act, HBM),
        (latent, HBM),
        (field_edge, HBM),
        scratch=[
            pltpu.VMEM((28 * 128, 128), BF16),
            pltpu.VMEM((384, 1024), BF16),
            pltpu.VMEM((2, 4, cols, 128), BF16),
            pltpu.VMEM((cols, 1024), BF16),
            pltpu.VMEM((4, cols, 512), BF16),
            pltpu.VMEM((4 * cols, 256), BF16),
            pltpu.VMEM((768, 4 * cols), BF16),
            pltpu.VMEM((384, 1024), F32),
            dma((11,)),
        ],
        macs=3 * big,
    )
    local, second = lax.optimization_barrier((local, second))
    pieces = lax.all_to_all(local.reshape(size, -1, 128), "band", 0, 0)
    mine = jnp.sum(pieces.astype(F32), axis=0).astype(BF16)
    whole = lax.all_to_all(jnp.broadcast_to(mine, (size,) + mine.shape), "band", 0, 0)
    (grad_latent,) = call(
        latent_kernel,
        [shape((4, 2, cols, 128), F32)],
        odd_ref,
        grad_frames,
        dec,
        rgb,
        first,
        second,
        grad_pre,
        scratch=[
            pltpu.VMEM((768, 768), BF16),
            pltpu.VMEM((768, 768), BF16),
            pltpu.VMEM((384, 1024), BF16),
            pltpu.VMEM((4 * cols, 256), BF16),
            pltpu.VMEM((384, 1024), F32),
        ],
        macs=2 * big,
    )
    whole = whole.reshape(28 * 128, 128)
    pixels = 4 * latent.shape[1] * size * cols
    factor = float(pixels) ** (-0.5)
    grad_dec = whole[: 27 * 128].astype(F32).reshape(3, 3, 3, 128, 128) * factor
    grad_rgb = whole[27 * 128 : 27 * 128 + 81].astype(F32).reshape(3, 3, 3, 3, 128) * factor
    return (grad_latent, grad_dec, grad_rgb.transpose(0, 1, 2, 4, 3))


def solution(mesh):
    placed = (
        P("clip", "band", None, None),
        P(),
        P(),
        P("clip", "band", None, None),
        P(),
        P(),
        P(),
        P(),
    )
    return jax.shard_map(
        per_device,
        mesh=mesh,
        in_specs=placed,
        out_specs=(
            P("clip", "band", None, None),
            P("clip", None, None, None, None),
            P("clip", None, None, None, None),
        ),
        check_vma=False,
    )
```

```python
import jax
import jax.numpy as jnp
from jax import lax
from jax.experimental import pallas as pl
from jax.experimental.pallas import tpu as pltpu
from jax.sharding import PartitionSpec as P

F32 = jnp.float32
BF16 = jnp.bfloat16
HBM = pltpu.HBM
PREPARE_MIB = 24
EDGE_MIB = 24
ROWS = 80000
SLOTS = 80
HALO = 4


def sigmoid(value):
    return 0.5 * jnp.tanh(0.5 * value) + 0.5


def slope_of(value, gate):
    return gate * (1.0 + value * (1.0 - gate))


def dot(left, right, contract=((1,), (0,))):
    return lax.dot_general(left, right, (contract, ((), ())), preferred_element_type=F32)


def call(kernel, outs, *args, scratch=(), macs=0, limit=60):
    args = [a if isinstance(a, tuple) else (a, pltpu.VMEM) for a in args]
    outs = [o if isinstance(o, tuple) else (o, pltpu.VMEM) for o in outs]
    moved = sum(a.size * a.dtype.itemsize for a, _ in args + outs)
    return pl.pallas_call(
        kernel,
        out_shape=[o for o, _ in outs],
        in_specs=[pl.BlockSpec(memory_space=m) for _, m in args],
        out_specs=[pl.BlockSpec(memory_space=m) for _, m in outs],
        scratch_shapes=list(scratch),
        compiler_params=pltpu.CompilerParams(vmem_limit_bytes=limit * 1024 * 1024),
        cost_estimate=pl.CostEstimate(flops=2 * macs, bytes_accessed=moved, transcendentals=0),
    )(*[a for a, _ in args])


def start(source, target, sem):
    copy = pltpu.make_async_copy(source, target, sem)
    copy.start()
    return copy


def shape(dims, dtype):
    return jax.ShapeDtypeStruct(dims, dtype)


def before(value):
    row = lax.broadcasted_iota(jnp.int32, value.shape, 0)
    return jnp.where(row >= 1, pltpu.roll(value, 1, 0), 0.0)


def after(value):
    size = value.shape[0]
    row = lax.broadcasted_iota(jnp.int32, value.shape, 0)
    return jnp.where(row < size - 1, pltpu.roll(value, size - 1, 0), 0.0)


def colour_rows(rgb, scr, rows):
    scr[...] = jnp.zeros_like(scr)
    for f in range(4):
        for k, j in enumerate(rows):
            lanes = slice((f * 2 + k) * 128, (f * 2 + k + 1) * 128)
            for a in range(3):
                to = f - a + 1
                if not 0 <= to < 4:
                    continue
                for e in range(3):
                    at = e * 128 + to * 24 + (j + 1) * 3
                    scr[at : at + 9, lanes] = rgb[a * 3 + e]


def frames_of(f, step):
    return [(a, f + step * (a - 1)) for a in range(3) if 0 <= f + step * (a - 1) < 4]


def wide_taps(field, taps):
    return jnp.concatenate([field[g] for _, g in taps], axis=1)


def conv_rows(field, kernel, f):
    taps = frames_of(f, 1)
    kernel = kernel[taps[0][0] * 256 : (taps[-1][0] + 1) * 256, :]
    wide = dot(wide_taps(field, taps), kernel)
    return before(wide[:, :256]) + wide[:, 256:512] + after(wide[:, 512:])


def conv_rows_t(pairs, f):
    taps = frames_of(f, -1)
    lanes = slice(taps[0][0] * 256, (taps[-1][0] + 1) * 256)
    wide = sum(
        dot(wide_taps(field, taps), kernel[:, lanes], ((1,), (1,)))
        for field, kernel in pairs
    )
    return after(wide[:, :256]) + wide[:, 256:512] + before(wide[:, 512:])


def blocks_of(dec, edge, place):
    for a in range(3):
        for e in range(3):
            tap = [dec[(a * 3 + b) * 3 + e] for b in range(3)]
            for j in range(2):
                if edge:
                    place(a * 256 + j * 128, e * 256 + j * 128, tap, 2 * j)
                else:
                    for r in range(2):
                        place(a * 256 + j * 128, e * 256 + r * 128, tap, j - r + 1)


def rows_kernel(odd_ref, latent, first, second, sems):
    odd = odd_ref[0]
    copies = [
        start(latent.at[:, 1 - odd], first, sems.at[0]),
        start(latent.at[:, odd], second, sems.at[1]),
    ]
    for copy in copies:
        copy.wait()


def prepare_kernel(
    latent, dec, rgb, vgg_first, vgg_second, critic,
    edge, pre, colour, branch,
    own, field, scr, w1_f, w1, w2, sems,
):
    loads = [
        start(latent.at[:, r], field.at[:, :, pl.ds(r * 128, 128)], sems.at[r]) for r in range(2)
    ]

    def put_own(one, two, tap, b):
        own[one : one + 128, two : two + 128] = tap[b]

    def put_edge(one, two, tap, b):
        edge[one : one + 128, two : two + 128] = tap[b]

    edge[...] = jnp.zeros_like(edge)
    blocks_of(dec, False, put_own)
    blocks_of(dec, True, put_edge)
    w1_f[...] = jnp.zeros_like(w1_f)
    w2[...] = jnp.zeros_like(w2)
    for p in range(2):
        lanes = slice(p * 64, p * 64 + 64)
        kinds = (lanes, slice(128 + p * 64, 192 + p * 64))
        for b in range(3):
            rr = p + b
            for e in range(3):
                at, tap = (e * 256 + rr * 64, (b * 3 + e) * 64)
                w2[at : at + 64, p * 128 : p * 128 + 128] = vgg_second[tap : tap + 64, :]
                at, tap = ((3 + e) * 16 + rr * 3, (b * 3 + e) * 3)
                w1_f[at : at + 3, kinds[0]] = vgg_first[tap : tap + 3, lanes]
                for a in range(3):
                    at, tap = ((a * 3 + e) * 16 + rr * 3, ((a * 3 + b) * 3 + e) * 3)
                    w1_f[at : at + 3, kinds[1]] = critic[tap : tap + 3, lanes]
    w1[...] = w1_f[...].astype(BF16)
    stores = [
        start(w2, branch.at[pl.ds(0, 768)], sems.at[2]),
        start(w1, branch.at[pl.ds(768, 144)], sems.at[3]),
    ]
    for load in loads:
        load.wait()
    for f in range(4):
        pre[f] = conv_rows(field, own, f)
    colour_rows(rgb, scr, (0, 1))
    colour[...] = scr[...].astype(BF16)
    for store in stores:
        store.wait()


def edge_kernel(
    odd_ref, first, second, kernel, own, colour, target,
    kept, parts,
    act_s, slope_s, field_s, t_scr, p_scr, sems,
):
    odd = odd_ref[0]
    cols = first.shape[1]
    copies = []

    def keep(source, target):
        copies.append(start(source, target, sems.at[len(copies)]))

    for f in range(4):
        field_s[f, :, :128] = jnp.where(odd == 1, first[f], second[f])
        field_s[f, :, 128:] = jnp.where(odd == 1, second[f], first[f])
    keep(first, kept.at[3 - odd])
    keep(second, kept.at[2 + odd])
    for f in range(4):
        pre = own[f] + conv_rows(field_s, kernel, f)
        gate = sigmoid(pre)
        act = (pre * gate).astype(BF16)
        slope = slope_of(pre, gate).astype(BF16)
        for r in range(2):
            act_s[r, f] = act[:, r * 128 : (r + 1) * 128]
            slope_s[r, f] = slope[:, r * 128 : (r + 1) * 128]
        keep(slope_s.at[1 - odd, f], kept.at[0, f])
        keep(slope_s.at[odd, f], kept.at[1, f])
        keep(act_s.at[0, f], kept.at[4, f])
        keep(act_s.at[1, f], kept.at[5, f])
    wide = dot(wide_act(act_s), colour[...], ((1,), (1,)))
    part = before(wide[:, :128]) + wide[:, 128:256] + after(wide[:, 256:])
    t_scr[...] = jnp.zeros_like(t_scr)
    for f in range(4):
        t_scr[f * 24 + 18 : f * 24 + 24, :] = target[f * 6 : f * 6 + 6, :].astype(F32)
    p_scr[0:8, :] = jnp.zeros((8, 128), F32)
    p_scr[cols : cols + 8, :] = jnp.zeros((8, 128), F32)
    p_scr[HALO : HALO + cols, :] = part + t_scr[...].T
    blocks, width, _ = parts.shape
    for d in range(blocks):
        at = d * (width - 2 * HALO)
        parts[d] = p_scr[at : at + width, :]
    for copy in copies:
        copy.wait()


def wide_act(act):
    return jnp.concatenate([act[r, f] for f in range(4) for r in range(2)], axis=1)


def branch_scratch(bands, wide):
    return [
        pltpu.VMEM((bands * wide, 128), F32),
        pltpu.VMEM((1, 64), F32),
        pltpu.VMEM((768, 256), BF16),
        pltpu.VMEM((144, 256), BF16),
        pltpu.VMEM((256, 144), BF16),
        pltpu.VMEM((48, 768), BF16),
        pltpu.VMEM((256, 768), BF16),
        pltpu.VMEM((256, 768), BF16),
        pltpu.VMEM((wide, 24, 128), F32),
        pltpu.VMEM((wide, 16, 128), F32),
        pltpu.VMEM((4, wide + 2, 16, 128), BF16),
        pltpu.VMEM((2, wide, 256, 128), BF16),
        pltpu.VMEM((wide, 128, 128), F32),
        pltpu.VMEM((wide, 256, 128), BF16),
        pltpu.VMEM((wide, 256, 128), BF16),
        pltpu.VMEM((bands * (wide - 2 * HALO), 128), F32),
        pltpu.SemaphoreType.DMA((4,)),
    ]


def branch_kernel(
    me_ref, parts_in, branch_in, head_in,
    out,
    parts, head_row, w2_t, w1_t, w1, w1_z, w2, w2_b,
    rows, taps, colours, feats, slopes, grads_two, grads, turned, sems,
):
    copies = [
        start(source, target, sems.at[k])
        for k, (source, target) in enumerate(
            [
                (parts_in, parts),
                (branch_in.at[pl.ds(0, 768)], w2_t),
                (branch_in.at[pl.ds(768, 144)], w1_t),
                (head_in, head_row),
            ]
        )
    ]
    wide = rows.shape[0]
    bands = parts.shape[0] // wide
    own = wide - 2 * HALO
    lane = lax.broadcasted_iota(jnp.int32, (1, 128), 1)
    frame, band = (lane // bands, lane % bands)

    def rolled(value, by):
        by = by % 128
        return value if by == 0 else pltpu.roll(value, by, value.ndim - 1)

    def down(value):
        return jnp.where(band >= 1, rolled(value, 1), 0.0)

    def up(value):
        return jnp.where(band < bands - 1, rolled(value, -1), 0.0)

    def earlier(value):
        return jnp.where(frame >= 1, rolled(value, bands), 0.0)

    def later(value):
        return jnp.where(frame < 3, rolled(value, -bands), 0.0)

    def rounded(value):
        return value.astype(BF16).astype(F32)

    def tile(value, n):
        return value[:, n * 128 : (n + 1) * 128]

    def stacked(get, first, step):
        return jnp.concatenate(
            [
                jnp.concatenate([get(first + n + step * (e - 1)) for e in range(3)], axis=0)
                for n in range(4)
            ],
            axis=1,
        )

    def inside(column):
        place = column + me_ref[0] * own - HALO
        kept = jnp.logical_and(place >= 0, place < own * bands)
        return jnp.full((1, 128), jnp.where(kept, 1.0, 0.0), F32)

    def masks(first):
        return jnp.concatenate([inside(first + n) for n in range(4)], axis=1)

    taps[...] = jnp.zeros_like(taps)
    colours[...] = jnp.zeros_like(colours)
    grads_two[1] = jnp.zeros((256, 128), BF16)
    grads_two[wide - 2] = jnp.zeros((256, 128), BF16)
    for copy in copies:
        copy.wait()
    w1[...] = w1_t[...].astype(F32).T.astype(BF16)
    w2[...] = w2_t[...].astype(F32).T.astype(BF16)
    for e in range(3):
        w2_b[:, e * 256 : (e + 1) * 256] = w2_t[e * 256 : (e + 1) * 256, :]
        for a in range(3):
            at = (a * 3 + e) * 16
            w1_z[a * 16 : (a + 1) * 16, e * 256 : (e + 1) * 256] = w1_t[at : at + 16, :]
    head = jnp.broadcast_to(head_row[...], (8, 64)).T[:, 0:1]
    head = jnp.concatenate([head, head], axis=0)

    for k in range(wide // 4):
        block = jnp.concatenate(
            [parts[pl.ds(4 * k + m, bands, stride=wide), :] for m in range(4)], axis=0
        ).T
        for m in range(4):
            value = jnp.zeros((24, 128), F32)
            for f in range(4):
                piece = rolled(block[f * 24 : (f + 1) * 24], (f - m) * bands)
                value = jnp.where(frame == f, piece, value)
            rows[4 * k + m] = value

    mask = jnp.stack([inside(column) for column in range(wide)])

    def place(even, odd):
        taps[:, 0:3, :] = down(odd)
        taps[:, 3:6, :] = even
        taps[:, 6:9, :] = odd
        taps[:, 9:12, :] = up(even)
        return taps[...]

    colours[0, 1 : wide + 1] = place(rows[:, 18:21, :] * mask, rows[:, 21:24, :] * mask).astype(BF16)
    even = rounded((rows[:, 6:9, :] + down(rows[:, 12:15, :])) * mask)
    odd = rounded((rows[:, 9:12, :] + up(rows[:, 3:6, :])) * mask)
    field = place(even, odd)
    for a, value in enumerate((earlier(field), field, later(field))):
        colours[1 + a, 1 : wide + 1] = value.astype(BF16)

    def keep_feats(kind, first, feat):
        for n in range(4):
            value = tile(feat, n)
            feats[kind, first + n, 0:64] = down(value[64:]).astype(BF16)
            feats[kind, first + n, 64:192] = value.astype(BF16)
            feats[kind, first + n, 192:256] = up(value[:64]).astype(BF16)

    def first_layer(t, carry):
        c = t * 4
        mask = masks(c)
        pre = dot(w1[0:128, 48:96], stacked(lambda at: colours[0, at], c + 1, 1))
        keep_feats(0, c, rounded(pre * sigmoid(pre) * mask))
        field = [stacked(lambda at: colours[1 + a, at], c + 1, 1) for a in range(3)]
        both = dot(w1[...], jnp.concatenate(field, axis=0))
        pre, crit = (both[:128], both[128:])
        gate = sigmoid(pre)
        keep_feats(1, c, rounded(pre * gate * mask))
        slope = slope_of(pre, gate) * mask
        gate = sigmoid(crit)
        scored = crit * gate * head
        slope_c = slope_of(crit, gate) * head * mask
        logits = [jnp.sum(scored[r * 64 : r * 64 + 64], axis=0, keepdims=True) for r in range(2)]
        grad = [-sigmoid(-logits[r]) * slope_c[r * 64 : r * 64 + 64] for r in range(2)]
        grad = jnp.concatenate(grad, axis=0).astype(BF16)
        for n in range(4):
            slopes[c + n] = tile(slope, n)
            grads[c + n, 128:256] = tile(grad, n)
        return carry

    lax.fori_loop(0, wide // 4, first_layer, 0, unroll=True)

    def second_layer(t, carry):
        c = t * 4 + 2
        pre = dot(w2[...], stacked(lambda at: feats[0, at], c, 1))
        wanted = pre * sigmoid(pre)
        pre = dot(w2[...], stacked(lambda at: feats[1, at], c, 1))
        gate = sigmoid(pre)
        gap = pre * gate - wanted
        grad = (0.25 * gap * slope_of(pre, gate) * masks(c)).astype(BF16)
        for n in range(4):
            grads_two[c + n] = tile(grad, n)
        return carry

    lax.fori_loop(0, (wide - 4) // 4, second_layer, 0, unroll=True)

    def second_back(t, carry):
        c = t * 4 + 2
        spread = dot(w2_b[...], stacked(lambda at: grads_two[at], c, -1))
        for n in range(4):
            value = tile(spread, n)
            even = value[64:128] + down(value[192:256])
            odd = value[128:192] + up(value[0:64])
            grad = jnp.concatenate([even, odd], axis=0) * slopes[c + n]
            grads[c + n, 0:128] = grad.astype(BF16)
        return carry

    lax.fori_loop(0, (wide - 4) // 4, second_back, 0, unroll=True)

    def first_back(t, carry):
        c = t * 4 + HALO
        spread = dot(w1_z[...], stacked(lambda at: grads[at], c, -1))
        for n in range(4):
            value = tile(spread, n)
            taps[c + n] = later(value[0:16]) + value[16:32] + earlier(value[32:48])
        return carry

    lax.fori_loop(0, own // 4, first_back, 0, unroll=True)
    mid = slice(HALO, HALO + own)
    even = rounded(taps[mid, 3:6, :] + down(taps[mid, 9:12, :]))
    odd = rounded(taps[mid, 6:9, :] + up(taps[mid, 0:3, :]))
    for k, value in enumerate((down(even), down(odd), even, odd, up(even), up(odd))):
        rows[mid, 3 * k : 3 * k + 3, :] = value
    for k in range(own // 4):
        block = []
        for f in range(4):
            value = jnp.zeros((24, 128), F32)
            for m in range(4):
                piece = rolled(rows[HALO + 4 * k + m], (m - f) * bands)
                value = jnp.where(frame == m, piece, value)
            block.append(value)
        block = jnp.concatenate(block + [jnp.zeros((32, 128), F32)], axis=0).T
        for m in range(4):
            turned[pl.ds(4 * k + m, bands, stride=own), :] = block[m * bands : (m + 1) * bands]
    out[...] = turned[...].astype(BF16)


def taps_of(grad_in, cols):
    grad = grad_in[...].reshape(cols, 128).astype(F32)
    return jnp.concatenate([after(grad), grad, before(grad)], axis=1)


def dec_grad_kernel(
    odd_ref, grad_in, colour_in, kept, latent,
    local_out, grad_pre, grad_kept,
    local, colour, slope, act, field, pre_s, moved, gram, sems,
):
    cols = act.shape[2]
    odd = odd_ref[0]
    moves = [
        (colour_in, colour),
        (kept.at[0], slope.at[1 - odd]),
        (kept.at[1], slope.at[odd]),
        (kept.at[pl.ds(4, 2)], act),
        (latent.at[:, 0], field.at[:, :, pl.ds(0, 128)]),
        (latent.at[:, 1], field.at[:, :, pl.ds(128, 128)]),
        (kept.at[2], field.at[:, :, pl.ds(256, 128)]),
        (kept.at[3], field.at[:, :, pl.ds(384, 128)]),
    ]
    copies = [start(source, target, sems.at[k]) for k, (source, target) in enumerate(moves)]
    taps = taps_of(grad_in, cols)
    for copy in copies[:3]:
        copy.wait()
    grad_act = dot(taps.astype(BF16), colour[...])
    lane = lax.broadcasted_iota(jnp.int32, (1, cols), 1)
    for f in range(4):
        wide = grad_act[:, f * 256 : (f + 1) * 256]
        zero = (wide[:, :128] * slope[0, f].astype(F32)).astype(BF16)
        one = (wide[:, 128:] * slope[1, f].astype(F32)).astype(BF16)
        pre_s[f, :, :128] = zero
        pre_s[f, :, 128:] = one
        turned = jnp.concatenate([zero.astype(F32).T, one.astype(F32).T], axis=0)
        later = jnp.where(lane < cols - 1, pltpu.roll(turned, cols - 1, 1), 0.0)
        sooner = jnp.where(lane >= 1, pltpu.roll(turned, 1, 1), 0.0)
        for e, value in enumerate((later, turned, sooner)):
            moved[e * 256 : (e + 1) * 256, f * cols : (f + 1) * cols] = value.astype(BF16)
    outs = [start(pre_s, grad_pre, sems.at[8])]
    outs.append(start(grad_in, grad_kept, sems.at[7]))
    copies[3].wait()
    gram[...] = dot(taps.T.astype(BF16), wide_act(act))
    rows = []
    for a in range(3):
        sums = []
        for e in range(3):
            total = jnp.zeros((9, 128), F32)
            for f in range(4):
                to = f - a + 1
                if not 0 <= to < 4:
                    continue
                for r in range(2):
                    at = e * 128 + to * 24 + (r + 1) * 3
                    total += gram[at : at + 9, (f * 2 + r) * 128 : (f * 2 + r + 1) * 128]
            sums.append(total)
        for b in range(3):
            for e in range(3):
                rows.append(sums[e][(2 - b) * 3 : (2 - b) * 3 + 3])
    gram[0:128, 0:128] = jnp.zeros((128, 128), F32)
    for k, value in enumerate(rows):
        gram[k * 3 : k * 3 + 3, 0:128] = value
    local[27 * 128 :, :] = gram[0:128, 0:128].astype(BF16)
    last = pl.ds(27 * 128, 128)
    outs.append(start(local.at[last], local_out.at[last], sems.at[36]))
    for copy in copies[4:]:
        copy.wait()
    rows_of = (2, 0, 1, 3)
    for a in range(3):
        lo, hi = (max(0, 1 - a), min(4, 5 - a))
        first, last = (lo * cols, hi * cols)
        source = field[lo + a - 1 : hi + a - 1].reshape((hi - lo) * cols, 512)
        for e in range(3):
            wide = dot(moved[e * 256 : (e + 1) * 256, first:last], source)
            for b in range(3):
                one, two = (rows_of[b] * 128, rows_of[b + 1] * 128)
                total = wide[:128, one : one + 128] + wide[128:, two : two + 128]
                at = ((a * 3 + b) * 3 + e) * 128
                local[at : at + 128, :] = total.T.astype(BF16)
                part = pl.ds(at, 128)
                outs.append(start(local.at[part], local_out.at[part], sems.at[9 + at // 128]))
    for copy in outs:
        copy.wait()


def latent_kernel(
    odd_ref, grad_in, dec, rgb, first, second, pre,
    out,
    own_t, edge_t, colour, edge_s, scr, out_s, sems,
):
    cols = first.shape[1]
    odd = odd_ref[0]
    copies = []
    colour_rows(rgb, scr, (-1, 2))
    colour[...] = scr[...].astype(BF16)

    def put_own(one, two, tap, b):
        at, to = (two // 256 * 256 + one % 256, one // 256 * 256 + two % 256)
        own_t[at : at + 128, to : to + 128] = tap[b]

    def put_edge(one, two, tap, b):
        edge_t[two : two + 128, one : one + 128] = tap[2 - b]

    edge_t[...] = jnp.zeros_like(edge_t)
    blocks_of(dec, False, put_own)
    blocks_of(dec, True, put_edge)
    grad_act = dot(taps_of(grad_in, cols).astype(BF16), colour[...])
    for f in range(4):
        slopes = (
            jnp.where(odd == 1, first[f], second[f]),
            jnp.where(odd == 1, second[f], first[f]),
        )
        for k in range(2):
            at = (f * 2 + k) * 128
            value = grad_act[:, at : at + 128] * slopes[k].astype(F32)
            edge_s[f, :, k * 128 : (k + 1) * 128] = value.astype(BF16)
    for f in range(4):
        wide = conv_rows_t([(pre, own_t), (edge_s, edge_t)], f)
        out_s[f, 0] = wide[:, :128]
        out_s[f, 1] = wide[:, 128:]
        copies.append(start(out_s.at[f], out.at[f], sems.at[f]))
    for copy in copies:
        copy.wait()


def per_device(
    latent, dec_kernel, rgb_kernel, target, vgg_first, vgg_second, critic_kernel, critic_head
):
    size = lax.axis_size("band")
    me = lax.axis_index("band")
    cols = latent.shape[2]
    width = cols // size
    wide = width + 2 * HALO
    pairs = [[(i, i + 1), (i + 1, i)] for i in range(size - 1)]
    first_pairs, second_pairs = (sum(pairs[0::2], []), sum(pairs[1::2], []))
    odd = me % 2
    odd_ref = (jnp.reshape(odd, (1,)).astype(jnp.int32), pltpu.SMEM)

    half = shape((4, cols, 128), BF16)
    sent_first, sent_second = call(
        rows_kernel,
        [half, half],
        odd_ref,
        (latent, HBM),
        scratch=[pltpu.SemaphoreType.DMA((2,))],
        limit=16,
    )
    first = lax.ppermute(sent_first, "band", first_pairs)
    second = lax.ppermute(sent_second, "band", second_pairs)
    rgb = rgb_kernel.transpose(0, 2, 1, 4, 3)[:, :, ::-1].reshape(9, 9, 128).astype(F32)
    big = 4 * cols * 768 * 640
    square = shape((768, 768), BF16)
    toeplitz = shape((384, 1024), BF16)
    field = shape((4, cols, 256), BF16)
    dma = pltpu.SemaphoreType.DMA
    dec = dec_kernel.reshape(27, 128, 128)
    edge_w, pre_own, colour, branch = call(
        prepare_kernel,
        [square, shape((4, cols, 256), F32), toeplitz, (shape((ROWS, 256), BF16), HBM)],
        (latent, HBM),
        dec,
        rgb,
        jnp.tile(vgg_first.reshape(27, 64).astype(F32), (1, 2)),
        vgg_second.reshape(576, 128),
        jnp.tile(critic_kernel.reshape(81, 64).astype(F32), (1, 2)),
        scratch=[
            pltpu.VMEM((768, 768), BF16),
            pltpu.VMEM((4, cols, 256), BF16),
            pltpu.VMEM((384, 1024), F32),
            pltpu.VMEM((144, 256), F32),
            pltpu.VMEM((144, 256), BF16),
            pltpu.VMEM((768, 256), BF16),
            dma((4,)),
        ],
        macs=big,
        limit=PREPARE_MIB,
    )
    kept, parts = call(
        edge_kernel,
        [(shape((SLOTS, 4, cols, 128), BF16), HBM), shape((size, wide, 128), F32)],
        odd_ref,
        first,
        second,
        edge_w,
        pre_own,
        colour,
        target.transpose(0, 1, 3, 2).reshape(24, cols),
        scratch=[
            pltpu.VMEM((2, 4, cols, 128), BF16),
            pltpu.VMEM((2, 4, cols, 128), BF16),
            pltpu.VMEM((4, cols, 256), BF16),
            pltpu.VMEM((128, cols), F32),
            pltpu.VMEM((cols + 8, 128), F32),
            dma((18,)),
        ],
        macs=big,
        limit=EDGE_MIB,
    )
    parts = lax.all_to_all(parts, "band", 0, 0)
    parts, sent = lax.optimization_barrier((parts, kept[0]))
    first = lax.ppermute(sent, "band", first_pairs)
    (grad_frames,) = call(
        branch_kernel,
        [shape((size * width, 128), BF16)],
        (jnp.reshape(me, (1,)).astype(jnp.int32), pltpu.SMEM),
        (parts.reshape(size * wide, 128), HBM),
        (branch, HBM),
        (critic_head.reshape(1, 64), HBM),
        scratch=branch_scratch(size, wide),
        macs=4 * 768 * 768 * 700,
    )
    grad_frames, sent = lax.optimization_barrier((grad_frames, kept[1]))
    second = lax.ppermute(sent, "band", second_pairs)
    grad_frames = lax.all_to_all(grad_frames.reshape(size, width, 128), "band", 0, 0)
    local, grad_pre, grad_kept = call(
        dec_grad_kernel,
        [(shape((28 * 128, 128), BF16), HBM), (field, HBM), (shape((size, width, 128), BF16), HBM)],
        odd_ref,
        grad_frames,
        (colour, HBM),
        (kept, HBM),
        (latent, HBM),
        scratch=[
            pltpu.VMEM((28 * 128, 128), BF16),
            pltpu.VMEM((384, 1024), BF16),
            pltpu.VMEM((2, 4, cols, 128), BF16),
            pltpu.VMEM((2, 4, cols, 128), BF16),
            pltpu.VMEM((4, cols, 512), BF16),
            pltpu.VMEM((4, cols, 256), BF16),
            pltpu.VMEM((768, 4 * cols), BF16),
            pltpu.VMEM((384, 1024), F32),
            dma((37,)),
        ],
        macs=3 * big,
    )
    local, first, second = lax.optimization_barrier((local, first, second))
    pieces = lax.all_to_all(local.reshape(size, -1, 128), "band", 0, 0)
    mine = jnp.sum(pieces.astype(F32), axis=0).astype(BF16)
    whole = lax.all_to_all(jnp.broadcast_to(mine, (size,) + mine.shape), "band", 0, 0)
    (grad_latent,) = call(
        latent_kernel,
        [(shape((4, 2, cols, 128), F32), HBM)],
        odd_ref,
        grad_kept,
        dec,
        rgb,
        first,
        second,
        grad_pre,
        scratch=[
            pltpu.VMEM((768, 768), BF16),
            pltpu.VMEM((768, 768), BF16),
            pltpu.VMEM((384, 1024), BF16),
            pltpu.VMEM((4, cols, 256), BF16),
            pltpu.VMEM((384, 1024), F32),
            pltpu.VMEM((4, 2, cols, 128), F32),
            dma((4,)),
        ],
        macs=2 * big,
    )
    whole = whole.reshape(28 * 128, 128)
    pixels = 4 * latent.shape[1] * size * cols
    factor = float(pixels) ** (-0.5)
    grad_dec = whole[: 27 * 128].astype(F32).reshape(3, 3, 3, 128, 128) * factor
    grad_rgb = whole[27 * 128 : 27 * 128 + 81].astype(F32).reshape(3, 3, 3, 3, 128) * factor
    return (grad_latent, grad_dec, grad_rgb.transpose(0, 1, 2, 4, 3))


def solution(mesh):
    placed = (
        P("clip", "band", None, None),
        P(),
        P(),
        P("clip", "band", None, None),
        P(),
        P(),
        P(),
        P(),
    )
    return jax.shard_map(
        per_device,
        mesh=mesh,
        in_specs=placed,
        out_specs=(
            P("clip", "band", None, None),
            P("clip", None, None, None, None),
            P("clip", None, None, None, None),
        ),
        check_vma=False,
    )
```

```python
import functools

import jax
import jax.numpy as jnp
from jax import lax
from jax.experimental import pallas as pl
from jax.experimental.pallas import tpu as pltpu
from jax.sharding import PartitionSpec as P

F32 = jnp.float32
BF16 = jnp.bfloat16
HBM = pltpu.HBM
PREPARE_MIB = 24
EDGE_MIB = 24
ROWS = 80000
SLOTS = 80
HALO = 4


def sigmoid(value):
    return 0.5 * jnp.tanh(0.5 * value) + 0.5


def slope_of(value, gate):
    return gate * (1.0 + value * (1.0 - gate))


def dot(left, right, contract=((1,), (0,))):
    return lax.dot_general(left, right, (contract, ((), ())), preferred_element_type=F32)


def call(kernel, outs, *args, scratch=(), macs=0, limit=60, aliases=None):
    args = [a if isinstance(a, tuple) else (a, pltpu.VMEM) for a in args]
    outs = [o if isinstance(o, tuple) else (o, pltpu.VMEM) for o in outs]
    moved = sum(a.size * a.dtype.itemsize for a, _ in args + outs)
    return pl.pallas_call(
        kernel,
        out_shape=[o for o, _ in outs],
        in_specs=[pl.BlockSpec(memory_space=m) for _, m in args],
        out_specs=[pl.BlockSpec(memory_space=m) for _, m in outs],
        scratch_shapes=list(scratch),
        input_output_aliases=aliases or {},
        compiler_params=pltpu.CompilerParams(vmem_limit_bytes=limit * 1024 * 1024),
        cost_estimate=pl.CostEstimate(flops=2 * macs, bytes_accessed=moved, transcendentals=0),
    )(*[a for a, _ in args])


def start(source, target, sem):
    copy = pltpu.make_async_copy(source, target, sem)
    copy.start()
    return copy


def shape(dims, dtype):
    return jax.ShapeDtypeStruct(dims, dtype)


def before(value):
    row = lax.broadcasted_iota(jnp.int32, value.shape, 0)
    return jnp.where(row >= 1, pltpu.roll(value, 1, 0), 0.0)


def after(value):
    size = value.shape[0]
    row = lax.broadcasted_iota(jnp.int32, value.shape, 0)
    return jnp.where(row < size - 1, pltpu.roll(value, size - 1, 0), 0.0)


def colour_rows(rgb, scr, rows):
    scr[...] = jnp.zeros_like(scr)
    for f in range(4):
        for k, j in enumerate(rows):
            lanes = slice((f * 2 + k) * 128, (f * 2 + k + 1) * 128)
            for a in range(3):
                to = f - a + 1
                if not 0 <= to < 4:
                    continue
                for e in range(3):
                    at = e * 128 + to * 24 + (j + 1) * 3
                    scr[at : at + 9, lanes] = rgb[a * 3 + e]


def frames_of(f, step):
    return [(a, f + step * (a - 1)) for a in range(3) if 0 <= f + step * (a - 1) < 4]


def wide_taps(field, taps):
    return jnp.concatenate([field[g] for _, g in taps], axis=1)


def conv_rows(field, kernel, f):
    taps = frames_of(f, 1)
    kernel = kernel[taps[0][0] * 256 : (taps[-1][0] + 1) * 256, :]
    wide = dot(wide_taps(field, taps), kernel)
    return before(wide[:, :256]) + wide[:, 256:512] + after(wide[:, 512:])


def conv_rows_t(pairs, f):
    taps = frames_of(f, -1)
    lanes = slice(taps[0][0] * 256, (taps[-1][0] + 1) * 256)
    wide = sum(
        dot(wide_taps(field, taps), kernel[:, lanes], ((1,), (1,)))
        for field, kernel in pairs
    )
    return after(wide[:, :256]) + wide[:, 256:512] + before(wide[:, 512:])


def blocks_of(dec, edge, place):
    for a in range(3):
        for e in range(3):
            tap = [dec[(a * 3 + b) * 3 + e] for b in range(3)]
            for j in range(2):
                if edge:
                    place(a * 256 + j * 128, e * 256 + j * 128, tap, 2 * j)
                else:
                    for r in range(2):
                        place(a * 256 + j * 128, e * 256 + r * 128, tap, j - r + 1)


def rows_kernel(odd_ref, latent, first, second, sems):
    odd = odd_ref[0]
    copies = [
        start(latent.at[:, 1 - odd], first, sems.at[0]),
        start(latent.at[:, odd], second, sems.at[1]),
    ]
    for copy in copies:
        copy.wait()


def prepare_kernel(
    latent, dec, rgb, vgg_first, vgg_second, critic,
    edge, pre, colour, branch,
    own, field, scr, w1_f, w1, w2, sems,
):
    loads = [
        start(latent.at[:, r], field.at[:, :, pl.ds(r * 128, 128)], sems.at[r]) for r in range(2)
    ]

    def put_own(one, two, tap, b):
        own[one : one + 128, two : two + 128] = tap[b]

    def put_edge(one, two, tap, b):
        edge[one : one + 128, two : two + 128] = tap[b]

    edge[...] = jnp.zeros_like(edge)
    blocks_of(dec, False, put_own)
    blocks_of(dec, True, put_edge)
    w1_f[...] = jnp.zeros_like(w1_f)
    w2[...] = jnp.zeros_like(w2)
    for p in range(2):
        lanes = slice(p * 64, p * 64 + 64)
        kinds = (lanes, slice(128 + p * 64, 192 + p * 64))
        for b in range(3):
            rr = p + b
            for e in range(3):
                at, tap = (e * 256 + rr * 64, (b * 3 + e) * 64)
                w2[at : at + 64, p * 128 : p * 128 + 128] = vgg_second[tap : tap + 64, :]
                at, tap = ((3 + e) * 16 + rr * 3, (b * 3 + e) * 3)
                w1_f[at : at + 3, kinds[0]] = vgg_first[tap : tap + 3, lanes]
                for a in range(3):
                    at, tap = ((a * 3 + e) * 16 + rr * 3, ((a * 3 + b) * 3 + e) * 3)
                    w1_f[at : at + 3, kinds[1]] = critic[tap : tap + 3, lanes]
    w1[...] = w1_f[...].astype(BF16)
    stores = [
        start(w2, branch.at[pl.ds(0, 768)], sems.at[2]),
        start(w1, branch.at[pl.ds(768, 144)], sems.at[3]),
    ]
    for load in loads:
        load.wait()
    for f in range(4):
        pre[f] = conv_rows(field, own, f)
    colour_rows(rgb, scr, (0, 1))
    colour[...] = scr[...].astype(BF16)
    for store in stores:
        store.wait()


def edge_kernel(
    odd_ref, first, second, kernel, own, colour, target,
    kept, parts,
    act_s, slope_s, field_s, t_scr, p_scr, sems,
):
    odd = odd_ref[0]
    cols = first.shape[1]
    copies = []

    def keep(source, target):
        copies.append(start(source, target, sems.at[len(copies)]))

    for f in range(4):
        field_s[f, :, :128] = jnp.where(odd == 1, first[f], second[f])
        field_s[f, :, 128:] = jnp.where(odd == 1, second[f], first[f])
    keep(first, kept.at[3 - odd])
    keep(second, kept.at[2 + odd])
    for f in range(4):
        pre = own[f] + conv_rows(field_s, kernel, f)
        gate = sigmoid(pre)
        act = (pre * gate).astype(BF16)
        slope = slope_of(pre, gate).astype(BF16)
        for r in range(2):
            act_s[r, f] = act[:, r * 128 : (r + 1) * 128]
            slope_s[r, f] = slope[:, r * 128 : (r + 1) * 128]
        keep(slope_s.at[1 - odd, f], kept.at[0, f])
        keep(slope_s.at[odd, f], kept.at[1, f])
        keep(act_s.at[0, f], kept.at[4, f])
        keep(act_s.at[1, f], kept.at[5, f])
    wide = dot(wide_act(act_s), colour[...], ((1,), (1,)))
    part = before(wide[:, :128]) + wide[:, 128:256] + after(wide[:, 256:])
    t_scr[...] = jnp.zeros_like(t_scr)
    for f in range(4):
        t_scr[f * 24 + 18 : f * 24 + 24, :] = target[f * 6 : f * 6 + 6, :].astype(F32)
    p_scr[0:8, :] = jnp.zeros((8, 128), F32)
    p_scr[cols : cols + 16, :] = jnp.zeros((16, 128), F32)
    p_scr[HALO : HALO + cols, :] = part + t_scr[...].T
    blocks, length, _ = parts.shape
    for d in range(blocks):
        at = d * (cols // blocks)
        parts[d] = p_scr[at : at + length, :].astype(BF16)
    for copy in copies:
        copy.wait()


def wide_act(act):
    return jnp.concatenate([act[r, f] for f in range(4) for r in range(2)], axis=1)


def branch_scratch(bands, wide):
    return [
        pltpu.VMEM((bands * 2 * (wide - 2 * HALO), 128), F32),
        pltpu.VMEM((1, 64), F32),
        pltpu.VMEM((768, 256), BF16),
        pltpu.VMEM((144, 256), BF16),
        pltpu.VMEM((256, 144), BF16),
        pltpu.VMEM((48, 768), BF16),
        pltpu.VMEM((256, 768), BF16),
        pltpu.VMEM((256, 768), BF16),
        pltpu.VMEM((wide, 24, 128), F32),
        pltpu.VMEM((wide, 16, 128), F32),
        pltpu.VMEM((4, wide + 2, 16, 128), BF16),
        pltpu.VMEM((2, wide, 256, 128), BF16),
        pltpu.VMEM((wide, 128, 128), F32),
        pltpu.VMEM((wide, 256, 128), BF16),
        pltpu.VMEM((wide, 256, 128), BF16),
        pltpu.VMEM((bands * (wide - 2 * HALO), 128), F32),
        pltpu.SemaphoreType.DMA((3,)),
    ]


def branch_kernel(
    me_ref, parts_in, branch_in, head_in,
    out,
    parts, head_row, w2_t, w1_t, w1, w1_z, w2, w2_b,
    rows, taps, colours, feats, slopes, grads_two, grads, turned, sems,
):
    copies = [
        start(source, target, sems.at[k])
        for k, (source, target) in enumerate(
            [
                (branch_in.at[pl.ds(0, 768)], w2_t),
                (branch_in.at[pl.ds(768, 144)], w1_t),
                (head_in, head_row),
            ]
        )
    ]
    wide = rows.shape[0]
    own = wide - 2 * HALO
    bands = parts.shape[0] // (2 * own)
    parts[...] = parts_in[...].astype(F32)
    lane = lax.broadcasted_iota(jnp.int32, (1, 128), 1)
    frame, band = (lane // bands, lane % bands)

    def rolled(value, by):
        by = by % 128
        return value if by == 0 else pltpu.roll(value, by, value.ndim - 1)

    def down(value):
        return jnp.where(band >= 1, rolled(value, 1), 0.0)

    def up(value):
        return jnp.where(band < bands - 1, rolled(value, -1), 0.0)

    def earlier(value):
        return jnp.where(frame >= 1, rolled(value, bands), 0.0)

    def later(value):
        return jnp.where(frame < 3, rolled(value, -bands), 0.0)

    def rounded(value):
        return value.astype(BF16).astype(F32)

    def tile(value, n):
        return value[:, n * 128 : (n + 1) * 128]

    def stacked(get, first, step):
        return jnp.concatenate(
            [
                jnp.concatenate([get(first + n + step * (e - 1)) for e in range(3)], axis=0)
                for n in range(4)
            ],
            axis=1,
        )

    def inside(column):
        place = column + me_ref[0] * own - HALO
        kept = jnp.logical_and(place >= 0, place < own * bands)
        return jnp.full((1, 128), jnp.where(kept, 1.0, 0.0), F32)

    def masks(first):
        return jnp.concatenate([inside(first + n) for n in range(4)], axis=1)

    taps[...] = jnp.zeros_like(taps)
    colours[...] = jnp.zeros_like(colours)
    grads_two[1] = jnp.zeros((256, 128), BF16)
    grads_two[wide - 2] = jnp.zeros((256, 128), BF16)
    for k in range(wide // 4):
        block = jnp.concatenate(
            [parts[pl.ds(4 * k + m, bands, stride=2 * own), :] for m in range(4)], axis=0
        ).T
        for m in range(4):
            value = jnp.zeros((24, 128), F32)
            for f in range(4):
                piece = rolled(block[f * 24 : (f + 1) * 24], (f - m) * bands)
                value = jnp.where(frame == f, piece, value)
            rows[4 * k + m] = value

    mask = jnp.stack([inside(column) for column in range(wide)])

    def place(even, odd):
        taps[:, 0:3, :] = down(odd)
        taps[:, 3:6, :] = even
        taps[:, 6:9, :] = odd
        taps[:, 9:12, :] = up(even)
        return taps[...]

    colours[0, 1 : wide + 1] = place(rows[:, 18:21, :] * mask, rows[:, 21:24, :] * mask).astype(BF16)
    even = rounded((rows[:, 6:9, :] + down(rows[:, 12:15, :])) * mask)
    odd = rounded((rows[:, 9:12, :] + up(rows[:, 3:6, :])) * mask)
    field = place(even, odd)
    for a, value in enumerate((earlier(field), field, later(field))):
        colours[1 + a, 1 : wide + 1] = value.astype(BF16)

    for copy in copies:
        copy.wait()
    w1[...] = w1_t[...].astype(F32).T.astype(BF16)
    w2[...] = w2_t[...].astype(F32).T.astype(BF16)
    for e in range(3):
        w2_b[:, e * 256 : (e + 1) * 256] = w2_t[e * 256 : (e + 1) * 256, :]
        for a in range(3):
            at = (a * 3 + e) * 16
            w1_z[a * 16 : (a + 1) * 16, e * 256 : (e + 1) * 256] = w1_t[at : at + 16, :]
    head = jnp.broadcast_to(head_row[...], (8, 64)).T[:, 0:1]
    head = jnp.concatenate([head, head], axis=0)

    def keep_feats(kind, first, feat):
        for n in range(4):
            value = tile(feat, n)
            feats[kind, first + n, 0:64] = down(value[64:]).astype(BF16)
            feats[kind, first + n, 64:192] = value.astype(BF16)
            feats[kind, first + n, 192:256] = up(value[:64]).astype(BF16)

    def first_layer(t, carry):
        c = t * 4
        mask = masks(c)
        pre = dot(w1[0:128, 48:96], stacked(lambda at: colours[0, at], c + 1, 1))
        keep_feats(0, c, rounded(pre * sigmoid(pre) * mask))
        field = [stacked(lambda at: colours[1 + a, at], c + 1, 1) for a in range(3)]
        both = dot(w1[...], jnp.concatenate(field, axis=0))
        pre, crit = (both[:128], both[128:])
        gate = sigmoid(pre)
        keep_feats(1, c, rounded(pre * gate * mask))
        slope = slope_of(pre, gate) * mask
        gate = sigmoid(crit)
        scored = crit * gate * head
        slope_c = slope_of(crit, gate) * head * mask
        logits = [jnp.sum(scored[r * 64 : r * 64 + 64], axis=0, keepdims=True) for r in range(2)]
        grad = [-sigmoid(-logits[r]) * slope_c[r * 64 : r * 64 + 64] for r in range(2)]
        grad = jnp.concatenate(grad, axis=0).astype(BF16)
        for n in range(4):
            slopes[c + n] = tile(slope, n)
            grads[c + n, 128:256] = tile(grad, n)
        return carry

    lax.fori_loop(0, wide // 4, first_layer, 0, unroll=True)

    def second_layer(t, carry):
        c = t * 4 + 2
        pre = dot(w2[...], stacked(lambda at: feats[0, at], c, 1))
        wanted = pre * sigmoid(pre)
        pre = dot(w2[...], stacked(lambda at: feats[1, at], c, 1))
        gate = sigmoid(pre)
        gap = pre * gate - wanted
        grad = (0.25 * gap * slope_of(pre, gate) * masks(c)).astype(BF16)
        for n in range(4):
            grads_two[c + n] = tile(grad, n)
        return carry

    lax.fori_loop(0, (wide - 4) // 4, second_layer, 0, unroll=True)

    def second_back(t, carry):
        c = t * 4 + 2
        spread = dot(w2_b[...], stacked(lambda at: grads_two[at], c, -1))
        for n in range(4):
            value = tile(spread, n)
            even = value[64:128] + down(value[192:256])
            odd = value[128:192] + up(value[0:64])
            grad = jnp.concatenate([even, odd], axis=0) * slopes[c + n]
            grads[c + n, 0:128] = grad.astype(BF16)
        return carry

    lax.fori_loop(0, (wide - 4) // 4, second_back, 0, unroll=True)

    def first_back(t, carry):
        c = t * 4 + HALO
        spread = dot(w1_z[...], stacked(lambda at: grads[at], c, -1))
        for n in range(4):
            value = tile(spread, n)
            taps[c + n] = later(value[0:16]) + value[16:32] + earlier(value[32:48])
        return carry

    lax.fori_loop(0, own // 4, first_back, 0, unroll=True)
    mid = slice(HALO, HALO + own)
    even = rounded(taps[mid, 3:6, :] + down(taps[mid, 9:12, :]))
    odd = rounded(taps[mid, 6:9, :] + up(taps[mid, 0:3, :]))
    for k, value in enumerate((down(even), down(odd), even, odd, up(even), up(odd))):
        rows[mid, 3 * k : 3 * k + 3, :] = value
    for k in range(own // 4):
        block = []
        for f in range(4):
            value = jnp.zeros((24, 128), F32)
            for m in range(4):
                piece = rolled(rows[HALO + 4 * k + m], (m - f) * bands)
                value = jnp.where(frame == m, piece, value)
            block.append(value)
        block = jnp.concatenate(block + [jnp.zeros((32, 128), F32)], axis=0).T
        for m in range(4):
            turned[pl.ds(4 * k + m, bands, stride=own), :] = block[m * bands : (m + 1) * bands]
    out[...] = turned[...].astype(BF16)


def taps_of(grad_in, cols):
    grad = grad_in[...].reshape(cols, 128).astype(F32)
    return jnp.concatenate([after(grad), grad, before(grad)], axis=1)


def dec_grad_kernel(
    odd_ref, grad_in, colour_in, kept, latent,
    local_out, grad_pre, grad_kept,
    local, colour, slope, act, field, pre_s, moved, gram, sems,
):
    cols = act.shape[2]
    odd = odd_ref[0]
    moves = [
        (colour_in, colour),
        (kept.at[0], slope.at[1 - odd]),
        (kept.at[1], slope.at[odd]),
        (kept.at[pl.ds(4, 2)], act),
        (latent.at[:, 0], field.at[:, :, pl.ds(0, 128)]),
        (latent.at[:, 1], field.at[:, :, pl.ds(128, 128)]),
        (kept.at[2], field.at[:, :, pl.ds(256, 128)]),
        (kept.at[3], field.at[:, :, pl.ds(384, 128)]),
    ]
    copies = [start(source, target, sems.at[k]) for k, (source, target) in enumerate(moves)]
    taps = taps_of(grad_in, cols)
    for copy in copies[:3]:
        copy.wait()
    grad_act = dot(taps.astype(BF16), colour[...])
    lane = lax.broadcasted_iota(jnp.int32, (1, cols), 1)
    for f in range(4):
        wide = grad_act[:, f * 256 : (f + 1) * 256]
        zero = (wide[:, :128] * slope[0, f].astype(F32)).astype(BF16)
        one = (wide[:, 128:] * slope[1, f].astype(F32)).astype(BF16)
        pre_s[f, :, :128] = zero
        pre_s[f, :, 128:] = one
        turned = jnp.concatenate([zero.astype(F32).T, one.astype(F32).T], axis=0)
        later = jnp.where(lane < cols - 1, pltpu.roll(turned, cols - 1, 1), 0.0)
        sooner = jnp.where(lane >= 1, pltpu.roll(turned, 1, 1), 0.0)
        for e, value in enumerate((later, turned, sooner)):
            moved[e * 256 : (e + 1) * 256, f * cols : (f + 1) * cols] = value.astype(BF16)
    outs = [start(pre_s, grad_pre, sems.at[8])]
    outs.append(start(grad_in, grad_kept, sems.at[7]))
    copies[3].wait()
    gram[...] = dot(taps.T.astype(BF16), wide_act(act))
    rows = []
    for a in range(3):
        sums = []
        for e in range(3):
            total = jnp.zeros((9, 128), F32)
            for f in range(4):
                to = f - a + 1
                if not 0 <= to < 4:
                    continue
                for r in range(2):
                    at = e * 128 + to * 24 + (r + 1) * 3
                    total += gram[at : at + 9, (f * 2 + r) * 128 : (f * 2 + r + 1) * 128]
            sums.append(total)
        for b in range(3):
            for e in range(3):
                rows.append(sums[e][(2 - b) * 3 : (2 - b) * 3 + 3])
    gram[0:128, 0:128] = jnp.zeros((128, 128), F32)
    for k, value in enumerate(rows):
        gram[k * 3 : k * 3 + 3, 0:128] = value
    local[27 * 128 :, :] = gram[0:128, 0:128].astype(BF16)
    last = pl.ds(27 * 128, 128)
    outs.append(start(local.at[last], local_out.at[last], sems.at[36]))
    for copy in copies[4:]:
        copy.wait()
    rows_of = (2, 0, 1, 3)
    for a in range(3):
        lo, hi = (max(0, 1 - a), min(4, 5 - a))
        first, last = (lo * cols, hi * cols)
        source = field[lo + a - 1 : hi + a - 1].reshape((hi - lo) * cols, 512)
        for e in range(3):
            wide = dot(moved[e * 256 : (e + 1) * 256, first:last], source)
            for b in range(3):
                one, two = (rows_of[b] * 128, rows_of[b + 1] * 128)
                total = wide[:128, one : one + 128] + wide[128:, two : two + 128]
                at = ((a * 3 + b) * 3 + e) * 128
                local[at : at + 128, :] = total.T.astype(BF16)
                part = pl.ds(at, 128)
                outs.append(start(local.at[part], local_out.at[part], sems.at[9 + at // 128]))
    for copy in outs:
        copy.wait()


def latent_kernel(frames, odd_ref, grad_in, dec, rgb, first, second, pre, *rest):
    out, own_t, edge_t, colour, edge_s, scr, out_s, sems = rest[-8:]
    needed = range(max(0, frames[0] - 1), min(4, frames[-1] + 2))
    cols = first.shape[1]
    odd = odd_ref[0]
    copies = []
    colour_rows(rgb, scr, (-1, 2))
    colour[...] = scr[...].astype(BF16)

    def put_own(one, two, tap, b):
        at, to = (two // 256 * 256 + one % 256, one // 256 * 256 + two % 256)
        own_t[at : at + 128, to : to + 128] = tap[b]

    def put_edge(one, two, tap, b):
        edge_t[two : two + 128, one : one + 128] = tap[2 - b]

    edge_t[...] = jnp.zeros_like(edge_t)
    blocks_of(dec, False, put_own)
    blocks_of(dec, True, put_edge)
    grad_act = dot(taps_of(grad_in, cols).astype(BF16), colour[...])
    for f in needed:
        slopes = (
            jnp.where(odd == 1, first[f], second[f]),
            jnp.where(odd == 1, second[f], first[f]),
        )
        for k in range(2):
            at = (f * 2 + k) * 128
            value = grad_act[:, at : at + 128] * slopes[k].astype(F32)
            edge_s[f, :, k * 128 : (k + 1) * 128] = value.astype(BF16)
    for n, f in enumerate(frames):
        wide = conv_rows_t([(pre, own_t), (edge_s, edge_t)], f)
        out_s[n, 0] = wide[:, :128]
        out_s[n, 1] = wide[:, 128:]
        copies.append(start(out_s.at[n], out.at[f], sems.at[n]))
    for copy in copies:
        copy.wait()


def per_device(
    latent, dec_kernel, rgb_kernel, target, vgg_first, vgg_second, critic_kernel, critic_head
):
    size = lax.axis_size("band")
    me = lax.axis_index("band")
    cols = latent.shape[2]
    width = cols // size
    wide = width + 2 * HALO
    pairs = [[(i, i + 1), (i + 1, i)] for i in range(size - 1)]
    first_pairs, second_pairs = (sum(pairs[0::2], []), sum(pairs[1::2], []))
    odd = me % 2
    odd_ref = (jnp.reshape(odd, (1,)).astype(jnp.int32), pltpu.SMEM)

    half = shape((4, cols, 128), BF16)
    sent_first, sent_second = call(
        rows_kernel,
        [half, half],
        odd_ref,
        (latent, HBM),
        scratch=[pltpu.SemaphoreType.DMA((2,))],
        limit=16,
    )
    first = lax.ppermute(sent_first, "band", first_pairs)
    second = lax.ppermute(sent_second, "band", second_pairs)
    rgb = rgb_kernel.transpose(0, 2, 1, 4, 3)[:, :, ::-1].reshape(9, 9, 128).astype(F32)
    big = 4 * cols * 768 * 640
    square = shape((768, 768), BF16)
    toeplitz = shape((384, 1024), BF16)
    field = shape((4, cols, 256), BF16)
    dma = pltpu.SemaphoreType.DMA
    dec = dec_kernel.reshape(27, 128, 128)
    edge_w, pre_own, colour, branch = call(
        prepare_kernel,
        [square, shape((4, cols, 256), F32), toeplitz, (shape((ROWS, 256), BF16), HBM)],
        (latent, HBM),
        dec,
        rgb,
        jnp.tile(vgg_first.reshape(27, 64).astype(F32), (1, 2)),
        vgg_second.reshape(576, 128),
        jnp.tile(critic_kernel.reshape(81, 64).astype(F32), (1, 2)),
        scratch=[
            pltpu.VMEM((768, 768), BF16),
            pltpu.VMEM((4, cols, 256), BF16),
            pltpu.VMEM((384, 1024), F32),
            pltpu.VMEM((144, 256), F32),
            pltpu.VMEM((144, 256), BF16),
            pltpu.VMEM((768, 256), BF16),
            dma((4,)),
        ],
        macs=big,
        limit=PREPARE_MIB,
    )
    kept, parts = call(
        edge_kernel,
        [(shape((SLOTS, 4, cols, 128), BF16), HBM), shape((size, 2 * width, 128), BF16)],
        odd_ref,
        first,
        second,
        edge_w,
        pre_own,
        colour,
        target.transpose(0, 1, 3, 2).reshape(24, cols),
        scratch=[
            pltpu.VMEM((2, 4, cols, 128), BF16),
            pltpu.VMEM((2, 4, cols, 128), BF16),
            pltpu.VMEM((4, cols, 256), BF16),
            pltpu.VMEM((128, cols), F32),
            pltpu.VMEM((cols + 16, 128), F32),
            dma((18,)),
        ],
        macs=big,
        limit=EDGE_MIB,
    )
    parts = lax.all_to_all(parts, "band", 0, 0)
    parts, sent = lax.optimization_barrier((parts, kept[0]))
    first = lax.ppermute(sent, "band", first_pairs)
    (grad_frames,) = call(
        branch_kernel,
        [shape((size * width, 128), BF16)],
        (jnp.reshape(me, (1,)).astype(jnp.int32), pltpu.SMEM),
        parts.reshape(size * 2 * width, 128),
        (branch, HBM),
        (critic_head.reshape(1, 64), HBM),
        scratch=branch_scratch(size, wide),
        macs=4 * 768 * 768 * 700,
        limit=40,
    )
    grad_frames, sent = lax.optimization_barrier((grad_frames, kept[1]))
    second = lax.ppermute(sent, "band", second_pairs)
    grad_frames = lax.all_to_all(grad_frames.reshape(size, width, 128), "band", 0, 0)
    local, grad_pre, grad_kept = call(
        dec_grad_kernel,
        [(shape((28 * 128, 128), BF16), HBM), (field, HBM), (shape((size, width, 128), BF16), HBM)],
        odd_ref,
        grad_frames,
        (colour, HBM),
        (kept, HBM),
        (latent, HBM),
        scratch=[
            pltpu.VMEM((28 * 128, 128), BF16),
            pltpu.VMEM((384, 1024), BF16),
            pltpu.VMEM((2, 4, cols, 128), BF16),
            pltpu.VMEM((2, 4, cols, 128), BF16),
            pltpu.VMEM((4, cols, 512), BF16),
            pltpu.VMEM((4, cols, 256), BF16),
            pltpu.VMEM((768, 4 * cols), BF16),
            pltpu.VMEM((384, 1024), F32),
            dma((37,)),
        ],
        macs=3 * big,
    )
    local, first, second = lax.optimization_barrier((local, first, second))
    def latent_part(frames, *earlier):
        (grad_latent,) = call(
            functools.partial(latent_kernel, frames),
            [(shape((4, 2, cols, 128), F32), HBM)],
            odd_ref,
            grad_kept,
            dec,
            rgb,
            first,
            second,
            grad_pre,
            *[(part, HBM) for part in earlier],
            scratch=[
                pltpu.VMEM((768, 768), BF16),
                pltpu.VMEM((768, 768), BF16),
                pltpu.VMEM((384, 1024), BF16),
                pltpu.VMEM((4, cols, 256), BF16),
                pltpu.VMEM((384, 1024), F32),
                pltpu.VMEM((2, 2, cols, 128), F32),
                dma((2,)),
            ],
            macs=big,
            aliases={7: 0} if earlier else None,
        )
        return grad_latent

    pieces = lax.all_to_all(local.reshape(size, -1, 128), "band", 0, 0)
    half_done = latent_part((0, 1))
    mine = jnp.sum(pieces.astype(F32), axis=0).astype(BF16)
    mine, half_done = lax.optimization_barrier((mine, half_done))
    whole = lax.all_to_all(jnp.broadcast_to(mine, (size,) + mine.shape), "band", 0, 0)
    grad_latent = latent_part((2, 3), half_done)
    whole = whole.reshape(28 * 128, 128)
    pixels = 4 * latent.shape[1] * size * cols
    factor = float(pixels) ** (-0.5)
    grad_dec = whole[: 27 * 128].astype(F32).reshape(3, 3, 3, 128, 128) * factor
    grad_rgb = whole[27 * 128 : 27 * 128 + 81].astype(F32).reshape(3, 3, 3, 3, 128) * factor
    return (grad_latent, grad_dec, grad_rgb.transpose(0, 1, 2, 4, 3))


def solution(mesh):
    placed = (
        P("clip", "band", None, None),
        P(),
        P(),
        P("clip", "band", None, None),
        P(),
        P(),
        P(),
        P(),
    )
    return jax.shard_map(
        per_device,
        mesh=mesh,
        in_specs=placed,
        out_specs=(
            P("clip", "band", None, None),
            P("clip", None, None, None, None),
            P("clip", None, None, None, None),
        ),
        check_vma=False,
    )
```

```python
import functools

import jax
import jax.numpy as jnp
from jax import lax
from jax.experimental import pallas as pl
from jax.experimental.pallas import tpu as pltpu
from jax.sharding import PartitionSpec as P

F32 = jnp.float32
BF16 = jnp.bfloat16
HBM = pltpu.HBM
PREPARE_MIB = 24
EDGE_MIB = 24
ROWS = 80000
SLOTS = 80
HALO = 4


def sigmoid(value):
    return 0.5 * jnp.tanh(0.5 * value) + 0.5


def slope_of(value, gate):
    return gate * (1.0 + value * (1.0 - gate))


def dot(left, right, contract=((1,), (0,))):
    return lax.dot_general(left, right, (contract, ((), ())), preferred_element_type=F32)


def call(kernel, outs, *args, scratch=(), macs=0, limit=60, aliases=None):
    args = [a if isinstance(a, tuple) else (a, pltpu.VMEM) for a in args]
    outs = [o if isinstance(o, tuple) else (o, pltpu.VMEM) for o in outs]
    moved = sum(a.size * a.dtype.itemsize for a, _ in args + outs)
    return pl.pallas_call(
        kernel,
        out_shape=[o for o, _ in outs],
        in_specs=[pl.BlockSpec(memory_space=m) for _, m in args],
        out_specs=[pl.BlockSpec(memory_space=m) for _, m in outs],
        scratch_shapes=list(scratch),
        input_output_aliases=aliases or {},
        compiler_params=pltpu.CompilerParams(vmem_limit_bytes=limit * 1024 * 1024),
        cost_estimate=pl.CostEstimate(flops=2 * macs, bytes_accessed=moved, transcendentals=0),
    )(*[a for a, _ in args])


def start(source, target, sem):
    copy = pltpu.make_async_copy(source, target, sem)
    copy.start()
    return copy


def shape(dims, dtype):
    return jax.ShapeDtypeStruct(dims, dtype)


def before(value):
    row = lax.broadcasted_iota(jnp.int32, value.shape, 0)
    return jnp.where(row >= 1, pltpu.roll(value, 1, 0), 0.0)


def after(value):
    size = value.shape[0]
    row = lax.broadcasted_iota(jnp.int32, value.shape, 0)
    return jnp.where(row < size - 1, pltpu.roll(value, size - 1, 0), 0.0)


def colour_rows(rgb, scr, rows):
    scr[...] = jnp.zeros_like(scr)
    for f in range(4):
        for k, j in enumerate(rows):
            lanes = slice((f * 2 + k) * 128, (f * 2 + k + 1) * 128)
            for a in range(3):
                to = f - a + 1
                if not 0 <= to < 4:
                    continue
                for e in range(3):
                    at = e * 128 + to * 24 + (j + 1) * 3
                    scr[at : at + 9, lanes] = rgb[a * 3 + e]


def frames_of(f, step):
    return [(a, f + step * (a - 1)) for a in range(3) if 0 <= f + step * (a - 1) < 4]


def wide_taps(field, taps):
    return jnp.concatenate([field[g] for _, g in taps], axis=1)


def conv_rows(field, kernel, f):
    taps = frames_of(f, 1)
    kernel = kernel[taps[0][0] * 256 : (taps[-1][0] + 1) * 256, :]
    wide = dot(wide_taps(field, taps), kernel)
    return before(wide[:, :256]) + wide[:, 256:512] + after(wide[:, 512:])


def conv_rows_t(pairs, f):
    taps = frames_of(f, -1)
    lanes = slice(taps[0][0] * 256, (taps[-1][0] + 1) * 256)
    wide = sum(
        dot(wide_taps(field, taps), kernel[:, lanes], ((1,), (1,)))
        for field, kernel in pairs
    )
    return after(wide[:, :256]) + wide[:, 256:512] + before(wide[:, 512:])


def blocks_of(dec, edge, place):
    for a in range(3):
        for e in range(3):
            tap = [dec[(a * 3 + b) * 3 + e] for b in range(3)]
            for j in range(2):
                if edge:
                    place(a * 256 + j * 128, e * 256 + j * 128, tap, 2 * j)
                else:
                    for r in range(2):
                        place(a * 256 + j * 128, e * 256 + r * 128, tap, j - r + 1)


def rows_kernel(odd_ref, latent, first, second, sems):
    odd = odd_ref[0]
    copies = [
        start(latent.at[:, 1 - odd], first, sems.at[0]),
        start(latent.at[:, odd], second, sems.at[1]),
    ]
    for copy in copies:
        copy.wait()


def prepare_kernel(
    latent, dec, rgb, vgg_first, vgg_second, critic,
    edge, pre, colour, branch,
    own, field, scr, w1_f, w1, w2, sems,
):
    loads = [
        start(latent.at[:, r], field.at[:, :, pl.ds(r * 128, 128)], sems.at[r]) for r in range(2)
    ]

    def put_own(one, two, tap, b):
        own[one : one + 128, two : two + 128] = tap[b]

    def put_edge(one, two, tap, b):
        one, two = (one // 256 * 128, two // 256 * 128)
        edge[b // 2, one : one + 128, two : two + 128] = tap[b]

    blocks_of(dec, False, put_own)
    blocks_of(dec, True, put_edge)
    w1_f[...] = jnp.zeros_like(w1_f)
    w2[...] = jnp.zeros_like(w2)
    for p in range(2):
        lanes = slice(p * 64, p * 64 + 64)
        kinds = (lanes, slice(128 + p * 64, 192 + p * 64))
        for b in range(3):
            rr = p + b
            for e in range(3):
                at, tap = (e * 256 + rr * 64, (b * 3 + e) * 64)
                w2[at : at + 64, p * 128 : p * 128 + 128] = vgg_second[tap : tap + 64, :]
                at, tap = ((3 + e) * 16 + rr * 3, (b * 3 + e) * 3)
                w1_f[at : at + 3, kinds[0]] = vgg_first[tap : tap + 3, lanes]
                for a in range(3):
                    at, tap = ((a * 3 + e) * 16 + rr * 3, ((a * 3 + b) * 3 + e) * 3)
                    w1_f[at : at + 3, kinds[1]] = critic[tap : tap + 3, lanes]
    w1[...] = w1_f[...].astype(BF16)
    stores = [
        start(w2, branch.at[pl.ds(0, 768)], sems.at[2]),
        start(w1, branch.at[pl.ds(768, 144)], sems.at[3]),
    ]
    for load in loads:
        load.wait()
    for f in range(4):
        both = conv_rows(field, own, f)
        pre[0, f] = both[:, :128]
        pre[1, f] = both[:, 128:]
    colour_rows(rgb, scr, (0, 1))
    colour[...] = scr[...].astype(BF16)
    for store in stores:
        store.wait()


def edge_row(source, kernel, own, row, act, slope, keep):
    for f in range(4):
        taps = frames_of(f, 1)
        part = kernel[row, taps[0][0] * 128 : (taps[-1][0] + 1) * 128, :]
        wide = dot(wide_taps(source, taps), part)
        pre = own[row, f] + before(wide[:, :128]) + wide[:, 128:256] + after(wide[:, 256:])
        gate = sigmoid(pre)
        act[f] = (pre * gate).astype(BF16)
        slope[f] = slope_of(pre, gate).astype(BF16)
        keep(f)


def first_edge_kernel(odd_ref, first, kernel, own, act, slope):
    edge_row(first, kernel, own, 1 - odd_ref[0], act, slope, lambda f: None)


def edge_kernel(
    odd_ref, first, second, kernel, own, colour, target, act_first, slope_first,
    kept, parts,
    act_s, slope_s, t_scr, p_scr, sems,
):
    odd = odd_ref[0]
    cols = first.shape[1]
    copies = []

    def keep(source, target):
        copies.append(start(source, target, sems.at[len(copies)]))

    def keep_frame(f):
        keep(slope_s.at[f], kept.at[1, f])
        keep(act_s.at[odd, f], kept.at[4 + odd, f])

    keep(first, kept.at[3 - odd])
    keep(second, kept.at[2 + odd])
    keep(act_first, kept.at[5 - odd])
    keep(slope_first, kept.at[0])
    act_s[1 - odd] = act_first[...]
    edge_row(second, kernel, own, odd, act_s.at[odd], slope_s, keep_frame)
    wide = dot(wide_act(act_s), colour[...], ((1,), (1,)))
    part = before(wide[:, :128]) + wide[:, 128:256] + after(wide[:, 256:])
    t_scr[...] = jnp.zeros_like(t_scr)
    for f in range(4):
        t_scr[f * 24 + 18 : f * 24 + 24, :] = target[f * 6 : f * 6 + 6, :].astype(F32)
    p_scr[0:8, :] = jnp.zeros((8, 128), F32)
    p_scr[cols : cols + 16, :] = jnp.zeros((16, 128), F32)
    p_scr[HALO : HALO + cols, :] = part + t_scr[...].T
    blocks, length, _ = parts.shape
    for d in range(blocks):
        at = d * (cols // blocks)
        parts[d] = p_scr[at : at + length, :].astype(BF16)
    for copy in copies:
        copy.wait()


def wide_act(act):
    return jnp.concatenate([act[r, f] for f in range(4) for r in range(2)], axis=1)


def branch_scratch(bands, wide):
    return [
        pltpu.VMEM((bands * 2 * (wide - 2 * HALO), 128), F32),
        pltpu.VMEM((1, 64), F32),
        pltpu.VMEM((768, 256), BF16),
        pltpu.VMEM((144, 256), BF16),
        pltpu.VMEM((256, 144), BF16),
        pltpu.VMEM((48, 768), BF16),
        pltpu.VMEM((256, 768), BF16),
        pltpu.VMEM((256, 768), BF16),
        pltpu.VMEM((wide, 24, 128), F32),
        pltpu.VMEM((wide, 16, 128), F32),
        pltpu.VMEM((4, wide + 2, 16, 128), BF16),
        pltpu.VMEM((2, wide, 256, 128), BF16),
        pltpu.VMEM((wide, 128, 128), F32),
        pltpu.VMEM((wide, 256, 128), BF16),
        pltpu.VMEM((wide, 256, 128), BF16),
        pltpu.VMEM((bands * (wide - 2 * HALO), 128), F32),
        pltpu.SemaphoreType.DMA((3,)),
    ]


def branch_kernel(
    me_ref, parts_in, branch_in, head_in,
    out,
    parts, head_row, w2_t, w1_t, w1, w1_z, w2, w2_b,
    rows, taps, colours, feats, slopes, grads_two, grads, turned, sems,
):
    copies = [
        start(source, target, sems.at[k])
        for k, (source, target) in enumerate(
            [
                (branch_in.at[pl.ds(0, 768)], w2_t),
                (branch_in.at[pl.ds(768, 144)], w1_t),
                (head_in, head_row),
            ]
        )
    ]
    wide = rows.shape[0]
    own = wide - 2 * HALO
    bands = parts.shape[0] // (2 * own)
    parts[...] = parts_in[...].astype(F32)
    lane = lax.broadcasted_iota(jnp.int32, (1, 128), 1)
    frame, band = (lane // bands, lane % bands)

    def rolled(value, by):
        by = by % 128
        return value if by == 0 else pltpu.roll(value, by, value.ndim - 1)

    def down(value):
        return jnp.where(band >= 1, rolled(value, 1), 0.0)

    def up(value):
        return jnp.where(band < bands - 1, rolled(value, -1), 0.0)

    def earlier(value):
        return jnp.where(frame >= 1, rolled(value, bands), 0.0)

    def later(value):
        return jnp.where(frame < 3, rolled(value, -bands), 0.0)

    def rounded(value):
        return value.astype(BF16).astype(F32)

    def tile(value, n):
        return value[:, n * 128 : (n + 1) * 128]

    def stacked(get, first, step):
        return jnp.concatenate(
            [
                jnp.concatenate([get(first + n + step * (e - 1)) for e in range(3)], axis=0)
                for n in range(4)
            ],
            axis=1,
        )

    def inside(column):
        place = column + me_ref[0] * own - HALO
        kept = jnp.logical_and(place >= 0, place < own * bands)
        return jnp.full((1, 128), jnp.where(kept, 1.0, 0.0), F32)

    def masks(first):
        return jnp.concatenate([inside(first + n) for n in range(4)], axis=1)

    taps[...] = jnp.zeros_like(taps)
    colours[...] = jnp.zeros_like(colours)
    grads_two[1] = jnp.zeros((256, 128), BF16)
    grads_two[wide - 2] = jnp.zeros((256, 128), BF16)
    for k in range(wide // 4):
        block = jnp.concatenate(
            [parts[pl.ds(4 * k + m, bands, stride=2 * own), :] for m in range(4)], axis=0
        ).T
        for m in range(4):
            value = jnp.zeros((24, 128), F32)
            for f in range(4):
                piece = rolled(block[f * 24 : (f + 1) * 24], (f - m) * bands)
                value = jnp.where(frame == f, piece, value)
            rows[4 * k + m] = value

    mask = jnp.stack([inside(column) for column in range(wide)])

    def place(even, odd):
        taps[:, 0:3, :] = down(odd)
        taps[:, 3:6, :] = even
        taps[:, 6:9, :] = odd
        taps[:, 9:12, :] = up(even)
        return taps[...]

    colours[0, 1 : wide + 1] = place(rows[:, 18:21, :] * mask, rows[:, 21:24, :] * mask).astype(BF16)
    even = rounded((rows[:, 6:9, :] + down(rows[:, 12:15, :])) * mask)
    odd = rounded((rows[:, 9:12, :] + up(rows[:, 3:6, :])) * mask)
    field = place(even, odd)
    for a, value in enumerate((earlier(field), field, later(field))):
        colours[1 + a, 1 : wide + 1] = value.astype(BF16)

    for copy in copies:
        copy.wait()
    w1[...] = w1_t[...].astype(F32).T.astype(BF16)
    w2[...] = w2_t[...].astype(F32).T.astype(BF16)
    for e in range(3):
        w2_b[:, e * 256 : (e + 1) * 256] = w2_t[e * 256 : (e + 1) * 256, :]
        for a in range(3):
            at = (a * 3 + e) * 16
            w1_z[a * 16 : (a + 1) * 16, e * 256 : (e + 1) * 256] = w1_t[at : at + 16, :]
    head = jnp.broadcast_to(head_row[...], (8, 64)).T[:, 0:1]
    head = jnp.concatenate([head, head], axis=0)

    def keep_feats(kind, first, feat):
        for n in range(4):
            value = tile(feat, n)
            feats[kind, first + n, 0:64] = down(value[64:]).astype(BF16)
            feats[kind, first + n, 64:192] = value.astype(BF16)
            feats[kind, first + n, 192:256] = up(value[:64]).astype(BF16)

    def first_layer(t, carry):
        c = t * 4
        mask = masks(c)
        pre = dot(w1[0:128, 48:96], stacked(lambda at: colours[0, at], c + 1, 1))
        keep_feats(0, c, rounded(pre * sigmoid(pre) * mask))
        field = [stacked(lambda at: colours[1 + a, at], c + 1, 1) for a in range(3)]
        both = dot(w1[...], jnp.concatenate(field, axis=0))
        pre, crit = (both[:128], both[128:])
        gate = sigmoid(pre)
        keep_feats(1, c, rounded(pre * gate * mask))
        slope = slope_of(pre, gate) * mask
        gate = sigmoid(crit)
        scored = crit * gate * head
        slope_c = slope_of(crit, gate) * head * mask
        logits = [jnp.sum(scored[r * 64 : r * 64 + 64], axis=0, keepdims=True) for r in range(2)]
        grad = [-sigmoid(-logits[r]) * slope_c[r * 64 : r * 64 + 64] for r in range(2)]
        grad = jnp.concatenate(grad, axis=0).astype(BF16)
        for n in range(4):
            slopes[c + n] = tile(slope, n)
            grads[c + n, 128:256] = tile(grad, n)
        return carry

    lax.fori_loop(0, wide // 4, first_layer, 0, unroll=True)

    def second_layer(t, carry):
        c = t * 4 + 2
        pre = dot(w2[...], stacked(lambda at: feats[0, at], c, 1))
        wanted = pre * sigmoid(pre)
        pre = dot(w2[...], stacked(lambda at: feats[1, at], c, 1))
        gate = sigmoid(pre)
        gap = pre * gate - wanted
        grad = (0.25 * gap * slope_of(pre, gate) * masks(c)).astype(BF16)
        for n in range(4):
            grads_two[c + n] = tile(grad, n)
        return carry

    lax.fori_loop(0, (wide - 4) // 4, second_layer, 0, unroll=True)

    def second_back(t, carry):
        c = t * 4 + 2
        spread = dot(w2_b[...], stacked(lambda at: grads_two[at], c, -1))
        for n in range(4):
            value = tile(spread, n)
            even = value[64:128] + down(value[192:256])
            odd = value[128:192] + up(value[0:64])
            grad = jnp.concatenate([even, odd], axis=0) * slopes[c + n]
            grads[c + n, 0:128] = grad.astype(BF16)
        return carry

    lax.fori_loop(0, (wide - 4) // 4, second_back, 0, unroll=True)

    def first_back(t, carry):
        c = t * 4 + HALO
        spread = dot(w1_z[...], stacked(lambda at: grads[at], c, -1))
        for n in range(4):
            value = tile(spread, n)
            taps[c + n] = later(value[0:16]) + value[16:32] + earlier(value[32:48])
        return carry

    lax.fori_loop(0, own // 4, first_back, 0, unroll=True)
    mid = slice(HALO, HALO + own)
    even = rounded(taps[mid, 3:6, :] + down(taps[mid, 9:12, :]))
    odd = rounded(taps[mid, 6:9, :] + up(taps[mid, 0:3, :]))
    for k, value in enumerate((down(even), down(odd), even, odd, up(even), up(odd))):
        rows[mid, 3 * k : 3 * k + 3, :] = value
    for k in range(own // 4):
        block = []
        for f in range(4):
            value = jnp.zeros((24, 128), F32)
            for m in range(4):
                piece = rolled(rows[HALO + 4 * k + m], (m - f) * bands)
                value = jnp.where(frame == m, piece, value)
            block.append(value)
        block = jnp.concatenate(block + [jnp.zeros((32, 128), F32)], axis=0).T
        for m in range(4):
            turned[pl.ds(4 * k + m, bands, stride=own), :] = block[m * bands : (m + 1) * bands]
    out[...] = turned[...].astype(BF16)


def taps_of(grad_in, cols):
    grad = grad_in[...].reshape(cols, 128).astype(F32)
    return jnp.concatenate([after(grad), grad, before(grad)], axis=1)


def dec_grad_kernel(
    odd_ref, grad_in, colour_in, kept, latent,
    local_out, grad_pre, grad_kept,
    local, colour, slope, act, field, pre_s, moved, gram, sems,
):
    cols = act.shape[2]
    odd = odd_ref[0]
    moves = [
        (colour_in, colour),
        (kept.at[0], slope.at[1 - odd]),
        (kept.at[1], slope.at[odd]),
        (kept.at[pl.ds(4, 2)], act),
        (latent.at[:, 0], field.at[:, :, pl.ds(0, 128)]),
        (latent.at[:, 1], field.at[:, :, pl.ds(128, 128)]),
        (kept.at[2], field.at[:, :, pl.ds(256, 128)]),
        (kept.at[3], field.at[:, :, pl.ds(384, 128)]),
    ]
    copies = [start(source, target, sems.at[k]) for k, (source, target) in enumerate(moves)]
    taps = taps_of(grad_in, cols)
    for copy in copies[:3]:
        copy.wait()
    grad_act = dot(taps.astype(BF16), colour[...])
    lane = lax.broadcasted_iota(jnp.int32, (1, cols), 1)
    for f in range(4):
        wide = grad_act[:, f * 256 : (f + 1) * 256]
        zero = (wide[:, :128] * slope[0, f].astype(F32)).astype(BF16)
        one = (wide[:, 128:] * slope[1, f].astype(F32)).astype(BF16)
        pre_s[f, :, :128] = zero
        pre_s[f, :, 128:] = one
        turned = jnp.concatenate([zero.astype(F32).T, one.astype(F32).T], axis=0)
        later = jnp.where(lane < cols - 1, pltpu.roll(turned, cols - 1, 1), 0.0)
        sooner = jnp.where(lane >= 1, pltpu.roll(turned, 1, 1), 0.0)
        for e, value in enumerate((later, turned, sooner)):
            moved[e * 256 : (e + 1) * 256, f * cols : (f + 1) * cols] = value.astype(BF16)
    outs = [start(pre_s, grad_pre, sems.at[8])]
    outs.append(start(grad_in, grad_kept, sems.at[7]))
    copies[3].wait()
    gram[...] = dot(taps.T.astype(BF16), wide_act(act))
    rows = []
    for a in range(3):
        sums = []
        for e in range(3):
            total = jnp.zeros((9, 128), F32)
            for f in range(4):
                to = f - a + 1
                if not 0 <= to < 4:
                    continue
                for r in range(2):
                    at = e * 128 + to * 24 + (r + 1) * 3
                    total += gram[at : at + 9, (f * 2 + r) * 128 : (f * 2 + r + 1) * 128]
            sums.append(total)
        for b in range(3):
            for e in range(3):
                rows.append(sums[e][(2 - b) * 3 : (2 - b) * 3 + 3])
    gram[0:128, 0:128] = jnp.zeros((128, 128), F32)
    for k, value in enumerate(rows):
        gram[k * 3 : k * 3 + 3, 0:128] = value
    local[27 * 128 :, :] = gram[0:128, 0:128].astype(BF16)
    last = pl.ds(27 * 128, 128)
    outs.append(start(local.at[last], local_out.at[last], sems.at[36]))
    for copy in copies[4:]:
        copy.wait()
    rows_of = (2, 0, 1, 3)
    for a in range(3):
        lo, hi = (max(0, 1 - a), min(4, 5 - a))
        first, last = (lo * cols, hi * cols)
        source = field[lo + a - 1 : hi + a - 1].reshape((hi - lo) * cols, 512)
        for e in range(3):
            wide = dot(moved[e * 256 : (e + 1) * 256, first:last], source)
            for b in range(3):
                one, two = (rows_of[b] * 128, rows_of[b + 1] * 128)
                total = wide[:128, one : one + 128] + wide[128:, two : two + 128]
                at = ((a * 3 + b) * 3 + e) * 128
                local[at : at + 128, :] = total.T.astype(BF16)
                part = pl.ds(at, 128)
                outs.append(start(local.at[part], local_out.at[part], sems.at[9 + at // 128]))
    for copy in outs:
        copy.wait()


def latent_kernel(frames, odd_ref, grad_in, dec, rgb, first, second, pre, *rest):
    out, own_t, edge_t, colour, edge_s, scr, out_s, sems = rest[-8:]
    needed = range(max(0, frames[0] - 1), min(4, frames[-1] + 2))
    cols = first.shape[1]
    odd = odd_ref[0]
    copies = []
    colour_rows(rgb, scr, (-1, 2))
    colour[...] = scr[...].astype(BF16)

    def put_own(one, two, tap, b):
        at, to = (two // 256 * 256 + one % 256, one // 256 * 256 + two % 256)
        own_t[at : at + 128, to : to + 128] = tap[b]

    def put_edge(one, two, tap, b):
        edge_t[two : two + 128, one : one + 128] = tap[2 - b]

    edge_t[...] = jnp.zeros_like(edge_t)
    blocks_of(dec, False, put_own)
    blocks_of(dec, True, put_edge)
    grad_act = dot(taps_of(grad_in, cols).astype(BF16), colour[...])
    for f in needed:
        slopes = (
            jnp.where(odd == 1, first[f], second[f]),
            jnp.where(odd == 1, second[f], first[f]),
        )
        for k in range(2):
            at = (f * 2 + k) * 128
            value = grad_act[:, at : at + 128] * slopes[k].astype(F32)
            edge_s[f, :, k * 128 : (k + 1) * 128] = value.astype(BF16)
    for n, f in enumerate(frames):
        wide = conv_rows_t([(pre, own_t), (edge_s, edge_t)], f)
        out_s[n, 0] = wide[:, :128]
        out_s[n, 1] = wide[:, 128:]
        copies.append(start(out_s.at[n], out.at[f], sems.at[n]))
    for copy in copies:
        copy.wait()


def per_device(
    latent, dec_kernel, rgb_kernel, target, vgg_first, vgg_second, critic_kernel, critic_head
):
    size = lax.axis_size("band")
    me = lax.axis_index("band")
    cols = latent.shape[2]
    width = cols // size
    wide = width + 2 * HALO
    pairs = [[(i, i + 1), (i + 1, i)] for i in range(size - 1)]
    first_pairs, second_pairs = (sum(pairs[0::2], []), sum(pairs[1::2], []))
    odd = me % 2
    odd_ref = (jnp.reshape(odd, (1,)).astype(jnp.int32), pltpu.SMEM)

    half = shape((4, cols, 128), BF16)
    sent_first, sent_second = call(
        rows_kernel,
        [half, half],
        odd_ref,
        (latent, HBM),
        scratch=[pltpu.SemaphoreType.DMA((2,))],
        limit=16,
    )
    first = lax.ppermute(sent_first, "band", first_pairs)
    second = lax.ppermute(sent_second, "band", second_pairs)
    rgb = rgb_kernel.transpose(0, 2, 1, 4, 3)[:, :, ::-1].reshape(9, 9, 128).astype(F32)
    big = 4 * cols * 768 * 640
    toeplitz = shape((384, 1024), BF16)
    field = shape((4, cols, 256), BF16)
    dma = pltpu.SemaphoreType.DMA
    dec = dec_kernel.reshape(27, 128, 128)
    edge_w, pre_own, colour, branch = call(
        prepare_kernel,
        [shape((2, 384, 384), BF16), shape((2, 4, cols, 128), F32), toeplitz, (shape((ROWS, 256), BF16), HBM)],
        (latent, HBM),
        dec,
        rgb,
        jnp.tile(vgg_first.reshape(27, 64).astype(F32), (1, 2)),
        vgg_second.reshape(576, 128),
        jnp.tile(critic_kernel.reshape(81, 64).astype(F32), (1, 2)),
        scratch=[
            pltpu.VMEM((768, 768), BF16),
            pltpu.VMEM((4, cols, 256), BF16),
            pltpu.VMEM((384, 1024), F32),
            pltpu.VMEM((144, 256), F32),
            pltpu.VMEM((144, 256), BF16),
            pltpu.VMEM((768, 256), BF16),
            dma((4,)),
        ],
        macs=big,
        limit=PREPARE_MIB,
    )
    act_first, slope_first = call(
        first_edge_kernel, [half, half], odd_ref, first, edge_w, pre_own, macs=big // 2, limit=EDGE_MIB
    )
    kept, parts = call(
        edge_kernel,
        [(shape((SLOTS, 4, cols, 128), BF16), HBM), shape((size, 2 * width, 128), BF16)],
        odd_ref,
        first,
        second,
        edge_w,
        pre_own,
        colour,
        target.transpose(0, 1, 3, 2).reshape(24, cols),
        act_first,
        slope_first,
        scratch=[
            pltpu.VMEM((2, 4, cols, 128), BF16),
            pltpu.VMEM((4, cols, 128), BF16),
            pltpu.VMEM((128, cols), F32),
            pltpu.VMEM((cols + 16, 128), F32),
            dma((12,)),
        ],
        macs=big,
        limit=EDGE_MIB,
    )
    parts = lax.all_to_all(parts, "band", 0, 0)
    parts, sent = lax.optimization_barrier((parts, kept[0]))
    first = lax.ppermute(sent, "band", first_pairs)
    (grad_frames,) = call(
        branch_kernel,
        [shape((size * width, 128), BF16)],
        (jnp.reshape(me, (1,)).astype(jnp.int32), pltpu.SMEM),
        parts.reshape(size * 2 * width, 128),
        (branch, HBM),
        (critic_head.reshape(1, 64), HBM),
        scratch=branch_scratch(size, wide),
        macs=4 * 768 * 768 * 700,
        limit=40,
    )
    grad_frames, sent = lax.optimization_barrier((grad_frames, kept[1]))
    second = lax.ppermute(sent, "band", second_pairs)
    grad_frames = lax.all_to_all(grad_frames.reshape(size, width, 128), "band", 0, 0)
    local, grad_pre, grad_kept = call(
        dec_grad_kernel,
        [(shape((28 * 128, 128), BF16), HBM), (field, HBM), (shape((size, width, 128), BF16), HBM)],
        odd_ref,
        grad_frames,
        (colour, HBM),
        (kept, HBM),
        (latent, HBM),
        scratch=[
            pltpu.VMEM((28 * 128, 128), BF16),
            pltpu.VMEM((384, 1024), BF16),
            pltpu.VMEM((2, 4, cols, 128), BF16),
            pltpu.VMEM((2, 4, cols, 128), BF16),
            pltpu.VMEM((4, cols, 512), BF16),
            pltpu.VMEM((4, cols, 256), BF16),
            pltpu.VMEM((768, 4 * cols), BF16),
            pltpu.VMEM((384, 1024), F32),
            dma((37,)),
        ],
        macs=3 * big,
    )
    local, first, second = lax.optimization_barrier((local, first, second))
    def latent_part(frames, *earlier):
        (grad_latent,) = call(
            functools.partial(latent_kernel, frames),
            [(shape((4, 2, cols, 128), F32), HBM)],
            odd_ref,
            grad_kept,
            dec,
            rgb,
            first,
            second,
            grad_pre,
            *[(part, HBM) for part in earlier],
            scratch=[
                pltpu.VMEM((768, 768), BF16),
                pltpu.VMEM((768, 768), BF16),
                pltpu.VMEM((384, 1024), BF16),
                pltpu.VMEM((4, cols, 256), BF16),
                pltpu.VMEM((384, 1024), F32),
                pltpu.VMEM((2, 2, cols, 128), F32),
                dma((2,)),
            ],
            macs=big,
            aliases={7: 0} if earlier else None,
        )
        return grad_latent

    pieces = lax.all_to_all(local.reshape(size, -1, 128), "band", 0, 0)
    half_done = latent_part((0, 1))
    mine = jnp.sum(pieces.astype(F32), axis=0).astype(BF16)
    mine, half_done = lax.optimization_barrier((mine, half_done))
    whole = lax.all_to_all(jnp.broadcast_to(mine, (size,) + mine.shape), "band", 0, 0)
    grad_latent = latent_part((2, 3), half_done)
    whole = whole.reshape(28 * 128, 128)
    pixels = 4 * latent.shape[1] * size * cols
    factor = float(pixels) ** (-0.5)
    grad_dec = whole[: 27 * 128].astype(F32).reshape(3, 3, 3, 128, 128) * factor
    grad_rgb = whole[27 * 128 : 27 * 128 + 81].astype(F32).reshape(3, 3, 3, 3, 128) * factor
    return (grad_latent, grad_dec, grad_rgb.transpose(0, 1, 2, 4, 3))


def solution(mesh):
    placed = (
        P("clip", "band", None, None),
        P(),
        P(),
        P("clip", "band", None, None),
        P(),
        P(),
        P(),
        P(),
    )
    return jax.shard_map(
        per_device,
        mesh=mesh,
        in_specs=placed,
        out_specs=(
            P("clip", "band", None, None),
            P("clip", None, None, None, None),
            P("clip", None, None, None, None),
        ),
        check_vma=False,
    )
```

```python
import jax
import jax.numpy as jnp
from jax import lax
from jax.experimental import pallas as pl
from jax.experimental.pallas import tpu as pltpu
from jax.sharding import PartitionSpec as P

F32 = jnp.float32
BF16 = jnp.bfloat16
HBM = pltpu.HBM
PREPARE_MIB = 24
EDGE_MIB = 24
LATE = 110
ROWS = 60000
SLOTS = 60
HALO = 4


def sigmoid(value):
    return 0.5 * jnp.tanh(0.5 * value) + 0.5


def slope_of(value, gate):
    return gate * (1.0 + value * (1.0 - gate))


def dot(left, right, contract=((1,), (0,))):
    return lax.dot_general(left, right, (contract, ((), ())), preferred_element_type=F32)


def call(kernel, outs, *args, scratch=(), macs=0, limit=60):
    args = [a if isinstance(a, tuple) else (a, pltpu.VMEM) for a in args]
    outs = [o if isinstance(o, tuple) else (o, pltpu.VMEM) for o in outs]
    moved = sum(a.size * a.dtype.itemsize for a, _ in args + outs)
    return pl.pallas_call(
        kernel,
        out_shape=[o for o, _ in outs],
        in_specs=[pl.BlockSpec(memory_space=m) for _, m in args],
        out_specs=[pl.BlockSpec(memory_space=m) for _, m in outs],
        scratch_shapes=list(scratch),
        compiler_params=pltpu.CompilerParams(vmem_limit_bytes=limit * 1024 * 1024),
        cost_estimate=pl.CostEstimate(flops=2 * macs, bytes_accessed=moved, transcendentals=0),
    )(*[a for a, _ in args])


def start(source, target, sem):
    copy = pltpu.make_async_copy(source, target, sem)
    copy.start()
    return copy


def shape(dims, dtype):
    return jax.ShapeDtypeStruct(dims, dtype)


def before(value):
    row = lax.broadcasted_iota(jnp.int32, value.shape, 0)
    return jnp.where(row >= 1, pltpu.roll(value, 1, 0), 0.0)


def after(value):
    size = value.shape[0]
    row = lax.broadcasted_iota(jnp.int32, value.shape, 0)
    return jnp.where(row < size - 1, pltpu.roll(value, size - 1, 0), 0.0)


def colour_rows(rgb, scr, rows):
    scr[...] = jnp.zeros_like(scr)
    for f in range(4):
        for k, j in enumerate(rows):
            lanes = slice((f * 2 + k) * 128, (f * 2 + k + 1) * 128)
            for a in range(3):
                to = f - a + 1
                if not 0 <= to < 4:
                    continue
                for e in range(3):
                    at = e * 128 + to * 24 + (j + 1) * 3
                    scr[at : at + 9, lanes] = rgb[a * 3 + e]


def frames_of(f, step):
    return [(a, f + step * (a - 1)) for a in range(3) if 0 <= f + step * (a - 1) < 4]


def wide_taps(field, taps):
    return jnp.concatenate([field[g] for _, g in taps], axis=1)


def conv_rows(field, kernel, f):
    taps = frames_of(f, 1)
    kernel = kernel[taps[0][0] * 256 : (taps[-1][0] + 1) * 256, :]
    wide = dot(wide_taps(field, taps), kernel)
    return before(wide[:, :256]) + wide[:, 256:512] + after(wide[:, 512:])


def conv_rows_t(pairs, f):
    taps = frames_of(f, -1)
    lanes = slice(taps[0][0] * 256, (taps[-1][0] + 1) * 256)
    wide = sum(
        dot(wide_taps(field, taps), kernel[:, lanes], ((1,), (1,)))
        for field, kernel in pairs
    )
    return after(wide[:, :256]) + wide[:, 256:512] + before(wide[:, 512:])


def blocks_of(dec, edge, place):
    for a in range(3):
        for e in range(3):
            tap = [dec[(a * 3 + b) * 3 + e] for b in range(3)]
            for j in range(2):
                if edge:
                    place(a * 256 + j * 128, e * 256 + j * 128, tap, 2 * j)
                else:
                    for r in range(2):
                        place(a * 256 + j * 128, e * 256 + r * 128, tap, j - r + 1)


def rows_kernel(odd_ref, latent, first, second, sems):
    odd = odd_ref[0]
    copies = [
        start(latent.at[:, 1 - odd], first, sems.at[0]),
        start(latent.at[:, odd], second, sems.at[1]),
    ]
    for copy in copies:
        copy.wait()


def prepare_kernel(
    latent, dec, rgb, vgg_first, vgg_second, critic,
    edge, pre, colour, branch,
    own, field, scr, w1_f, w1, w2, sems,
):
    loads = [
        start(latent.at[:, r], field.at[:, :, pl.ds(r * 128, 128)], sems.at[r]) for r in range(2)
    ]

    def put_own(one, two, tap, b):
        own[one : one + 128, two : two + 128] = tap[b]

    def put_edge(one, two, tap, b):
        one, two = (one // 256 * 128, two // 256 * 128)
        edge[b // 2, one : one + 128, two : two + 128] = tap[b]

    blocks_of(dec, False, put_own)
    blocks_of(dec, True, put_edge)
    w1_f[...] = jnp.zeros_like(w1_f)
    w2[...] = jnp.zeros_like(w2)
    for p in range(2):
        lanes = slice(p * 64, p * 64 + 64)
        kinds = (lanes, slice(128 + p * 64, 192 + p * 64))
        for b in range(3):
            rr = p + b
            for e in range(3):
                at, tap = (e * 256 + rr * 64, (b * 3 + e) * 64)
                w2[at : at + 64, p * 128 : p * 128 + 128] = vgg_second[tap : tap + 64, :]
                at, tap = ((3 + e) * 16 + rr * 3, (b * 3 + e) * 3)
                w1_f[at : at + 3, kinds[0]] = vgg_first[tap : tap + 3, lanes]
                for a in range(3):
                    at, tap = ((a * 3 + e) * 16 + rr * 3, ((a * 3 + b) * 3 + e) * 3)
                    w1_f[at : at + 3, kinds[1]] = critic[tap : tap + 3, lanes]
    w1[...] = w1_f[...].astype(BF16)
    stores = [
        start(w2, branch.at[pl.ds(0, 768)], sems.at[2]),
        start(w1, branch.at[pl.ds(768, 144)], sems.at[3]),
    ]
    for load in loads:
        load.wait()
    for f in range(4):
        both = conv_rows(field, own, f)
        pre[0, f] = both[:, :128]
        pre[1, f] = both[:, 128:]
    colour_rows(rgb, scr, (0, 1))
    colour[...] = scr[...].astype(BF16)
    for store in stores:
        store.wait()


def edge_row(source, kernel, own, row, act, slope, keep):
    for f in range(4):
        taps = frames_of(f, 1)
        part = kernel[row, taps[0][0] * 128 : (taps[-1][0] + 1) * 128, :]
        wide = dot(wide_taps(source, taps), part)
        pre = own[row, f] + before(wide[:, :128]) + wide[:, 128:256] + after(wide[:, 256:])
        gate = sigmoid(pre)
        act[f] = (pre * gate).astype(BF16)
        slope[f] = slope_of(pre, gate).astype(BF16)
        keep(f)


def first_edge_kernel(odd_ref, first, kernel, own, act, slope):
    edge_row(first, kernel, own, 1 - odd_ref[0], act, slope, lambda f: None)


def edge_kernel(
    odd_ref, first, second, kernel, own, colour, target, act_first, slope_first,
    kept, parts,
    act_s, slope_s, t_scr, p_scr, sems,
):
    odd = odd_ref[0]
    cols = first.shape[1]
    copies = []

    def keep(source, target):
        copies.append(start(source, target, sems.at[len(copies)]))

    def keep_frame(f):
        keep(slope_s.at[f], kept.at[1, f])
        keep(act_s.at[odd, f], kept.at[4 + odd, f])

    keep(first, kept.at[3 - odd])
    keep(second, kept.at[2 + odd])
    keep(act_first, kept.at[5 - odd])
    keep(slope_first, kept.at[0])
    act_s[1 - odd] = act_first[...]
    edge_row(second, kernel, own, odd, act_s.at[odd], slope_s, keep_frame)
    wide = dot(wide_act(act_s), colour[...], ((1,), (1,)))
    part = before(wide[:, :128]) + wide[:, 128:256] + after(wide[:, 256:])
    t_scr[...] = jnp.zeros_like(t_scr)
    for f in range(4):
        t_scr[f * 24 + 18 : f * 24 + 24, :] = target[f * 6 : f * 6 + 6, :].astype(F32)
    p_scr[0:8, :] = jnp.zeros((8, 128), F32)
    p_scr[cols : cols + 16, :] = jnp.zeros((16, 128), F32)
    p_scr[HALO : HALO + cols, :] = part + t_scr[...].T
    blocks, length, _ = parts.shape
    for d in range(blocks):
        at = d * (cols // blocks)
        parts[d] = p_scr[at : at + length, :].astype(BF16)
    for copy in copies:
        copy.wait()


def wide_act(act):
    return jnp.concatenate([act[r, f] for f in range(4) for r in range(2)], axis=1)


def branch_scratch(bands, wide):
    return [
        pltpu.VMEM((bands * 2 * (wide - 2 * HALO), 128), F32),
        pltpu.VMEM((1, 64), F32),
        pltpu.VMEM((768, 256), BF16),
        pltpu.VMEM((144, 256), BF16),
        pltpu.VMEM((256, 144), BF16),
        pltpu.VMEM((48, 768), BF16),
        pltpu.VMEM((256, 768), BF16),
        pltpu.VMEM((256, 768), BF16),
        pltpu.VMEM((wide, 24, 128), F32),
        pltpu.VMEM((wide, 16, 128), F32),
        pltpu.VMEM((4, wide + 2, 16, 128), BF16),
        pltpu.VMEM((2, wide, 256, 128), BF16),
        pltpu.VMEM((wide, 128, 128), F32),
        pltpu.VMEM((wide, 256, 128), BF16),
        pltpu.VMEM((wide, 256, 128), BF16),
        pltpu.VMEM((bands * (wide - 2 * HALO), 128), F32),
        pltpu.SemaphoreType.DMA((3,)),
    ]


def branch_kernel(
    me_ref, parts_in, branch_in, head_in,
    out,
    parts, head_row, w2_t, w1_t, w1, w1_z, w2, w2_b,
    rows, taps, colours, feats, slopes, grads_two, grads, turned, sems,
):
    copies = [
        start(source, target, sems.at[k])
        for k, (source, target) in enumerate(
            [
                (branch_in.at[pl.ds(0, 768)], w2_t),
                (branch_in.at[pl.ds(768, 144)], w1_t),
                (head_in, head_row),
            ]
        )
    ]
    wide = rows.shape[0]
    own = wide - 2 * HALO
    bands = parts.shape[0] // (2 * own)
    parts[...] = parts_in[...].astype(F32)
    lane = lax.broadcasted_iota(jnp.int32, (1, 128), 1)
    frame, band = (lane // bands, lane % bands)

    def rolled(value, by):
        by = by % 128
        return value if by == 0 else pltpu.roll(value, by, value.ndim - 1)

    def down(value):
        return jnp.where(band >= 1, rolled(value, 1), 0.0)

    def up(value):
        return jnp.where(band < bands - 1, rolled(value, -1), 0.0)

    def earlier(value):
        return jnp.where(frame >= 1, rolled(value, bands), 0.0)

    def later(value):
        return jnp.where(frame < 3, rolled(value, -bands), 0.0)

    def rounded(value):
        return value.astype(BF16).astype(F32)

    def tile(value, n):
        return value[:, n * 128 : (n + 1) * 128]

    def stacked(get, first, step):
        return jnp.concatenate(
            [
                jnp.concatenate([get(first + n + step * (e - 1)) for e in range(3)], axis=0)
                for n in range(4)
            ],
            axis=1,
        )

    def inside(column):
        place = column + me_ref[0] * own - HALO
        kept = jnp.logical_and(place >= 0, place < own * bands)
        return jnp.full((1, 128), jnp.where(kept, 1.0, 0.0), F32)

    def masks(first):
        return jnp.concatenate([inside(first + n) for n in range(4)], axis=1)

    taps[...] = jnp.zeros_like(taps)
    colours[...] = jnp.zeros_like(colours)
    grads_two[1] = jnp.zeros((256, 128), BF16)
    grads_two[wide - 2] = jnp.zeros((256, 128), BF16)
    for k in range(wide // 4):
        block = jnp.concatenate(
            [parts[pl.ds(4 * k + m, bands, stride=2 * own), :] for m in range(4)], axis=0
        ).T
        for m in range(4):
            value = jnp.zeros((24, 128), F32)
            for f in range(4):
                piece = rolled(block[f * 24 : (f + 1) * 24], (f - m) * bands)
                value = jnp.where(frame == f, piece, value)
            rows[4 * k + m] = value

    mask = jnp.stack([inside(column) for column in range(wide)])

    def place(even, odd):
        taps[:, 0:3, :] = down(odd)
        taps[:, 3:6, :] = even
        taps[:, 6:9, :] = odd
        taps[:, 9:12, :] = up(even)
        return taps[...]

    colours[0, 1 : wide + 1] = place(rows[:, 18:21, :] * mask, rows[:, 21:24, :] * mask).astype(BF16)
    even = rounded((rows[:, 6:9, :] + down(rows[:, 12:15, :])) * mask)
    odd = rounded((rows[:, 9:12, :] + up(rows[:, 3:6, :])) * mask)
    field = place(even, odd)
    for a, value in enumerate((earlier(field), field, later(field))):
        colours[1 + a, 1 : wide + 1] = value.astype(BF16)

    for copy in copies:
        copy.wait()
    w1[...] = w1_t[...].astype(F32).T.astype(BF16)
    w2[...] = w2_t[...].astype(F32).T.astype(BF16)
    for e in range(3):
        w2_b[:, e * 256 : (e + 1) * 256] = w2_t[e * 256 : (e + 1) * 256, :]
        for a in range(3):
            at = (a * 3 + e) * 16
            w1_z[a * 16 : (a + 1) * 16, e * 256 : (e + 1) * 256] = w1_t[at : at + 16, :]
    head = jnp.broadcast_to(head_row[...], (8, 64)).T[:, 0:1]
    head = jnp.concatenate([head, head], axis=0)

    def keep_feats(kind, first, feat):
        for n in range(4):
            value = tile(feat, n)
            feats[kind, first + n, 0:64] = down(value[64:]).astype(BF16)
            feats[kind, first + n, 64:192] = value.astype(BF16)
            feats[kind, first + n, 192:256] = up(value[:64]).astype(BF16)

    def first_layer(t, carry):
        c = t * 4
        mask = masks(c)
        pre = dot(w1[0:128, 48:96], stacked(lambda at: colours[0, at], c + 1, 1))
        keep_feats(0, c, rounded(pre * sigmoid(pre) * mask))
        field = [stacked(lambda at: colours[1 + a, at], c + 1, 1) for a in range(3)]
        both = dot(w1[...], jnp.concatenate(field, axis=0))
        pre, crit = (both[:128], both[128:])
        gate = sigmoid(pre)
        keep_feats(1, c, rounded(pre * gate * mask))
        slope = slope_of(pre, gate) * mask
        gate = sigmoid(crit)
        scored = crit * gate * head
        slope_c = slope_of(crit, gate) * head * mask
        logits = [jnp.sum(scored[r * 64 : r * 64 + 64], axis=0, keepdims=True) for r in range(2)]
        grad = [-sigmoid(-logits[r]) * slope_c[r * 64 : r * 64 + 64] for r in range(2)]
        grad = jnp.concatenate(grad, axis=0).astype(BF16)
        for n in range(4):
            slopes[c + n] = tile(slope, n)
            grads[c + n, 128:256] = tile(grad, n)
        return carry

    lax.fori_loop(0, wide // 4, first_layer, 0, unroll=True)

    def second_layer(t, carry):
        c = t * 4 + 2
        pre = dot(w2[...], stacked(lambda at: feats[0, at], c, 1))
        wanted = pre * sigmoid(pre)
        pre = dot(w2[...], stacked(lambda at: feats[1, at], c, 1))
        gate = sigmoid(pre)
        gap = pre * gate - wanted
        grad = (0.25 * gap * slope_of(pre, gate) * masks(c)).astype(BF16)
        for n in range(4):
            grads_two[c + n] = tile(grad, n)
        return carry

    lax.fori_loop(0, (wide - 4) // 4, second_layer, 0, unroll=True)

    def second_back(t, carry):
        c = t * 4 + 2
        spread = dot(w2_b[...], stacked(lambda at: grads_two[at], c, -1))
        for n in range(4):
            value = tile(spread, n)
            even = value[64:128] + down(value[192:256])
            odd = value[128:192] + up(value[0:64])
            grad = jnp.concatenate([even, odd], axis=0) * slopes[c + n]
            grads[c + n, 0:128] = grad.astype(BF16)
        return carry

    lax.fori_loop(0, (wide - 4) // 4, second_back, 0, unroll=True)

    def first_back(t, carry):
        c = t * 4 + HALO
        spread = dot(w1_z[...], stacked(lambda at: grads[at], c, -1))
        for n in range(4):
            value = tile(spread, n)
            taps[c + n] = later(value[0:16]) + value[16:32] + earlier(value[32:48])
        return carry

    lax.fori_loop(0, own // 4, first_back, 0, unroll=True)
    mid = slice(HALO, HALO + own)
    even = rounded(taps[mid, 3:6, :] + down(taps[mid, 9:12, :]))
    odd = rounded(taps[mid, 6:9, :] + up(taps[mid, 0:3, :]))
    for k, value in enumerate((down(even), down(odd), even, odd, up(even), up(odd))):
        rows[mid, 3 * k : 3 * k + 3, :] = value
    for k in range(own // 4):
        block = []
        for f in range(4):
            value = jnp.zeros((24, 128), F32)
            for m in range(4):
                piece = rolled(rows[HALO + 4 * k + m], (m - f) * bands)
                value = jnp.where(frame == m, piece, value)
            block.append(value)
        block = jnp.concatenate(block + [jnp.zeros((32, 128), F32)], axis=0).T
        for m in range(4):
            turned[pl.ds(4 * k + m, bands, stride=own), :] = block[m * bands : (m + 1) * bands]
    out[...] = turned[...].astype(BF16)


def taps_of(grad_in):
    grad = grad_in[...].astype(F32)
    return jnp.concatenate([after(grad), grad, before(grad)], axis=1)


def dec_grad_kernel(
    odd_ref, grad_in, colour_in, kept, latent,
    local, late,
    colour, slope, act, field, pre_s, moved, gram, sems,
):
    cols = act.shape[2]
    odd = odd_ref[0]
    moves = [
        (colour_in, colour),
        (kept.at[0], slope.at[1 - odd]),
        (kept.at[1], slope.at[odd]),
        (kept.at[pl.ds(4, 2)], act),
        (latent.at[:, 0], field.at[:, :, pl.ds(0, 128)]),
        (latent.at[:, 1], field.at[:, :, pl.ds(128, 128)]),
        (kept.at[2], field.at[:, :, pl.ds(256, 128)]),
        (kept.at[3], field.at[:, :, pl.ds(384, 128)]),
    ]
    copies = [start(source, target, sems.at[k]) for k, (source, target) in enumerate(moves)]
    taps = taps_of(grad_in)
    for copy in copies[:3]:
        copy.wait()
    grad_act = dot(taps.astype(BF16), colour[...])
    lane = lax.broadcasted_iota(jnp.int32, (1, cols), 1)
    for f in range(4):
        wide = grad_act[:, f * 256 : (f + 1) * 256]
        zero = (wide[:, :128] * slope[0, f].astype(F32)).astype(BF16)
        one = (wide[:, 128:] * slope[1, f].astype(F32)).astype(BF16)
        pre_s[f, :, :128] = zero
        pre_s[f, :, 128:] = one
        turned = jnp.concatenate([zero.astype(F32).T, one.astype(F32).T], axis=0)
        later = jnp.where(lane < cols - 1, pltpu.roll(turned, cols - 1, 1), 0.0)
        sooner = jnp.where(lane >= 1, pltpu.roll(turned, 1, 1), 0.0)
        for e, value in enumerate((later, turned, sooner)):
            moved[e * 256 : (e + 1) * 256, f * cols : (f + 1) * cols] = value.astype(BF16)
    outs = [start(pre_s, late.at[pl.ds(0, 4)], sems.at[8])]
    outs.append(start(grad_in, late.at[4, :, pl.ds(0, 128)], sems.at[7]))
    copies[3].wait()
    gram[...] = dot(taps.T.astype(BF16), wide_act(act))
    rows = []
    for a in range(3):
        sums = []
        for e in range(3):
            total = jnp.zeros((9, 128), F32)
            for f in range(4):
                to = f - a + 1
                if not 0 <= to < 4:
                    continue
                for r in range(2):
                    at = e * 128 + to * 24 + (r + 1) * 3
                    total += gram[at : at + 9, (f * 2 + r) * 128 : (f * 2 + r + 1) * 128]
            sums.append(total)
        for b in range(3):
            for e in range(3):
                rows.append(sums[e][(2 - b) * 3 : (2 - b) * 3 + 3])
    gram[0:128, 0:128] = jnp.zeros((128, 128), F32)
    for k, value in enumerate(rows):
        gram[k * 3 : k * 3 + 3, 0:128] = value
    local[27 * 128 :, :] = gram[0:128, 0:128].astype(BF16)
    for copy in copies[4:]:
        copy.wait()
    rows_of = (2, 0, 1, 3)
    for a in range(3):
        lo, hi = (max(0, 1 - a), min(4, 5 - a))
        first, last = (lo * cols, hi * cols)
        source = field[lo + a - 1 : hi + a - 1].reshape((hi - lo) * cols, 512)
        for e in range(3):
            wide = dot(moved[e * 256 : (e + 1) * 256, first:last], source)
            for b in range(3):
                one, two = (rows_of[b] * 128, rows_of[b + 1] * 128)
                total = wide[:128, one : one + 128] + wide[128:, two : two + 128]
                at = ((a * 3 + b) * 3 + e) * 128
                local[at : at + 128, :] = total.T.astype(BF16)
    for copy in outs:
        copy.wait()


def latent_kernel(
    odd_ref, late, dec, rgb, first, second,
    out,
    pre, grad_in, own_t, edge_t, colour, edge_s, scr, out_s, sems,
):
    cols = first.shape[1]
    odd = odd_ref[0]
    copies = []
    loads = [
        start(late.at[pl.ds(0, 4)], pre, sems.at[4]),
        start(late.at[4, :, pl.ds(0, 128)], grad_in, sems.at[5]),
    ]
    colour_rows(rgb, scr, (-1, 2))
    colour[...] = scr[...].astype(BF16)

    def put_own(one, two, tap, b):
        at, to = (two // 256 * 256 + one % 256, one // 256 * 256 + two % 256)
        own_t[at : at + 128, to : to + 128] = tap[b]

    def put_edge(one, two, tap, b):
        edge_t[two : two + 128, one : one + 128] = tap[2 - b]

    edge_t[...] = jnp.zeros_like(edge_t)
    blocks_of(dec, False, put_own)
    blocks_of(dec, True, put_edge)
    for load in loads:
        load.wait()
    grad_act = dot(taps_of(grad_in).astype(BF16), colour[...])
    for f in range(4):
        slopes = (
            jnp.where(odd == 1, first[f], second[f]),
            jnp.where(odd == 1, second[f], first[f]),
        )
        for k in range(2):
            at = (f * 2 + k) * 128
            value = grad_act[:, at : at + 128] * slopes[k].astype(F32)
            edge_s[f, :, k * 128 : (k + 1) * 128] = value.astype(BF16)
    for f in range(4):
        wide = conv_rows_t([(pre, own_t), (edge_s, edge_t)], f)
        out_s[f, 0] = wide[:, :128]
        out_s[f, 1] = wide[:, 128:]
        copies.append(start(out_s.at[f], out.at[f], sems.at[f]))
    for copy in copies:
        copy.wait()


def per_device(
    latent, dec_kernel, rgb_kernel, target, vgg_first, vgg_second, critic_kernel, critic_head
):
    size = lax.axis_size("band")
    me = lax.axis_index("band")
    cols = latent.shape[2]
    width = cols // size
    wide = width + 2 * HALO
    pairs = [[(i, i + 1), (i + 1, i)] for i in range(size - 1)]
    first_pairs, second_pairs = (sum(pairs[0::2], []), sum(pairs[1::2], []))
    odd = me % 2
    odd_ref = (jnp.reshape(odd, (1,)).astype(jnp.int32), pltpu.SMEM)

    half = shape((4, cols, 128), BF16)
    sent_first, sent_second = call(
        rows_kernel,
        [half, half],
        odd_ref,
        (latent, HBM),
        scratch=[pltpu.SemaphoreType.DMA((2,))],
        limit=16,
    )
    first = lax.ppermute(sent_first, "band", first_pairs)
    second = lax.ppermute(sent_second, "band", second_pairs)
    rgb = rgb_kernel.transpose(0, 2, 1, 4, 3)[:, :, ::-1].reshape(9, 9, 128).astype(F32)
    big = 4 * cols * 768 * 640
    toeplitz = shape((384, 1024), BF16)
    field = shape((4, cols, 256), BF16)
    dma = pltpu.SemaphoreType.DMA
    dec = dec_kernel.reshape(27, 128, 128)
    edge_w, pre_own, colour, branch = call(
        prepare_kernel,
        [shape((2, 384, 384), BF16), shape((2, 4, cols, 128), F32), toeplitz, (shape((ROWS, 256), BF16), HBM)],
        (latent, HBM),
        dec,
        rgb,
        jnp.tile(vgg_first.reshape(27, 64).astype(F32), (1, 2)),
        vgg_second.reshape(576, 128),
        jnp.tile(critic_kernel.reshape(81, 64).astype(F32), (1, 2)),
        scratch=[
            pltpu.VMEM((768, 768), BF16),
            pltpu.VMEM((4, cols, 256), BF16),
            pltpu.VMEM((384, 1024), F32),
            pltpu.VMEM((144, 256), F32),
            pltpu.VMEM((144, 256), BF16),
            pltpu.VMEM((768, 256), BF16),
            dma((4,)),
        ],
        macs=big,
        limit=PREPARE_MIB,
    )
    act_first, slope_first = call(
        first_edge_kernel, [half, half], odd_ref, first, edge_w, pre_own, macs=big // 2, limit=EDGE_MIB
    )
    kept, parts = call(
        edge_kernel,
        [(shape((SLOTS, 4, cols, 128), BF16), HBM), shape((size, 2 * width, 128), BF16)],
        odd_ref,
        first,
        second,
        edge_w,
        pre_own,
        colour,
        target.transpose(0, 1, 3, 2).reshape(24, cols),
        act_first,
        slope_first,
        scratch=[
            pltpu.VMEM((2, 4, cols, 128), BF16),
            pltpu.VMEM((4, cols, 128), BF16),
            pltpu.VMEM((128, cols), F32),
            pltpu.VMEM((cols + 16, 128), F32),
            dma((12,)),
        ],
        macs=big,
        limit=EDGE_MIB,
    )
    parts = lax.all_to_all(parts, "band", 0, 0)
    parts, sent = lax.optimization_barrier((parts, kept[0]))
    first = lax.ppermute(sent, "band", first_pairs)
    (grad_frames,) = call(
        branch_kernel,
        [shape((size * width, 128), BF16)],
        (jnp.reshape(me, (1,)).astype(jnp.int32), pltpu.SMEM),
        parts.reshape(size * 2 * width, 128),
        (branch, HBM),
        (critic_head.reshape(1, 64), HBM),
        scratch=branch_scratch(size, wide),
        macs=4 * 768 * 768 * 700,
        limit=40,
    )
    grad_frames, sent = lax.optimization_barrier((grad_frames, kept[1]))
    second = lax.ppermute(sent, "band", second_pairs)
    grad_frames = lax.all_to_all(grad_frames.reshape(size, width, 128), "band", 0, 0)
    grad_frames = grad_frames.reshape(cols, 128)
    local, late = call(
        dec_grad_kernel,
        [shape((28 * 128, 128), BF16), (shape((LATE, cols, 256), BF16), HBM)],
        odd_ref,
        grad_frames,
        (colour, HBM),
        (kept, HBM),
        (latent, HBM),
        scratch=[
            pltpu.VMEM((384, 1024), BF16),
            pltpu.VMEM((2, 4, cols, 128), BF16),
            pltpu.VMEM((2, 4, cols, 128), BF16),
            pltpu.VMEM((4, cols, 512), BF16),
            pltpu.VMEM((4, cols, 256), BF16),
            pltpu.VMEM((768, 4 * cols), BF16),
            pltpu.VMEM((384, 1024), F32),
            dma((9,)),
        ],
        macs=3 * big,
        limit=40,
    )
    local, first = lax.optimization_barrier((local, first))
    pieces = lax.all_to_all(local.reshape(size, -1, 128), "band", 0, 0)
    (grad_latent,) = call(
        latent_kernel,
        [(shape((4, 2, cols, 128), F32), HBM)],
        odd_ref,
        (late, HBM),
        dec,
        rgb,
        first,
        second,
        scratch=[
            pltpu.VMEM((4, cols, 256), BF16),
            pltpu.VMEM((cols, 128), BF16),
            pltpu.VMEM((768, 768), BF16),
            pltpu.VMEM((768, 768), BF16),
            pltpu.VMEM((384, 1024), BF16),
            pltpu.VMEM((4, cols, 256), BF16),
            pltpu.VMEM((384, 1024), F32),
            pltpu.VMEM((4, 2, cols, 128), F32),
            dma((6,)),
        ],
        macs=2 * big,
    )
    mine = jnp.sum(pieces.astype(F32), axis=0).astype(BF16)
    mine, grad_latent = lax.optimization_barrier((mine, grad_latent))
    whole = lax.all_to_all(jnp.broadcast_to(mine, (size,) + mine.shape), "band", 0, 0)
    whole = whole.reshape(28 * 128, 128)
    pixels = 4 * latent.shape[1] * size * cols
    factor = float(pixels) ** (-0.5)
    grad_dec = whole[: 27 * 128].astype(F32).reshape(3, 3, 3, 128, 128) * factor
    grad_rgb = whole[27 * 128 : 27 * 128 + 81].astype(F32).reshape(3, 3, 3, 3, 128) * factor
    return (grad_latent, grad_dec, grad_rgb.transpose(0, 1, 2, 4, 3))


def solution(mesh):
    placed = (
        P("clip", "band", None, None),
        P(),
        P(),
        P("clip", "band", None, None),
        P(),
        P(),
        P(),
        P(),
    )
    return jax.shard_map(
        per_device,
        mesh=mesh,
        in_specs=placed,
        out_specs=(
            P("clip", "band", None, None),
            P("clip", None, None, None, None),
            P("clip", None, None, None, None),
        ),
        check_vma=False,
    )
```

```python
import jax
import jax.numpy as jnp
from jax import lax
from jax.experimental import pallas as pl
from jax.experimental.pallas import tpu as pltpu
from jax.sharding import PartitionSpec as P

F32 = jnp.float32
BF16 = jnp.bfloat16
HBM = pltpu.HBM
PREPARE_MIB = 24
EDGE_MIB = 24
LATE = 110
ROWS = 60000
SLOTS = 60
HALO = 4


def sigmoid(value):
    return 0.5 * jnp.tanh(0.5 * value) + 0.5


def slope_of(value, gate):
    return gate * (1.0 + value * (1.0 - gate))


def dot(left, right, contract=((1,), (0,))):
    return lax.dot_general(left, right, (contract, ((), ())), preferred_element_type=F32)


def call(kernel, outs, *args, scratch=(), macs=0, limit=60):
    args = [a if isinstance(a, tuple) else (a, pltpu.VMEM) for a in args]
    outs = [o if isinstance(o, tuple) else (o, pltpu.VMEM) for o in outs]
    moved = sum(a.size * a.dtype.itemsize for a, _ in args + outs)
    return pl.pallas_call(
        kernel,
        out_shape=[o for o, _ in outs],
        in_specs=[pl.BlockSpec(memory_space=m) for _, m in args],
        out_specs=[pl.BlockSpec(memory_space=m) for _, m in outs],
        scratch_shapes=list(scratch),
        compiler_params=pltpu.CompilerParams(vmem_limit_bytes=limit * 1024 * 1024),
        cost_estimate=pl.CostEstimate(flops=2 * macs, bytes_accessed=moved, transcendentals=0),
    )(*[a for a, _ in args])


def start(source, target, sem):
    copy = pltpu.make_async_copy(source, target, sem)
    copy.start()
    return copy


def shape(dims, dtype):
    return jax.ShapeDtypeStruct(dims, dtype)


def before(value):
    row = lax.broadcasted_iota(jnp.int32, value.shape, 0)
    return jnp.where(row >= 1, pltpu.roll(value, 1, 0), 0.0)


def after(value):
    size = value.shape[0]
    row = lax.broadcasted_iota(jnp.int32, value.shape, 0)
    return jnp.where(row < size - 1, pltpu.roll(value, size - 1, 0), 0.0)


def colour_rows(rgb, scr, rows):
    scr[...] = jnp.zeros_like(scr)
    for f in range(4):
        for k, j in enumerate(rows):
            lanes = slice((f * 2 + k) * 128, (f * 2 + k + 1) * 128)
            for a in range(3):
                to = f - a + 1
                if not 0 <= to < 4:
                    continue
                for e in range(3):
                    at = e * 128 + to * 24 + (j + 1) * 3
                    scr[at : at + 9, lanes] = rgb[a * 3 + e]


def frames_of(f, step):
    return [(a, f + step * (a - 1)) for a in range(3) if 0 <= f + step * (a - 1) < 4]


def wide_taps(field, taps):
    return jnp.concatenate([field[g] for _, g in taps], axis=1)


def conv_rows(field, kernel, f):
    taps = frames_of(f, 1)
    kernel = kernel[taps[0][0] * 256 : (taps[-1][0] + 1) * 256, :]
    wide = dot(wide_taps(field, taps), kernel)
    return before(wide[:, :256]) + wide[:, 256:512] + after(wide[:, 512:])


def conv_rows_t(pairs, f):
    taps = frames_of(f, -1)
    lanes = slice(taps[0][0] * 256, (taps[-1][0] + 1) * 256)
    wide = sum(
        dot(wide_taps(field, taps), kernel[:, lanes], ((1,), (1,)))
        for field, kernel in pairs
    )
    return after(wide[:, :256]) + wide[:, 256:512] + before(wide[:, 512:])


def blocks_of(dec, edge, place):
    for a in range(3):
        for e in range(3):
            tap = [dec[(a * 3 + b) * 3 + e] for b in range(3)]
            for j in range(2):
                if edge:
                    place(a * 256 + j * 128, e * 256 + j * 128, tap, 2 * j)
                else:
                    for r in range(2):
                        place(a * 256 + j * 128, e * 256 + r * 128, tap, j - r + 1)


def rows_kernel(odd_ref, latent, first, second, sems):
    odd = odd_ref[0]
    copies = [
        start(latent.at[:, 1 - odd], first, sems.at[0]),
        start(latent.at[:, odd], second, sems.at[1]),
    ]
    for copy in copies:
        copy.wait()


def prepare_kernel(
    latent, dec, rgb, vgg_first, vgg_second, critic,
    edge, pre, colour, branch,
    own, field, scr, w1_f, w1, w2, sems,
):
    loads = [
        start(latent.at[:, r], field.at[:, :, pl.ds(r * 128, 128)], sems.at[r]) for r in range(2)
    ]

    def put_own(one, two, tap, b):
        own[one : one + 128, two : two + 128] = tap[b]

    def put_edge(one, two, tap, b):
        one, two = (one // 256 * 128, two // 256 * 128)
        edge[b // 2, one : one + 128, two : two + 128] = tap[b]

    blocks_of(dec, False, put_own)
    blocks_of(dec, True, put_edge)
    w1_f[...] = jnp.zeros_like(w1_f)
    w2[...] = jnp.zeros_like(w2)
    for p in range(2):
        lanes = slice(p * 64, p * 64 + 64)
        kinds = (lanes, slice(128 + p * 64, 192 + p * 64))
        for b in range(3):
            rr = p + b
            for e in range(3):
                at, tap = (e * 256 + rr * 64, (b * 3 + e) * 64)
                w2[at : at + 64, p * 128 : p * 128 + 128] = vgg_second[tap : tap + 64, :]
                at, tap = ((3 + e) * 16 + rr * 3, (b * 3 + e) * 3)
                w1_f[at : at + 3, kinds[0]] = vgg_first[tap : tap + 3, lanes]
                for a in range(3):
                    at, tap = ((a * 3 + e) * 16 + rr * 3, ((a * 3 + b) * 3 + e) * 3)
                    w1_f[at : at + 3, kinds[1]] = critic[tap : tap + 3, lanes]
    w1[...] = w1_f[...].astype(BF16)
    stores = [
        start(w2, branch.at[pl.ds(0, 768)], sems.at[2]),
        start(w1, branch.at[pl.ds(768, 144)], sems.at[3]),
    ]
    for load in loads:
        load.wait()
    for f in range(4):
        both = conv_rows(field, own, f)
        pre[0, f] = both[:, :128]
        pre[1, f] = both[:, 128:]
    colour_rows(rgb, scr, (0, 1))
    colour[...] = scr[...].astype(BF16)
    for store in stores:
        store.wait()


def edge_row(source, kernel, own, row, act, slope, keep):
    for f in range(4):
        taps = frames_of(f, 1)
        part = kernel[row, taps[0][0] * 128 : (taps[-1][0] + 1) * 128, :]
        wide = dot(wide_taps(source, taps), part)
        pre = own[row, f] + before(wide[:, :128]) + wide[:, 128:256] + after(wide[:, 256:])
        gate = sigmoid(pre)
        act[f] = (pre * gate).astype(BF16)
        slope[f] = slope_of(pre, gate).astype(BF16)
        keep(f)


def first_edge_kernel(odd_ref, first, kernel, own, act, slope):
    edge_row(first, kernel, own, 1 - odd_ref[0], act, slope, lambda f: None)


def edge_kernel(
    odd_ref, first, second, kernel, own, colour, target, act_first, slope_first,
    kept, parts,
    act_s, slope_s, t_scr, p_scr, sems,
):
    odd = odd_ref[0]
    cols = first.shape[1]
    copies = []

    def keep(source, target):
        copies.append(start(source, target, sems.at[len(copies)]))

    def keep_frame(f):
        keep(slope_s.at[f], kept.at[1, f])
        keep(act_s.at[odd, f], kept.at[4 + odd, f])

    keep(first, kept.at[3 - odd])
    keep(second, kept.at[2 + odd])
    keep(act_first, kept.at[5 - odd])
    keep(slope_first, kept.at[0])
    act_s[1 - odd] = act_first[...]
    edge_row(second, kernel, own, odd, act_s.at[odd], slope_s, keep_frame)
    wide = dot(wide_act(act_s), colour[...], ((1,), (1,)))
    part = before(wide[:, :128]) + wide[:, 128:256] + after(wide[:, 256:])
    t_scr[...] = jnp.zeros_like(t_scr)
    for f in range(4):
        t_scr[f * 24 + 18 : f * 24 + 24, :] = target[f * 6 : f * 6 + 6, :].astype(F32)
    p_scr[0:8, :] = jnp.zeros((8, 128), F32)
    p_scr[cols : cols + 16, :] = jnp.zeros((16, 128), F32)
    p_scr[HALO : HALO + cols, :] = part + t_scr[...].T
    blocks, length, _ = parts.shape
    for d in range(blocks):
        at = d * (cols // blocks)
        parts[d] = p_scr[at : at + length, :].astype(BF16)
    for copy in copies:
        copy.wait()


def wide_act(act):
    return jnp.concatenate([act[r, f] for f in range(4) for r in range(2)], axis=1)


def branch_scratch(bands, wide):
    return [
        pltpu.VMEM((bands * 2 * (wide - 2 * HALO), 128), F32),
        pltpu.VMEM((1, 64), F32),
        pltpu.VMEM((768, 256), BF16),
        pltpu.VMEM((144, 256), BF16),
        pltpu.VMEM((256, 144), BF16),
        pltpu.VMEM((48, 768), BF16),
        pltpu.VMEM((256, 768), BF16),
        pltpu.VMEM((256, 768), BF16),
        pltpu.VMEM((wide, 24, 128), F32),
        pltpu.VMEM((wide, 16, 128), F32),
        pltpu.VMEM((4, wide + 2, 16, 128), BF16),
        pltpu.VMEM((2, wide, 256, 128), BF16),
        pltpu.VMEM((wide, 128, 128), F32),
        pltpu.VMEM((wide, 256, 128), BF16),
        pltpu.VMEM((wide, 256, 128), BF16),
        pltpu.VMEM((bands * (wide - 2 * HALO), 128), F32),
        pltpu.SemaphoreType.DMA((3,)),
    ]


def branch_kernel(
    me_ref, parts_in, branch_in, head_in,
    out,
    parts, head_row, w2_t, w1_t, w1, w1_z, w2, w2_b,
    rows, taps, colours, feats, slopes, grads_two, grads, turned, sems,
):
    copies = [
        start(source, target, sems.at[k])
        for k, (source, target) in enumerate(
            [
                (branch_in.at[pl.ds(0, 768)], w2_t),
                (branch_in.at[pl.ds(768, 144)], w1_t),
                (head_in, head_row),
            ]
        )
    ]
    wide = rows.shape[0]
    own = wide - 2 * HALO
    bands = parts.shape[0] // (2 * own)
    parts[...] = parts_in[...].astype(F32)
    lane = lax.broadcasted_iota(jnp.int32, (1, 128), 1)
    frame, band = (lane // bands, lane % bands)

    def rolled(value, by):
        by = by % 128
        return value if by == 0 else pltpu.roll(value, by, value.ndim - 1)

    def down(value):
        return jnp.where(band >= 1, rolled(value, 1), 0.0)

    def up(value):
        return jnp.where(band < bands - 1, rolled(value, -1), 0.0)

    def earlier(value):
        return jnp.where(frame >= 1, rolled(value, bands), 0.0)

    def later(value):
        return jnp.where(frame < 3, rolled(value, -bands), 0.0)

    def rounded(value):
        return value.astype(BF16).astype(F32)

    def tile(value, n):
        return value[:, n * 128 : (n + 1) * 128]

    def stacked(get, first, step):
        return jnp.concatenate(
            [
                jnp.concatenate([get(first + n + step * (e - 1)) for e in range(3)], axis=0)
                for n in range(4)
            ],
            axis=1,
        )

    def inside(column):
        place = column + me_ref[0] * own - HALO
        kept = jnp.logical_and(place >= 0, place < own * bands)
        return jnp.full((1, 128), jnp.where(kept, 1.0, 0.0), F32)

    def masks(first):
        return jnp.concatenate([inside(first + n) for n in range(4)], axis=1)

    taps[...] = jnp.zeros_like(taps)
    colours[...] = jnp.zeros_like(colours)
    grads_two[1] = jnp.zeros((256, 128), BF16)
    grads_two[wide - 2] = jnp.zeros((256, 128), BF16)
    for k in range(wide // 4):
        block = jnp.concatenate(
            [parts[pl.ds(4 * k + m, bands, stride=2 * own), :] for m in range(4)], axis=0
        ).T
        for m in range(4):
            value = jnp.zeros((24, 128), F32)
            for f in range(4):
                piece = rolled(block[f * 24 : (f + 1) * 24], (f - m) * bands)
                value = jnp.where(frame == f, piece, value)
            rows[4 * k + m] = value

    mask = jnp.stack([inside(column) for column in range(wide)])

    def place(even, odd):
        taps[:, 0:3, :] = down(odd)
        taps[:, 3:6, :] = even
        taps[:, 6:9, :] = odd
        taps[:, 9:12, :] = up(even)
        return taps[...]

    colours[0, 1 : wide + 1] = place(rows[:, 18:21, :] * mask, rows[:, 21:24, :] * mask).astype(BF16)
    even = rounded((rows[:, 6:9, :] + down(rows[:, 12:15, :])) * mask)
    odd = rounded((rows[:, 9:12, :] + up(rows[:, 3:6, :])) * mask)
    field = place(even, odd)
    for a, value in enumerate((earlier(field), field, later(field))):
        colours[1 + a, 1 : wide + 1] = value.astype(BF16)

    for copy in copies:
        copy.wait()
    w1[...] = w1_t[...].astype(F32).T.astype(BF16)
    w2[...] = w2_t[...].astype(F32).T.astype(BF16)
    for e in range(3):
        w2_b[:, e * 256 : (e + 1) * 256] = w2_t[e * 256 : (e + 1) * 256, :]
        for a in range(3):
            at = (a * 3 + e) * 16
            w1_z[a * 16 : (a + 1) * 16, e * 256 : (e + 1) * 256] = w1_t[at : at + 16, :]
    head = jnp.broadcast_to(head_row[...], (8, 64)).T[:, 0:1]
    head = jnp.concatenate([head, head], axis=0)

    def keep_feats(kind, first, feat):
        for n in range(4):
            value = tile(feat, n)
            feats[kind, first + n, 0:64] = down(value[64:]).astype(BF16)
            feats[kind, first + n, 64:192] = value.astype(BF16)
            feats[kind, first + n, 192:256] = up(value[:64]).astype(BF16)

    def first_layer(t, carry):
        c = t * 4
        mask = masks(c)
        pre = dot(w1[0:128, 48:96], stacked(lambda at: colours[0, at], c + 1, 1))
        keep_feats(0, c, rounded(pre * sigmoid(pre) * mask))
        field = [stacked(lambda at: colours[1 + a, at], c + 1, 1) for a in range(3)]
        both = dot(w1[...], jnp.concatenate(field, axis=0))
        pre, crit = (both[:128], both[128:])
        gate = sigmoid(pre)
        keep_feats(1, c, rounded(pre * gate * mask))
        slope = slope_of(pre, gate) * mask
        gate = sigmoid(crit)
        scored = crit * gate * head
        slope_c = slope_of(crit, gate) * head * mask
        logits = [jnp.sum(scored[r * 64 : r * 64 + 64], axis=0, keepdims=True) for r in range(2)]
        grad = [-sigmoid(-logits[r]) * slope_c[r * 64 : r * 64 + 64] for r in range(2)]
        grad = jnp.concatenate(grad, axis=0).astype(BF16)
        for n in range(4):
            slopes[c + n] = tile(slope, n)
            grads[c + n, 128:256] = tile(grad, n)
        return carry

    lax.fori_loop(0, wide // 4, first_layer, 0, unroll=True)

    def second_layer(t, carry):
        c = t * 4 + 2
        pre = dot(w2[...], stacked(lambda at: feats[0, at], c, 1))
        wanted = pre * sigmoid(pre)
        pre = dot(w2[...], stacked(lambda at: feats[1, at], c, 1))
        gate = sigmoid(pre)
        gap = pre * gate - wanted
        grad = (0.25 * gap * slope_of(pre, gate) * masks(c)).astype(BF16)
        for n in range(4):
            grads_two[c + n] = tile(grad, n)
        return carry

    lax.fori_loop(0, (wide - 4) // 4, second_layer, 0, unroll=True)

    def second_back(t, carry):
        c = t * 4 + 2
        spread = dot(w2_b[...], stacked(lambda at: grads_two[at], c, -1))
        for n in range(4):
            value = tile(spread, n)
            even = value[64:128] + down(value[192:256])
            odd = value[128:192] + up(value[0:64])
            grad = jnp.concatenate([even, odd], axis=0) * slopes[c + n]
            grads[c + n, 0:128] = grad.astype(BF16)
        return carry

    lax.fori_loop(0, (wide - 4) // 4, second_back, 0, unroll=True)

    def first_back(t, carry):
        c = t * 4 + HALO
        spread = dot(w1_z[...], stacked(lambda at: grads[at], c, -1))
        for n in range(4):
            value = tile(spread, n)
            taps[c + n] = later(value[0:16]) + value[16:32] + earlier(value[32:48])
        return carry

    lax.fori_loop(0, own // 4, first_back, 0, unroll=True)
    mid = slice(HALO, HALO + own)
    even = rounded(taps[mid, 3:6, :] + down(taps[mid, 9:12, :]))
    odd = rounded(taps[mid, 6:9, :] + up(taps[mid, 0:3, :]))
    for k, value in enumerate((down(even), down(odd), even, odd, up(even), up(odd))):
        rows[mid, 3 * k : 3 * k + 3, :] = value
    for k in range(own // 4):
        block = []
        for f in range(4):
            value = jnp.zeros((24, 128), F32)
            for m in range(4):
                piece = rolled(rows[HALO + 4 * k + m], (m - f) * bands)
                value = jnp.where(frame == m, piece, value)
            block.append(value)
        block = jnp.concatenate(block + [jnp.zeros((32, 128), F32)], axis=0).T
        for m in range(4):
            turned[pl.ds(4 * k + m, bands, stride=own), :] = block[m * bands : (m + 1) * bands]
    out[...] = turned[...].astype(BF16)


def taps_of(grad_in):
    grad = grad_in[...].astype(F32)
    return jnp.concatenate([after(grad), grad, before(grad)], axis=1)


def dec_grad_kernel(
    odd_ref, grad_in, colour_in, kept, latent,
    local, late,
    colour, slope, act, field, pre_s, moved, gram, sems,
):
    cols = act.shape[2]
    odd = odd_ref[0]
    moves = [
        (colour_in, colour),
        (kept.at[0], slope.at[1 - odd]),
        (kept.at[1], slope.at[odd]),
        (kept.at[pl.ds(4, 2)], act),
        (latent.at[:, 0], field.at[:, :, pl.ds(0, 128)]),
        (latent.at[:, 1], field.at[:, :, pl.ds(128, 128)]),
        (kept.at[2], field.at[:, :, pl.ds(256, 128)]),
        (kept.at[3], field.at[:, :, pl.ds(384, 128)]),
    ]
    copies = [start(source, target, sems.at[k]) for k, (source, target) in enumerate(moves)]
    taps = taps_of(grad_in)
    for copy in copies[:3]:
        copy.wait()
    grad_act = dot(taps.astype(BF16), colour[...])
    lane = lax.broadcasted_iota(jnp.int32, (1, cols), 1)
    for f in range(4):
        wide = grad_act[:, f * 256 : (f + 1) * 256]
        zero = (wide[:, :128] * slope[0, f].astype(F32)).astype(BF16)
        one = (wide[:, 128:] * slope[1, f].astype(F32)).astype(BF16)
        pre_s[f, :, :128] = zero
        pre_s[f, :, 128:] = one
        turned = jnp.concatenate([zero.T, one.T], axis=0)
        none = jnp.zeros_like(turned)
        later = jnp.where(lane < cols - 1, pltpu.roll(turned, cols - 1, 1), none)
        sooner = jnp.where(lane >= 1, pltpu.roll(turned, 1, 1), none)
        for e, value in enumerate((later, turned, sooner)):
            moved[e * 256 : (e + 1) * 256, f * cols : (f + 1) * cols] = value
    outs = [start(pre_s, late.at[pl.ds(0, 4)], sems.at[8])]
    outs.append(start(grad_in, late.at[4, :, pl.ds(0, 128)], sems.at[7]))
    copies[3].wait()
    gram[...] = dot(taps.T.astype(BF16), wide_act(act))
    rows = []
    for a in range(3):
        sums = []
        for e in range(3):
            total = jnp.zeros((9, 128), F32)
            for f in range(4):
                to = f - a + 1
                if not 0 <= to < 4:
                    continue
                for r in range(2):
                    at = e * 128 + to * 24 + (r + 1) * 3
                    total += gram[at : at + 9, (f * 2 + r) * 128 : (f * 2 + r + 1) * 128]
            sums.append(total)
        for b in range(3):
            for e in range(3):
                rows.append(sums[e][(2 - b) * 3 : (2 - b) * 3 + 3])
    gram[0:128, 0:128] = jnp.zeros((128, 128), F32)
    for k, value in enumerate(rows):
        gram[k * 3 : k * 3 + 3, 0:128] = value
    local[27 * 128 :, :] = gram[0:128, 0:128].astype(BF16)
    for copy in copies[4:]:
        copy.wait()
    rows_of = (2, 0, 1, 3)
    for a in range(3):
        lo, hi = (max(0, 1 - a), min(4, 5 - a))
        first, last = (lo * cols, hi * cols)
        source = field[lo + a - 1 : hi + a - 1].reshape((hi - lo) * cols, 512)
        gram_a = dot(moved[:, first:last], source)
        for e in range(3):
            wide = gram_a[e * 256 : (e + 1) * 256]
            for b in range(3):
                one, two = (rows_of[b] * 128, rows_of[b + 1] * 128)
                total = wide[:128, one : one + 128] + wide[128:, two : two + 128]
                at = ((a * 3 + b) * 3 + e) * 128
                local[at : at + 128, :] = total.T.astype(BF16)
    for copy in outs:
        copy.wait()


def latent_kernel(
    odd_ref, late, dec, rgb, first, second,
    out,
    pre, grad_in, own_t, edge_t, colour, edge_s, scr, out_s, sems,
):
    cols = first.shape[1]
    odd = odd_ref[0]
    copies = []
    loads = [
        start(late.at[pl.ds(0, 4)], pre, sems.at[4]),
        start(late.at[4, :, pl.ds(0, 128)], grad_in, sems.at[5]),
    ]
    colour_rows(rgb, scr, (-1, 2))
    colour[...] = scr[...].astype(BF16)

    def put_own(one, two, tap, b):
        at, to = (two // 256 * 256 + one % 256, one // 256 * 256 + two % 256)
        own_t[at : at + 128, to : to + 128] = tap[b]

    def put_edge(one, two, tap, b):
        edge_t[two : two + 128, one : one + 128] = tap[2 - b]

    edge_t[...] = jnp.zeros_like(edge_t)
    blocks_of(dec, False, put_own)
    blocks_of(dec, True, put_edge)
    for load in loads:
        load.wait()
    grad_act = dot(taps_of(grad_in).astype(BF16), colour[...])
    for f in range(4):
        slopes = (
            jnp.where(odd == 1, first[f], second[f]),
            jnp.where(odd == 1, second[f], first[f]),
        )
        for k in range(2):
            at = (f * 2 + k) * 128
            value = grad_act[:, at : at + 128] * slopes[k].astype(F32)
            edge_s[f, :, k * 128 : (k + 1) * 128] = value.astype(BF16)
    for f in range(4):
        wide = conv_rows_t([(pre, own_t), (edge_s, edge_t)], f)
        out_s[f, 0] = wide[:, :128]
        out_s[f, 1] = wide[:, 128:]
        copies.append(start(out_s.at[f], out.at[f], sems.at[f]))
    for copy in copies:
        copy.wait()


def per_device(
    latent, dec_kernel, rgb_kernel, target, vgg_first, vgg_second, critic_kernel, critic_head
):
    size = lax.axis_size("band")
    me = lax.axis_index("band")
    cols = latent.shape[2]
    width = cols // size
    wide = width + 2 * HALO
    pairs = [[(i, i + 1), (i + 1, i)] for i in range(size - 1)]
    first_pairs, second_pairs = (sum(pairs[0::2], []), sum(pairs[1::2], []))
    odd = me % 2
    odd_ref = (jnp.reshape(odd, (1,)).astype(jnp.int32), pltpu.SMEM)

    half = shape((4, cols, 128), BF16)
    sent_first, sent_second = call(
        rows_kernel,
        [half, half],
        odd_ref,
        (latent, HBM),
        scratch=[pltpu.SemaphoreType.DMA((2,))],
        limit=16,
    )
    first = lax.ppermute(sent_first, "band", first_pairs)
    second = lax.ppermute(sent_second, "band", second_pairs)
    rgb = rgb_kernel.transpose(0, 2, 1, 4, 3)[:, :, ::-1].reshape(9, 9, 128).astype(F32)
    big = 4 * cols * 768 * 640
    toeplitz = shape((384, 1024), BF16)
    field = shape((4, cols, 256), BF16)
    dma = pltpu.SemaphoreType.DMA
    dec = dec_kernel.reshape(27, 128, 128)
    edge_w, pre_own, colour, branch = call(
        prepare_kernel,
        [shape((2, 384, 384), BF16), shape((2, 4, cols, 128), F32), toeplitz, (shape((ROWS, 256), BF16), HBM)],
        (latent, HBM),
        dec,
        rgb,
        jnp.tile(vgg_first.reshape(27, 64).astype(F32), (1, 2)),
        vgg_second.reshape(576, 128),
        jnp.tile(critic_kernel.reshape(81, 64).astype(F32), (1, 2)),
        scratch=[
            pltpu.VMEM((768, 768), BF16),
            pltpu.VMEM((4, cols, 256), BF16),
            pltpu.VMEM((384, 1024), F32),
            pltpu.VMEM((144, 256), F32),
            pltpu.VMEM((144, 256), BF16),
            pltpu.VMEM((768, 256), BF16),
            dma((4,)),
        ],
        macs=big,
        limit=PREPARE_MIB,
    )
    act_first, slope_first = call(
        first_edge_kernel, [half, half], odd_ref, first, edge_w, pre_own, macs=big // 2, limit=EDGE_MIB
    )
    kept, parts = call(
        edge_kernel,
        [(shape((SLOTS, 4, cols, 128), BF16), HBM), shape((size, 2 * width, 128), BF16)],
        odd_ref,
        first,
        second,
        edge_w,
        pre_own,
        colour,
        target.transpose(0, 1, 3, 2).reshape(24, cols),
        act_first,
        slope_first,
        scratch=[
            pltpu.VMEM((2, 4, cols, 128), BF16),
            pltpu.VMEM((4, cols, 128), BF16),
            pltpu.VMEM((128, cols), F32),
            pltpu.VMEM((cols + 16, 128), F32),
            dma((12,)),
        ],
        macs=big,
        limit=EDGE_MIB,
    )
    parts = lax.all_to_all(parts, "band", 0, 0)
    parts, sent = lax.optimization_barrier((parts, kept[0]))
    first = lax.ppermute(sent, "band", first_pairs)
    (grad_frames,) = call(
        branch_kernel,
        [shape((size * width, 128), BF16)],
        (jnp.reshape(me, (1,)).astype(jnp.int32), pltpu.SMEM),
        parts.reshape(size * 2 * width, 128),
        (branch, HBM),
        (critic_head.reshape(1, 64), HBM),
        scratch=branch_scratch(size, wide),
        macs=4 * 768 * 768 * 700,
        limit=40,
    )
    grad_frames, sent = lax.optimization_barrier((grad_frames, kept[1]))
    second = lax.ppermute(sent, "band", second_pairs)
    grad_frames = lax.all_to_all(grad_frames.reshape(size, width, 128), "band", 0, 0)
    grad_frames = grad_frames.reshape(cols, 128)
    local, late = call(
        dec_grad_kernel,
        [shape((28 * 128, 128), BF16), (shape((LATE, cols, 256), BF16), HBM)],
        odd_ref,
        grad_frames,
        (colour, HBM),
        (kept, HBM),
        (latent, HBM),
        scratch=[
            pltpu.VMEM((384, 1024), BF16),
            pltpu.VMEM((2, 4, cols, 128), BF16),
            pltpu.VMEM((2, 4, cols, 128), BF16),
            pltpu.VMEM((4, cols, 512), BF16),
            pltpu.VMEM((4, cols, 256), BF16),
            pltpu.VMEM((768, 4 * cols), BF16),
            pltpu.VMEM((384, 1024), F32),
            dma((9,)),
        ],
        macs=3 * big,
        limit=40,
    )
    local, first = lax.optimization_barrier((local, first))
    pieces = lax.all_to_all(local.reshape(size, -1, 128), "band", 0, 0)
    (grad_latent,) = call(
        latent_kernel,
        [(shape((4, 2, cols, 128), F32), HBM)],
        odd_ref,
        (late, HBM),
        dec,
        rgb,
        first,
        second,
        scratch=[
            pltpu.VMEM((4, cols, 256), BF16),
            pltpu.VMEM((cols, 128), BF16),
            pltpu.VMEM((768, 768), BF16),
            pltpu.VMEM((768, 768), BF16),
            pltpu.VMEM((384, 1024), BF16),
            pltpu.VMEM((4, cols, 256), BF16),
            pltpu.VMEM((384, 1024), F32),
            pltpu.VMEM((4, 2, cols, 128), F32),
            dma((6,)),
        ],
        macs=2 * big,
    )
    mine = jnp.sum(pieces.astype(F32), axis=0).astype(BF16)
    mine, grad_latent = lax.optimization_barrier((mine, grad_latent))
    whole = lax.all_to_all(jnp.broadcast_to(mine, (size,) + mine.shape), "band", 0, 0)
    whole = whole.reshape(28 * 128, 128)
    pixels = 4 * latent.shape[1] * size * cols
    factor = float(pixels) ** (-0.5)
    grad_dec = whole[: 27 * 128].astype(F32).reshape(3, 3, 3, 128, 128) * factor
    grad_rgb = whole[27 * 128 : 27 * 128 + 81].astype(F32).reshape(3, 3, 3, 3, 128) * factor
    return (grad_latent, grad_dec, grad_rgb.transpose(0, 1, 2, 4, 3))


def solution(mesh):
    placed = (
        P("clip", "band", None, None),
        P(),
        P(),
        P("clip", "band", None, None),
        P(),
        P(),
        P(),
        P(),
    )
    return jax.shard_map(
        per_device,
        mesh=mesh,
        in_specs=placed,
        out_specs=(
            P("clip", "band", None, None),
            P("clip", None, None, None, None),
            P("clip", None, None, None, None),
        ),
        check_vma=False,
    )
```
